32 devices in a mesh: row: 8 (over z, y), col: 4 (over x, core).
Axes of the slice: x: 2, y: 2, z: 4, core: 2. Of those that a mesh axis runs over, the one named last changes fastest.
Arguments:
- features: bfloat16 [128, 64, 384], P('row', 'col'), may hold values from -6 to 6
- norm_gain: float32 [384], replicated, may hold values from 0.5 to 1.5
- in_weight: bfloat16 [384, 1536], replicated, may hold values from -0.3125 to 0.3125
- conv_weight: float32 [3, 3, 768], replicated, may hold values from -2 to 2
- conv_bias: float32 [768], replicated, may hold values from -3 to 3
- proj_weight: bfloat16 [4, 768, 56], replicated, may hold values from -0.21875 to 0.21875
- step_weight: float32 [4, 24, 768], replicated, may hold values from -1.25 to 1.25
- step_bias: float32 [4, 768], replicated, may hold values from -9 to 2
- decay_log: float32 [4, 768, 16], replicated, may hold values from -3 to 0
- skip_gain: float32 [4, 768], replicated, may hold values from 0.02 to 0.2
- out_gain: float32 [768], replicated, may hold values from 0.5 to 1.5
- out_weight: bfloat16 [768, 384], replicated, may hold values from -0.21875 to 0.21875
Outputs:
- block_out: bfloat16 [128, 64, 384], P('row', 'col')
The draws below stay inside these ranges and needn't reach their ends.
All inputs are finite; a program needn't handle non-finite values.
Results may differ from the reference program's by a relative error of at most 0.014.
Values may be sent and summed in bfloat16 or wider, within the bound.
No kernel may reach another device: no remote copies, remote signals or barrier semaphores. Data moves between devices by JAX's collectives and lax.ppermute only.
A program may use at most 192 MiB of HBM per device.

```python
import jax
import jax.numpy as jnp
from jax import lax

C = 384
E = 768
N = 16
R = 24
IMG_H = 128
IMG_W = 64


def draw_step_bias(key, part):
    lengths = jnp.array([IMG_W, IMG_W, IMG_H, IMG_H], jnp.float32)[:, None]
    lowest, highest = (2.0, 100.0)
    picked = jax.random.uniform(key, (4, E), jnp.float32)
    base_step = jnp.exp(jnp.log(lowest) + picked * (jnp.log(highest) - jnp.log(lowest))) / lengths
    return jnp.log(jnp.expm1(base_step))


def steps_of(key, extent, cuts, low, top_value):
    gain = 1.0
    for position, parts in cuts:
        steps = jax.random.uniform(jax.random.fold_in(jax.random.fold_in(key, 6), position), (parts,), jnp.float32, low / len(cuts), top_value / len(cuts))
        gain = gain * jnp.repeat(jnp.exp(steps), extent[position] // parts).reshape((-1,) + (1,) * (len(extent) - 1 - position))
    return gain


def normal_values(stream_key, shape, width, reach, cuts=(), held_as=jnp.bfloat16):
    level = steps_of(stream_key, shape, cuts, -0.22, 0.18) if cuts else 1.0
    drawn = jax.random.normal(stream_key, shape, jnp.float32) * width * level
    return jnp.minimum(jnp.maximum(drawn, -reach), reach).astype(held_as)


def setup_inputs(seed: int = 0) -> dict:
    key_list = jax.random.split(jax.random.key(seed), 13)
    features = normal_values(key_list[0], (IMG_H, IMG_W, C), 1.0, 6.0, ((0, 8), (1, 4)))
    norm_gain = jnp.clip(1.0 + 0.1 * jax.random.normal(key_list[1], (C,), jnp.float32), 0.5, 1.5)
    in_weight = normal_values(key_list[2], (C, 2 * E), C ** -0.5, 0.3125)
    conv_weight = normal_values(key_list[3], (3, 3, E), 9 ** -0.5, 2.0, (), jnp.float32)
    conv_bias = normal_values(key_list[4], (E,), 0.5, 3.0, (), jnp.float32)
    proj_weight = normal_values(key_list[5], (4, E, R + 2 * N), E ** -0.5, 0.21875)
    step_weight = normal_values(key_list[6], (4, R, E), R ** -0.5, 1.25, (), jnp.float32)
    step_bias = draw_step_bias(jax.random.fold_in(key_list[12], 71), 0)
    decay_log = jnp.clip(jax.random.uniform(key_list[8], (4, E, N), jnp.float32, -3.0, 0.0), -3.0, 0.0)
    skip_gain = jnp.clip(jax.random.uniform(key_list[9], (4, E), jnp.float32, 0.02, 0.2), 0.02, 0.2)
    out_gain = jnp.clip(1.0 + 0.1 * jax.random.normal(key_list[10], (E,), jnp.float32), 0.5, 1.5)
    out_weight = normal_values(key_list[11], (E, C), E ** -0.5, 0.21875)
    return dict(features=features, norm_gain=norm_gain, in_weight=in_weight, conv_weight=conv_weight, conv_bias=conv_bias, proj_weight=proj_weight, step_weight=step_weight, step_bias=step_bias, decay_log=decay_log, skip_gain=skip_gain, out_gain=out_gain, out_weight=out_weight)


def layer_norm(values, scale_gain):
    centred = values - lax.optimization_barrier(jnp.mean(values, axis=-1, keepdims=True))
    spread = lax.optimization_barrier(jnp.mean(centred * centred, axis=-1, keepdims=True))
    return centred * lax.rsqrt(spread + 1e-05) * scale_gain

def line_scan(line_input, proj_part, step_part, bias_part, decay_part, skip_part, reverse):
    rank_size = step_part.shape[0]
    state_size = decay_part.shape[1]
    widened = line_input.astype(jnp.float32)
    projected = jnp.einsum('lpe,ef->lpf', widened, proj_part.astype(jnp.float32))
    step_size = jax.nn.softplus(jnp.einsum('lpr,re->lpe', projected[..., :rank_size], step_part, precision=lax.Precision.HIGHEST) + bias_part)
    enter_coef = projected[..., rank_size:rank_size + state_size]
    leave_coef = projected[..., rank_size + state_size:]
    decay_rate = -jnp.exp(decay_part)

    def advance(hidden_state, pieces):
        step_now, input_now, enter_now, leave_now = pieces
        hidden_state = jnp.exp(step_now[:, :, None] * decay_rate) * hidden_state + (step_now * input_now)[:, :, None] * enter_now[:, None, :]
        return (hidden_state, lax.optimization_barrier(jnp.sum(hidden_state * leave_now[:, None, :], axis=-1)))
    sliced = tuple((jnp.moveaxis(member, 1, 0) for member in (step_size, widened, enter_coef, leave_coef)))
    initial = jnp.zeros((line_input.shape[0], line_input.shape[2], state_size), jnp.float32)
    _, outputs = lax.scan(advance, initial, sliced, reverse=reverse)
    return jnp.moveaxis(outputs, 0, 1) + skip_part * widened

def reference(features, norm_gain, in_weight, conv_weight, conv_bias, proj_weight, step_weight, step_bias, decay_log, skip_gain, out_gain, out_weight):
    height, breadth, channels = features.shape
    inner_width = out_weight.shape[0]
    normed = layer_norm(features.astype(jnp.float32), norm_gain).astype(jnp.bfloat16)
    mixed_proj = jnp.dot(normed.reshape(height * breadth, channels), in_weight, preferred_element_type=jnp.float32).reshape(height, breadth, 2 * inner_width)
    inner_part = mixed_proj[..., :inner_width].astype(jnp.bfloat16)
    gate_part = mixed_proj[..., inner_width:].astype(jnp.bfloat16)
    padded = jnp.pad(inner_part.astype(jnp.float32), ((1, 1), (1, 1), (0, 0)))
    summed = jnp.zeros((height, breadth, inner_width), jnp.float32) + conv_bias
    for tap_row in range(3):
        for tap_col in range(3):
            summed = summed + padded[tap_row:tap_row + height, tap_col:tap_col + breadth] * conv_weight[tap_row, tap_col]
    activated = jax.nn.silu(summed).astype(jnp.bfloat16)
    transposed = jnp.swapaxes(activated, 0, 1)

    def direction(line_input, which_dir, reverse):
        return line_scan(line_input, proj_weight[which_dir], step_weight[which_dir], step_bias[which_dir], decay_log[which_dir], skip_gain[which_dir], reverse)
    row_part = direction(activated, 0, False) + direction(activated, 1, True)
    column_part = direction(transposed, 2, False) + direction(transposed, 3, True)
    combined = row_part + jnp.swapaxes(column_part, 0, 1)
    gated_out = (layer_norm(combined, out_gain) * jax.nn.silu(gate_part.astype(jnp.float32))).astype(jnp.bfloat16)
    block_out = jnp.dot(gated_out.reshape(height * breadth, inner_width), out_weight, preferred_element_type=jnp.float32)
    return block_out.astype(jnp.bfloat16).reshape(height, breadth, channels)
```

```python
import functools

import jax
import jax.numpy as jnp
from jax import lax
from jax.experimental import pallas as pl
from jax.experimental.pallas import tpu as pltpu
from jax.sharding import PartitionSpec as P

F32 = jnp.float32
BF16 = jnp.bfloat16
LANES = 128
SLOTS = 8
LOG2E = 1.4426950408889634


def bits(value):
    assert value & (value - 1) == 0
    return value.bit_length() - 1


def one_hot(targets, width):
    lane = lax.broadcasted_iota(jnp.int32, targets[0].shape, 1)
    blocks = []
    for block in range(width // LANES):
        hit = targets[0] == lane + block * LANES
        for other in targets[1:]:
            hit = jnp.logical_or(hit, other == lane + block * LANES)
        blocks.append(jnp.where(hit, 1.0, 0.0).astype(BF16))
    return jnp.concatenate(blocks, axis=1)


def rows_of(count, start=0):
    return lax.broadcasted_iota(jnp.int32, (count, LANES), 0) + start


def dot(a, b):
    return jnp.dot(a, b, preferred_element_type=F32)


def layer_norm(values, scale_gain):
    centred = values - jnp.mean(values, axis=-1, keepdims=True)
    spread = jnp.mean(centred * centred, axis=-1, keepdims=True)
    return centred * lax.rsqrt(spread + 1e-05) * scale_gain


def cut_kernel(feat_ref, top_ref, bottom_ref, left_ref, right_ref, gain_ref, norm_ref, rows_ref, cols_ref):
    height, width, channels = feat_ref.shape
    gain = gain_ref[...]

    def normed(values):
        return layer_norm(values.astype(F32), gain).astype(BF16)

    tile = normed(feat_ref[...].reshape(height * width, channels))
    norm_ref[...] = tile
    top, bottom = normed(top_ref[...]), normed(bottom_ref[...])
    left, right = normed(left_ref[...]), normed(right_ref[...])
    row = rows_of(height * width)
    turned = dot(one_hot([((row & (height - 1)) << bits(width)) + (row >> bits(height))], height * width), tile).astype(
        BF16
    )

    def cut(out_ref, first, body, last, lines, length):
        parts, reach = out_ref.shape[0], out_ref.shape[1]
        for part in range(parts):
            for line in range(reach):
                at = part * (reach - 2) + line - 1
                if at < 0:
                    out_ref[part, line] = first
                elif at >= lines:
                    out_ref[part, line] = last
                else:
                    out_ref[part, line] = body[at * length : (at + 1) * length]

    cut(rows_ref, top, tile, bottom, height, width)
    cut(cols_ref, left, turned, right, width, height)


def gate_kernel(norm_ref, weight_ref, gate_ref):
    gate_ref[...] = dot(norm_ref[...], weight_ref[...]).astype(BF16)


def line_kernel(
    lines,
    x_ref,
    weight_ref,
    conv_ref,
    conv_bias_ref,
    proj_ref,
    step_ref,
    bias_ref,
    rate_ref,
    skip_ref,
    out_ref,
    inner_ref,
    active_ref,
    proj_out_ref,
    s_ref,
    v_ref,
    y_ref,
):
    parts, reach, length, channels = x_ref.shape
    time = parts * length
    low = time // SLOTS
    width = weight_ref.shape[1]
    chunk = s_ref.shape[2]
    halves = width // chunk
    slot_lines = SLOTS // (2 * halves)
    states = rate_ref.shape[0]

    row = rows_of(reach * time)
    when = (row & (time - 1)) >> 3
    when = ((row & 7) << bits(low)) + when
    line = row >> bits(time)
    source = (when >> bits(length)) * (reach * length) + line * length + (when & (length - 1))
    tokens = dot(one_hot([source], reach * time), x_ref[...].reshape(parts * reach * length, channels)).astype(BF16)
    inner = dot(tokens, weight_ref[...]).astype(BF16).astype(F32)
    inner = inner.reshape(reach, low, SLOTS, width)
    inner_ref[:, 1 : low + 1] = inner
    place = lax.broadcasted_iota(jnp.int32, (SLOTS, width), 0)
    for line in range(reach):
        inner_ref[line, 0] = jnp.where(place == 0, 0.0, pltpu.roll(inner[line, low - 1], 1, 0))
        inner_ref[line, low + 1] = jnp.where(place == SLOTS - 1, 0.0, pltpu.roll(inner[line, 0], SLOTS - 1, 0))

    for line in range(lines):
        for half in range(halves):
            cells = pl.ds(half * chunk, chunk)
            total = jnp.zeros((low, SLOTS, chunk), F32) + conv_bias_ref[:, cells]
            for across in range(3):
                for along in range(3):
                    tap = conv_ref[across, along, cells].reshape(1, 1, chunk)
                    total = total + inner_ref[line + across, along : along + low, :, cells] * tap
            total = total / (1.0 + jnp.exp(-total))
            active_ref[pl.ds((half * lines + line) * time, time), :] = total.reshape(time, chunk).astype(BF16)

    piece = 256
    for first in range(0, time * SLOTS, piece):
        row = rows_of(piece, first)
        now = row >> 3
        slot = row & 7
        line = slot & (slot_lines - 1)
        back = (slot >> bits(slot_lines)) & 1
        half = slot >> bits(2 * slot_lines)
        when = jnp.where(back == 1, time - 1 - now, now)
        source = half * (lines * time) + line * time + ((when & (low - 1)) << 3) + (when >> bits(low))
        if slot_lines > lines:
            source = jnp.where(line < lines, source, -1)
        u = dot(one_hot([source], halves * lines * time), active_ref[...])
        kind = slot >> bits(slot_lines)
        projected = dot(u.astype(BF16), proj_ref[...])
        p = projected[:, :LANES]
        for other in range(1, 2 * halves):
            p = jnp.where(kind == other, projected[:, other * LANES : (other + 1) * LANES], p)
        if halves == 2:
            p = p.reshape(piece // SLOTS, SLOTS, LANES)
            p = p + pltpu.roll(p, SLOTS // 2, 1)
            p = p.reshape(piece, LANES)
        steps = pl.ds(first // SLOTS, piece // SLOTS)
        proj_out_ref[steps] = p.reshape(piece // SLOTS, SLOTS, LANES)
        high = p.astype(BF16).astype(F32)
        lane = lax.broadcasted_iota(jnp.int32, p.shape, 1)
        rank = RANK
        mixed = jnp.where(jnp.logical_and(lane >= rank, lane < 2 * rank), p - high, high)
        stacked = jnp.concatenate([jnp.where(kind == k, mixed, 0.0).astype(BF16) for k in range(2 * halves)], axis=1)
        before = dot(stacked, step_ref[...]).reshape(piece // SLOTS, SLOTS, chunk) + bias_ref[...]
        small = jnp.exp(-jnp.abs(before))
        log1p = jnp.where(small < 0.01, small * (1.0 + small * (-0.5 + small * (1.0 / 3.0 - 0.25 * small))), jnp.log(1.0 + small))
        step = jnp.maximum(before, 0.0) + log1p
        u = u.reshape(piece // SLOTS, SLOTS, chunk)
        s_ref[steps] = step
        v_ref[steps] = step * u
        y_ref[steps] = skip_ref[...] * u

    groups = chunk // LANES
    at_once = max(1, 12 // groups)
    unroll = 8
    for first in range(0, states, at_once):
        rates = [
            [rate_ref[n, :, g * LANES : (g + 1) * LANES] for g in range(groups)] for n in range(first, first + at_once)
        ]

        def advance(lap, hidden):
            hidden = list(hidden)
            for sub in range(unroll):
                t = lap * unroll + sub
                coefs = proj_out_ref[t]
                enter = []
                leave = []
                for n in range(at_once):
                    lane = 3 * RANK + first + n
                    enter.append(jnp.broadcast_to(coefs[:, lane : lane + 1], (SLOTS, LANES)))
                    lane = lane + states
                    leave.append(jnp.broadcast_to(coefs[:, lane : lane + 1], (SLOTS, LANES)))
                for g in range(groups):
                    cells = pl.ds(g * LANES, LANES)
                    step = s_ref[t, :, cells]
                    value = v_ref[t, :, cells]
                    y = y_ref[t, :, cells]
                    for n in range(at_once):
                        k = n * groups + g
                        h = jnp.exp2(step * rates[n][g]) * hidden[k] + value * enter[n]
                        hidden[k] = h
                        y = y + h * leave[n]
                    y_ref[t, :, cells] = y
            return tuple(hidden)

        zero = jnp.zeros((SLOTS, LANES), F32)
        lax.fori_loop(0, time // unroll, advance, (zero,) * (at_once * groups))

    row = rows_of(lines * time)
    line = (row >> bits(length)) & (lines - 1)
    now = ((row >> bits(lines * length)) << bits(length)) + (row & (length - 1))
    scanned = y_ref[...].reshape(time * SLOTS, chunk).astype(BF16)
    for half in range(halves):
        ahead = now * SLOTS + (half * 2 * slot_lines) + line
        behind = (time - 1 - now) * SLOTS + (half * 2 * slot_lines + slot_lines) + line
        joined = dot(one_hot([ahead, behind], time * SLOTS), scanned)
        out_ref[:, half * chunk : (half + 1) * chunk] = joined.astype(BF16)


RANK = 24


def lines_of(x, in_weight, conv, conv_bias, proj, step_weight, step_bias, decay_log, skip):
    parts, reach, length, channels = x.shape
    lines = reach - 2
    time = parts * length
    width = conv.shape[2]
    rank = step_weight.shape[1]
    states = decay_log.shape[2]
    assert rank == RANK
    halves = 1 if lines >= 4 else 2
    slot_lines = SLOTS // (2 * halves)
    assert lines <= slot_lines
    chunk = width // halves

    def by_half(a):
        return jnp.swapaxes(a.reshape(a.shape[:-1] + (halves, chunk)), 0, -2)

    def slots(a):
        a = jnp.swapaxes(a.reshape(2, halves, 1, chunk), 0, 1)
        return jnp.broadcast_to(a, (halves, 2, slot_lines, chunk)).reshape(SLOTS, chunk)

    ranks = proj[:, :, :rank]
    wide = jnp.concatenate(
        [ranks, ranks, ranks, proj[:, :, rank:], jnp.zeros((2, width, LANES - 3 * rank - 2 * states), proj.dtype)],
        axis=2,
    )
    wide = wide.reshape(2, halves, chunk, LANES).transpose(2, 1, 0, 3).reshape(chunk, halves * 2 * LANES)
    high = lax.reduce_precision(step_weight, 8, 7)
    rest = step_weight - high
    tall = jnp.concatenate(
        [high, high, rest, jnp.zeros((2, LANES - 3 * rank, width), step_weight.dtype)], axis=1
    ).astype(BF16)
    tall = tall.reshape(2, LANES, halves, chunk).transpose(2, 0, 1, 3).reshape(halves * 2 * LANES, chunk)
    rates = -jnp.exp(decay_log) * LOG2E
    rates = rates.transpose(2, 0, 1).reshape(states, 2, halves, 1, chunk).transpose(0, 2, 1, 3, 4)
    rates = jnp.broadcast_to(rates, (states, halves, 2, slot_lines, chunk)).reshape(states, SLOTS, chunk)

    whole = pl.BlockSpec(memory_space=pltpu.VMEM)
    flops = 2 * time * (reach * channels * width + SLOTS * width * 256)
    return pl.pallas_call(
        functools.partial(line_kernel, lines),
        out_shape=jax.ShapeDtypeStruct((parts * lines * length, width), BF16),
        grid=(1,),
        in_specs=[whole, pl.BlockSpec((channels, width), lambda i: (0, 0))] + [whole] * 7,
        out_specs=whole,
        scratch_shapes=[
            pltpu.VMEM((reach, time // SLOTS + 2, SLOTS, width), F32),
            pltpu.VMEM((halves * lines * time, chunk), BF16),
            pltpu.VMEM((time, SLOTS, LANES), F32),
            pltpu.VMEM((time, SLOTS, chunk), F32),
            pltpu.VMEM((time, SLOTS, chunk), F32),
            pltpu.VMEM((time, SLOTS, chunk), F32),
        ],
        compiler_params=pltpu.CompilerParams(vmem_limit_bytes=50 * 1024 * 1024),
        cost_estimate=pl.CostEstimate(
            flops=flops, bytes_accessed=4 * 1024 * 1024, transcendentals=time * SLOTS * chunk * states
        ),
    )(x, in_weight, conv, conv_bias.reshape(1, width), wide, tall, slots(step_bias), rates, slots(skip))


def end_kernel(rows_ref, cols_ref, gate_ref, gain_ref, weight_ref, out_ref):
    height, width, channels = out_ref.shape
    row = rows_of(height * width)
    source = ((row & (width - 1)) << bits(height)) + (row >> bits(width))
    combined = rows_ref[...].astype(F32) + dot(one_hot([source], height * width), cols_ref[...])
    gate = gate_ref[...].astype(F32)
    gated = layer_norm(combined, gain_ref[...]) * (gate / (1.0 + jnp.exp(-gate)))
    out = dot(gated.astype(BF16), weight_ref[...]).astype(BF16)
    out_ref[...] = out.reshape(height, width, channels)


def both_ways(array, axis, dim):
    count = lax.axis_size(axis)
    size = array.shape[dim]
    head = lax.index_in_dim(array, 0, dim, False)
    tail = lax.index_in_dim(array, size - 1, dim, False)
    up = [(i, i + 1) for i in range(count - 1)]
    down = [(i + 1, i) for i in range(count - 1)]
    return lax.ppermute(tail, axis, up), lax.ppermute(head, axis, down)


def local(
    features,
    norm_gain,
    in_weight,
    conv_weight,
    conv_bias,
    proj_weight,
    step_weight,
    step_bias,
    decay_log,
    skip_gain,
    out_gain,
    out_weight,
):
    height, width, channels = features.shape
    inner = out_weight.shape[0]
    tokens = height * width
    row_lines = height // lax.axis_size("col")
    col_lines = width // lax.axis_size("row")
    top, bottom = both_ways(features, "row", 0)
    left, right = both_ways(features, "col", 1)

    normed, row_send, col_send = pl.pallas_call(
        cut_kernel,
        out_shape=(
            jax.ShapeDtypeStruct((tokens, channels), BF16),
            jax.ShapeDtypeStruct((lax.axis_size("col"), row_lines + 2, width, channels), BF16),
            jax.ShapeDtypeStruct((lax.axis_size("row"), col_lines + 2, height, channels), BF16),
        ),
    )(features, top, bottom, left, right, norm_gain.reshape(1, channels))
    row_x = lax.all_to_all(row_send, "col", 0, 0, tiled=True)
    col_x = lax.all_to_all(col_send, "row", 0, 0, tiled=True)
    gate = pl.pallas_call(
        gate_kernel,
        out_shape=jax.ShapeDtypeStruct((tokens, inner), BF16),
        grid=(1,),
        in_specs=[
            pl.BlockSpec((tokens, channels), lambda i: (0, 0)),
            pl.BlockSpec((channels, inner), lambda i: (0, 1)),
        ],
        out_specs=pl.BlockSpec((tokens, inner), lambda i: (0, 0)),
        cost_estimate=pl.CostEstimate(flops=2 * tokens * channels * inner, bytes_accessed=1 << 20, transcendentals=0),
    )(normed, in_weight)
    row_y = lines_of(
        row_x,
        in_weight,
        conv_weight,
        conv_bias,
        proj_weight[:2],
        step_weight[:2],
        step_bias[:2],
        decay_log[:2],
        skip_gain[:2],
    )
    row_y = lax.all_to_all(row_y.reshape(lax.axis_size("col"), -1, inner), "col", 0, 0, tiled=True)
    col_y = lines_of(
        col_x,
        in_weight,
        jnp.swapaxes(conv_weight, 0, 1),
        conv_bias,
        proj_weight[2:],
        step_weight[2:],
        step_bias[2:],
        decay_log[2:],
        skip_gain[2:],
    )
    col_y = lax.all_to_all(col_y.reshape(lax.axis_size("row"), -1, inner), "row", 0, 0, tiled=True)
    return pl.pallas_call(
        end_kernel,
        out_shape=jax.ShapeDtypeStruct(features.shape, BF16),
    )(row_y.reshape(tokens, inner), col_y.reshape(tokens, inner), gate, out_gain.reshape(1, inner), out_weight)


def solution(mesh):
    in_specs = (P("row", "col", None), P(), P(), P(), P(), P(), P(), P(), P(), P(), P(), P())
    out_specs = P("row", "col", None)
    return jax.shard_map(local, mesh=mesh, in_specs=in_specs, out_specs=out_specs, check_vma=False)
```

```python
import functools

import jax
import jax.numpy as jnp
from jax import lax
from jax.experimental import pallas as pl
from jax.experimental.pallas import tpu as pltpu
from jax.sharding import PartitionSpec as P

F32 = jnp.float32
BF16 = jnp.bfloat16
LANES = 128
SLOTS = 8
LOG2E = 1.4426950408889634


def bits(value):
    assert value & (value - 1) == 0
    return value.bit_length() - 1


def one_hot(targets, width):
    lane = lax.broadcasted_iota(jnp.int32, targets[0].shape, 1)
    blocks = []
    for block in range(pl.cdiv(width, LANES)):
        hit = targets[0] == lane + block * LANES
        for other in targets[1:]:
            hit = jnp.logical_or(hit, other == lane + block * LANES)
        blocks.append(jnp.where(hit, 1.0, 0.0).astype(BF16))
    return jnp.concatenate(blocks, axis=1)[:, :width]


def rows_of(count, start=0):
    return lax.broadcasted_iota(jnp.int32, (count, LANES), 0) + start


def dot(a, b):
    return jnp.dot(a, b, preferred_element_type=F32)


def layer_norm(values, scale_gain):
    centred = values - jnp.mean(values, axis=-1, keepdims=True)
    spread = jnp.mean(centred * centred, axis=-1, keepdims=True)
    return centred * lax.rsqrt(spread + 1e-05) * scale_gain


def cut_kernel(feat_ref, gain_ref, norm_ref, rows_ref, cols_ref):
    height, width, channels = feat_ref.shape
    tile = layer_norm(feat_ref[...].reshape(height * width, channels).astype(F32), gain_ref[...]).astype(BF16)
    norm_ref[...] = tile
    row = rows_of(height * width)
    turned = dot(one_hot([((row & (height - 1)) << bits(width)) + (row >> bits(height))], height * width), tile).astype(
        BF16
    )

    def cut(out_ref, body, lines, length):
        parts, reach = out_ref.shape[0], out_ref.shape[1]
        for part in range(parts):
            for line in range(reach):
                at = part * (reach - 2) + line - 1
                if 0 <= at < lines:
                    out_ref[part, line] = body[at * length : (at + 1) * length]
                else:
                    out_ref[part, line] = jnp.zeros((length, channels), BF16)

    cut(rows_ref, tile, height, width)
    cut(cols_ref, turned, width, height)


def gate_kernel(norm_ref, weight_ref, gate_ref):
    gate_ref[...] = dot(norm_ref[...], weight_ref[...]).astype(BF16)


def line_kernel(
    lines,
    x_ref,
    seam_ref,
    ends_ref,
    weight_ref,
    conv_ref,
    conv_bias_ref,
    proj_ref,
    step_ref,
    bias_ref,
    rate_ref,
    skip_ref,
    out_ref,
    inner_ref,
    active_ref,
    proj_out_ref,
    s_ref,
    v_ref,
    y_ref,
):
    parts, reach, length, channels = x_ref.shape
    time = parts * length
    low = time // SLOTS
    width = weight_ref.shape[1]
    chunk = s_ref.shape[2]
    halves = width // chunk
    slot_lines = SLOTS // (2 * halves)
    states = rate_ref.shape[0]

    row = rows_of(time)
    order = one_hot([((row & 7) << bits(low)) + (row >> 3)], time)
    place = lax.broadcasted_iota(jnp.int32, (SLOTS, width), 0)
    for line in range(reach):
        x = x_ref[:, line].reshape(time, channels)
        if line == 0 or line == reach - 1:
            missing = ends_ref[0 if line == 0 else 1] == 1
            x = jnp.where(missing, seam_ref[...].reshape(time, channels), x)
        tokens = dot(order, x).astype(BF16)
        inner = dot(tokens, weight_ref[...]).astype(BF16).astype(F32).reshape(low, SLOTS, width)
        inner_ref[line, 1 : low + 1] = inner
        inner_ref[line, 0] = jnp.where(place == 0, 0.0, pltpu.roll(inner[low - 1], 1, 0))
        inner_ref[line, low + 1] = jnp.where(place == SLOTS - 1, 0.0, pltpu.roll(inner[0], SLOTS - 1, 0))

    def convolve(pair, _):
        for group in range(width // (2 * LANES)):
            cells = slice(group * 2 * LANES, (group + 1) * 2 * LANES)
            half = (group * 2 * LANES) // chunk
            base = group * 2 * LANES - half * chunk
            bias = jnp.broadcast_to(conv_bias_ref[:, cells], (SLOTS, 2 * LANES))
            totals = [[bias for _ in range(2)] for _ in range(lines)]
            for across in range(3):
                for along in range(3):
                    tap = jnp.broadcast_to(conv_ref[across, along : along + 1, cells], (SLOTS, 2 * LANES))
                    for line in range(lines):
                        for sub in range(2):
                            totals[line][sub] += inner_ref[line + across, 2 * pair + sub + along, :, cells] * tap
            for line in range(lines):
                value = jnp.concatenate(totals[line], axis=0)
                value = 0.5 * value
                value = value * jnp.tanh(value) + value
                value = value.astype(BF16)
                for piece in range(2):
                    at = base + piece * LANES
                    start = ((half + at // chunk) * lines + line) * time
                    start = pl.multiple_of(start + pair * (2 * SLOTS), 2 * SLOTS)
                    active_ref[pl.ds(start, 2 * SLOTS), at % chunk : at % chunk + LANES] = value[
                        :, piece * LANES : (piece + 1) * LANES
                    ]
        return 0

    lax.fori_loop(0, low // 2, convolve, 0)

    piece = 256
    for first in range(0, time * SLOTS, piece):
        row = rows_of(piece, first)
        now = row >> 3
        slot = row & 7
        line = slot & (slot_lines - 1)
        back = (slot >> bits(slot_lines)) & 1
        half = slot >> bits(2 * slot_lines)
        when = jnp.where(back == 1, time - 1 - now, now)
        source = half * (lines * time) + line * time + ((when & (low - 1)) << 3) + (when >> bits(low))
        if slot_lines > lines:
            source = jnp.where(line < lines, source, -1)
        u = dot(one_hot([source], halves * lines * time), active_ref[...])
        steps = pl.ds(first // SLOTS, piece // SLOTS)
        v_ref[steps] = u.reshape(piece // SLOTS, SLOTS, chunk)
        kind = slot >> bits(slot_lines)
        projected = dot(u.astype(BF16), proj_ref[...])
        p = projected[:, :LANES]
        for other in range(1, 2 * halves):
            p = jnp.where(kind == other, projected[:, other * LANES : (other + 1) * LANES], p)
        if halves == 2:
            p = p.reshape(piece // SLOTS, SLOTS, LANES)
            p = p + pltpu.roll(p, SLOTS // 2, 1)
            p = p.reshape(piece, LANES)
        proj_out_ref[steps] = p.reshape(piece // SLOTS, SLOTS, LANES)
        high = p.astype(BF16).astype(F32)
        lane = lax.broadcasted_iota(jnp.int32, p.shape, 1)
        mixed = jnp.where(jnp.logical_and(lane >= RANK, lane < 2 * RANK), p - high, high)
        stacked = jnp.concatenate([jnp.where(kind == k, mixed, 0.0).astype(BF16) for k in range(2 * halves)], axis=1)
        s_ref[steps] = dot(stacked, step_ref[...]).reshape(piece // SLOTS, SLOTS, chunk)

    def soften(lap, _):
        for sub in range(4):
            t = lap * 4 + sub
            for g in range(chunk // LANES):
                cells = slice(g * LANES, (g + 1) * LANES)
                before = s_ref[t, :, cells] + bias_ref[:, cells]
                small = jnp.exp(-jnp.abs(before))
                series = small * (1.0 + small * (-0.5 + small * (1.0 / 3.0 - 0.25 * small)))
                step = jnp.maximum(before, 0.0) + jnp.where(small < 0.01, series, jnp.log(1.0 + small))
                u = v_ref[t, :, cells]
                s_ref[t, :, cells] = step
                v_ref[t, :, cells] = step * u
                y_ref[t, :, cells] = skip_ref[:, cells] * u
        return 0

    lax.fori_loop(0, time // 4, soften, 0)

    groups = chunk // LANES
    at_once = max(1, 12 // groups)
    unroll = 8
    for first in range(0, states, at_once):
        rates = [
            [rate_ref[n, :, g * LANES : (g + 1) * LANES] for g in range(groups)] for n in range(first, first + at_once)
        ]

        def advance(lap, hidden):
            hidden = list(hidden)
            for sub in range(unroll):
                t = lap * unroll + sub
                coefs = proj_out_ref[t]
                enter = []
                leave = []
                for n in range(at_once):
                    lane = 3 * RANK + first + n
                    enter.append(jnp.broadcast_to(coefs[:, lane : lane + 1], (SLOTS, LANES)))
                    lane = lane + states
                    leave.append(jnp.broadcast_to(coefs[:, lane : lane + 1], (SLOTS, LANES)))
                for g in range(groups):
                    cells = pl.ds(g * LANES, LANES)
                    step = s_ref[t, :, cells]
                    value = v_ref[t, :, cells]
                    y = y_ref[t, :, cells]
                    for n in range(at_once):
                        k = n * groups + g
                        h = jnp.exp2(step * rates[n][g]) * hidden[k] + value * enter[n]
                        hidden[k] = h
                        y = y + h * leave[n]
                    y_ref[t, :, cells] = y
            return tuple(hidden)

        zero = jnp.zeros((SLOTS, LANES), F32)
        lax.fori_loop(0, time // unroll, advance, (zero,) * (at_once * groups))

    row = rows_of(lines * time)
    line = (row >> bits(length)) & (lines - 1)
    now = ((row >> bits(lines * length)) << bits(length)) + (row & (length - 1))
    scanned = y_ref[...].reshape(time * SLOTS, chunk).astype(BF16)
    for half in range(halves):
        ahead = now * SLOTS + (half * 2 * slot_lines) + line
        behind = (time - 1 - now) * SLOTS + (half * 2 * slot_lines + slot_lines) + line
        joined = dot(one_hot([ahead, behind], time * SLOTS), scanned)
        out_ref[:, half * chunk : (half + 1) * chunk] = joined.astype(BF16)


RANK = 24


def lines_of(x, seam, ends, in_weight, conv, conv_bias, proj, step_weight, step_bias, decay_log, skip):
    parts, reach, length, channels = x.shape
    lines = reach - 2
    time = parts * length
    width = conv.shape[2]
    rank = step_weight.shape[1]
    states = decay_log.shape[2]
    assert rank == RANK
    halves = 1 if lines >= 4 else 2
    slot_lines = SLOTS // (2 * halves)
    assert lines <= slot_lines
    chunk = width // halves

    def by_half(a):
        return jnp.swapaxes(a.reshape(a.shape[:-1] + (halves, chunk)), 0, -2)

    def slots(a):
        a = jnp.swapaxes(a.reshape(2, halves, 1, chunk), 0, 1)
        return jnp.broadcast_to(a, (halves, 2, slot_lines, chunk)).reshape(SLOTS, chunk)

    ranks = proj[:, :, :rank]
    wide = jnp.concatenate(
        [ranks, ranks, ranks, proj[:, :, rank:], jnp.zeros((2, width, LANES - 3 * rank - 2 * states), proj.dtype)],
        axis=2,
    )
    wide = wide.reshape(2, halves, chunk, LANES).transpose(2, 1, 0, 3).reshape(chunk, halves * 2 * LANES)
    high = lax.reduce_precision(step_weight, 8, 7)
    rest = step_weight - high
    tall = jnp.concatenate(
        [high, high, rest, jnp.zeros((2, LANES - 3 * rank, width), step_weight.dtype)], axis=1
    ).astype(BF16)
    tall = tall.reshape(2, LANES, halves, chunk).transpose(2, 0, 1, 3).reshape(halves * 2 * LANES, chunk)
    rates = -jnp.exp(decay_log) * LOG2E
    rates = rates.transpose(2, 0, 1).reshape(states, 2, halves, 1, chunk).transpose(0, 2, 1, 3, 4)
    rates = jnp.broadcast_to(rates, (states, halves, 2, slot_lines, chunk)).reshape(states, SLOTS, chunk)

    whole = pl.BlockSpec(memory_space=pltpu.VMEM)
    flops = 2 * time * (reach * channels * width + SLOTS * width * 256)
    return pl.pallas_call(
        functools.partial(line_kernel, lines),
        out_shape=jax.ShapeDtypeStruct((parts * lines * length, width), BF16),
        grid=(1,),
        in_specs=[whole, whole, pl.BlockSpec(memory_space=pltpu.SMEM), pl.BlockSpec((channels, width), lambda i: (0, 0))]
        + [whole] * 7,
        out_specs=whole,
        scratch_shapes=[
            pltpu.VMEM((reach, time // SLOTS + 2, SLOTS, width), F32),
            pltpu.VMEM((halves * lines * time, chunk), BF16),
            pltpu.VMEM((time, SLOTS, LANES), F32),
            pltpu.VMEM((time, SLOTS, chunk), F32),
            pltpu.VMEM((time, SLOTS, chunk), F32),
            pltpu.VMEM((time, SLOTS, chunk), F32),
        ],
        compiler_params=pltpu.CompilerParams(vmem_limit_bytes=50 * 1024 * 1024),
        cost_estimate=pl.CostEstimate(
            flops=flops, bytes_accessed=4 * 1024 * 1024, transcendentals=time * SLOTS * chunk * states
        ),
    )(x, seam, ends, in_weight, conv, conv_bias.reshape(1, width), wide, tall, slots(step_bias), rates, slots(skip))


def end_kernel(rows_ref, cols_ref, gate_ref, gain_ref, weight_ref, out_ref):
    height, width, channels = out_ref.shape
    row = rows_of(height * width)
    source = ((row & (width - 1)) << bits(height)) + (row >> bits(width))
    combined = rows_ref[...].astype(F32) + dot(one_hot([source], height * width), cols_ref[...])
    gate = gate_ref[...].astype(F32)
    gated = layer_norm(combined, gain_ref[...]) * (gate / (1.0 + jnp.exp(-gate)))
    out = dot(gated.astype(BF16), weight_ref[...]).astype(BF16)
    out_ref[...] = out.reshape(height, width, channels)


def send_lines(send, axis):
    x = lax.all_to_all(send, axis, 0, 0, tiled=True)
    count, place = lax.axis_size(axis), lax.axis_index(axis)
    height, breadth = lax.axis_size("row"), lax.axis_size("col")
    if axis == "row":
        ends = [((count - 1) * breadth + c, c + 1) for c in range(breadth - 1)]
    else:
        ends = [(r * breadth + count - 1, (r + 1) * breadth) for r in range(height - 1)]
    pairs = ends + [(b, a) for a, b in ends]
    seam = lax.ppermute(jnp.where(place == 0, x[:, 1], x[:, -2]), ("row", "col"), pairs)
    return x, seam, jnp.stack([place == 0, place == count - 1]).astype(jnp.int32)


def local(
    features,
    norm_gain,
    in_weight,
    conv_weight,
    conv_bias,
    proj_weight,
    step_weight,
    step_bias,
    decay_log,
    skip_gain,
    out_gain,
    out_weight,
):
    height, width, channels = features.shape
    inner = out_weight.shape[0]
    tokens = height * width
    row_lines = height // lax.axis_size("col")
    col_lines = width // lax.axis_size("row")

    normed, row_send, col_send = pl.pallas_call(
        cut_kernel,
        out_shape=(
            jax.ShapeDtypeStruct((tokens, channels), BF16),
            jax.ShapeDtypeStruct((lax.axis_size("col"), row_lines + 2, width, channels), BF16),
            jax.ShapeDtypeStruct((lax.axis_size("row"), col_lines + 2, height, channels), BF16),
        ),
    )(features, norm_gain.reshape(1, channels))
    normed, conv_weight, proj_weight, step_weight, step_bias, decay_log, skip_gain = lax.optimization_barrier(
        (normed, conv_weight, proj_weight, step_weight, step_bias, decay_log, skip_gain)
    )

    def along(sent, ks, conv):
        return lines_of(
            *sent, in_weight, conv, conv_bias, proj_weight[ks], step_weight[ks], step_bias[ks], decay_log[ks], skip_gain[ks]
        )

    col_sent = send_lines(col_send, "row")
    row_send, _ = lax.optimization_barrier((row_send, col_sent[0]))
    row_sent = send_lines(row_send, "col")
    gate = pl.pallas_call(
        gate_kernel,
        out_shape=jax.ShapeDtypeStruct((tokens, inner), BF16),
        grid=(1,),
        in_specs=[
            pl.BlockSpec((tokens, channels), lambda i: (0, 0)),
            pl.BlockSpec((channels, inner), lambda i: (0, 1)),
        ],
        out_specs=pl.BlockSpec((tokens, inner), lambda i: (0, 0)),
        cost_estimate=pl.CostEstimate(flops=2 * tokens * channels * inner, bytes_accessed=1 << 20, transcendentals=0),
    )(normed, in_weight)
    col_y = along(col_sent, slice(2, 4), jnp.swapaxes(conv_weight, 0, 1))
    row_sent, _ = lax.optimization_barrier((row_sent, col_y))
    col_y = lax.all_to_all(col_y.reshape(lax.axis_size("row"), -1, inner), "row", 0, 0, tiled=True)
    row_y = along(row_sent, slice(0, 2), conv_weight)
    row_y = lax.all_to_all(row_y.reshape(lax.axis_size("col"), -1, inner), "col", 0, 0, tiled=True)
    return pl.pallas_call(
        end_kernel,
        out_shape=jax.ShapeDtypeStruct(features.shape, BF16),
    )(row_y.reshape(tokens, inner), col_y.reshape(tokens, inner), gate, out_gain.reshape(1, inner), out_weight)


def solution(mesh):
    in_specs = (P("row", "col", None), P(), P(), P(), P(), P(), P(), P(), P(), P(), P(), P())
    out_specs = P("row", "col", None)
    return jax.shard_map(local, mesh=mesh, in_specs=in_specs, out_specs=out_specs, check_vma=False)
```

```python
import functools

import jax
import jax.numpy as jnp
from jax import lax
from jax.experimental import pallas as pl
from jax.experimental.pallas import tpu as pltpu
from jax.sharding import PartitionSpec as P

F32 = jnp.float32
BF16 = jnp.bfloat16
LANES = 128
SLOTS = 8
LOG2E = 1.4426950408889634


def bits(value):
    assert value & (value - 1) == 0
    return value.bit_length() - 1


def one_hot(targets, width):
    lane = lax.broadcasted_iota(jnp.int32, targets[0].shape, 1)
    blocks = []
    for block in range(pl.cdiv(width, LANES)):
        hit = targets[0] == lane + block * LANES
        for other in targets[1:]:
            hit = jnp.logical_or(hit, other == lane + block * LANES)
        blocks.append(jnp.where(hit, 1.0, 0.0).astype(BF16))
    return jnp.concatenate(blocks, axis=1)[:, :width]


def rows_of(count, start=0):
    return lax.broadcasted_iota(jnp.int32, (count, LANES), 0) + start


def dot(a, b):
    return jnp.dot(a, b, preferred_element_type=F32)


def layer_norm(values, scale_gain):
    centred = values - jnp.mean(values, axis=-1, keepdims=True)
    spread = jnp.mean(centred * centred, axis=-1, keepdims=True)
    return centred * lax.rsqrt(spread + 1e-05) * scale_gain


def cut_kernel(feat_ref, gain_ref, norm_ref, rows_ref, cols_ref):
    height, width, channels = feat_ref.shape
    tile = layer_norm(feat_ref[...].reshape(height * width, channels).astype(F32), gain_ref[...]).astype(BF16)
    norm_ref[...] = tile
    row = rows_of(height * width)
    turned = dot(one_hot([((row & (height - 1)) << bits(width)) + (row >> bits(height))], height * width), tile).astype(
        BF16
    )

    def cut(out_ref, body, lines, length):
        parts, reach = out_ref.shape[0], out_ref.shape[1]
        for part in range(parts):
            for line in range(reach):
                at = part * (reach - 2) + line - 1
                if 0 <= at < lines:
                    out_ref[part, line] = body[at * length : (at + 1) * length]
                else:
                    out_ref[part, line] = jnp.zeros((length, channels), BF16)

    cut(rows_ref, tile, height, width)
    cut(cols_ref, turned, width, height)


def gate_kernel(norm_ref, weight_ref, gate_ref):
    gate_ref[...] = dot(norm_ref[...], weight_ref[...]).astype(BF16)


def line_kernel(
    lines,
    axis,
    after_ref,
    x_ref,
    seam_ref,
    weight_ref,
    conv_ref,
    conv_bias_ref,
    proj_raw_ref,
    step_raw_ref,
    bias_raw_ref,
    decay_ref,
    skip_raw_ref,
    out_ref,
    token_ref,
    inner_ref,
    active_ref,
    proj_ref,
    step_ref,
    bias_ref,
    skip_ref,
    proj_out_ref,
    s_ref,
    v_ref,
    y_ref,
    spread_ref,
):
    parts, reach, length, channels = x_ref.shape
    time = parts * length
    low = time // SLOTS
    width = weight_ref.shape[1]
    chunk = s_ref.shape[2]
    halves = width // chunk
    slot_lines = SLOTS // (2 * halves)
    states = decay_ref.shape[1]
    if axis == "row":
        across_first = lambda across, along: (along, across)
    else:
        across_first = lambda across, along: (across, along)

    place = lax.broadcasted_iota(jnp.int32, (SLOTS, chunk), 0)

    def by_slot(rows):
        found = None
        for half in range(halves):
            for way in range(2):
                row = rows(half, way)
                row = jnp.broadcast_to(row, (SLOTS, row.shape[1]))
                kind = half * 2 + way
                found = row if found is None else jnp.where(place[:, : row.shape[1]] >= kind * slot_lines, row, found)
        return found

    bias_ref[...] = by_slot(lambda half, way: bias_raw_ref[way : way + 1, half * chunk : (half + 1) * chunk])
    skip_ref[...] = by_slot(lambda half, way: skip_raw_ref[way : way + 1, half * chunk : (half + 1) * chunk])
    for half in range(halves):
        cells = slice(half * chunk, (half + 1) * chunk)
        for way in range(2):
            kind = slice((half * 2 + way) * LANES, (half * 2 + way + 1) * LANES)
            w = proj_raw_ref[way, :, cells].astype(F32)
            ranks = w[:RANK]
            rest = jnp.zeros((LANES - 3 * RANK - 2 * states, chunk), F32)
            w = jnp.concatenate([ranks, ranks, ranks, w[RANK:], rest], axis=0)
            proj_ref[:, kind] = w.T.astype(BF16)
            w = step_raw_ref[way, :, cells]
            high = w.astype(BF16).astype(F32)
            rest = jnp.zeros((LANES - 3 * RANK, chunk), F32)
            step_ref[kind, :] = jnp.concatenate([high, high, w - high, rest], axis=0).astype(BF16)

    row = rows_of(time)
    order = one_hot([((row & 7) << bits(low)) + (row >> 3)], time)
    for line in range(reach):
        x = x_ref[:, line].reshape(time, channels)
        if line == 0 or line == reach - 1:
            missing = lax.axis_index(axis) == (0 if line == 0 else lax.axis_size(axis) - 1)
            x = jnp.where(missing, seam_ref[...].reshape(time, channels), x)
        token_ref[line * time : (line + 1) * time] = dot(order, x).astype(BF16)
    inner = dot(token_ref[...], weight_ref[...]).astype(BF16).astype(F32)
    inner_ref[:, 1 : low + 1] = inner.reshape(reach, low, SLOTS, width)
    place = lax.broadcasted_iota(jnp.int32, (SLOTS, width), 0)
    for line in range(reach):
        inner_ref[line, 0] = jnp.where(place == 0, 0.0, pltpu.roll(inner_ref[line, low], 1, 0))
        inner_ref[line, low + 1] = jnp.where(place == SLOTS - 1, 0.0, pltpu.roll(inner_ref[line, 1], SLOTS - 1, 0))

    def convolve(pair, _):
        for group in range(width // (2 * LANES)):
            cells = slice(group * 2 * LANES, (group + 1) * 2 * LANES)
            half = (group * 2 * LANES) // chunk
            base = group * 2 * LANES - half * chunk
            bias = jnp.broadcast_to(conv_bias_ref[:, cells], (SLOTS, 2 * LANES))
            totals = [[bias for _ in range(2)] for _ in range(lines)]
            for across in range(3):
                for along in range(3):
                    first, second = across_first(across, along)
                    tap = jnp.broadcast_to(conv_ref[first, second : second + 1, cells], (SLOTS, 2 * LANES))
                    for line in range(lines):
                        for sub in range(2):
                            totals[line][sub] += inner_ref[line + across, 2 * pair + sub + along, :, cells] * tap
            for line in range(lines):
                value = jnp.concatenate(totals[line], axis=0)
                value = 0.5 * value
                value = value * jnp.tanh(value) + value
                value = value.astype(BF16)
                for piece in range(2):
                    at = base + piece * LANES
                    start = ((half + at // chunk) * lines + line) * time
                    start = pl.multiple_of(start + pair * (2 * SLOTS), 2 * SLOTS)
                    active_ref[pl.ds(start, 2 * SLOTS), at % chunk : at % chunk + LANES] = value[
                        :, piece * LANES : (piece + 1) * LANES
                    ]
        return 0

    lax.fori_loop(0, low // 2, convolve, 0)

    piece = 256
    for first in range(0, time * SLOTS, piece):
        row = rows_of(piece, first)
        now = row >> 3
        slot = row & 7
        line = slot & (slot_lines - 1)
        back = (slot >> bits(slot_lines)) & 1
        half = slot >> bits(2 * slot_lines)
        when = jnp.where(back == 1, time - 1 - now, now)
        source = half * (lines * time) + line * time + ((when & (low - 1)) << 3) + (when >> bits(low))
        if slot_lines > lines:
            source = jnp.where(line < lines, source, -1)
        u = dot(one_hot([source], halves * lines * time), active_ref[...])
        steps = pl.ds(first // SLOTS, piece // SLOTS)
        v_ref[steps] = u.reshape(piece // SLOTS, SLOTS, chunk)
        kind = slot >> bits(slot_lines)
        projected = dot(u.astype(BF16), proj_ref[...])
        p = projected[:, :LANES]
        for other in range(1, 2 * halves):
            p = jnp.where(kind == other, projected[:, other * LANES : (other + 1) * LANES], p)
        if halves == 2:
            p = p.reshape(piece // SLOTS, SLOTS, LANES)
            p = p + pltpu.roll(p, SLOTS // 2, 1)
            p = p.reshape(piece, LANES)
        proj_out_ref[steps] = p.reshape(piece // SLOTS, SLOTS, LANES)
        high = p.astype(BF16).astype(F32)
        lane = lax.broadcasted_iota(jnp.int32, p.shape, 1)
        mixed = jnp.where(jnp.logical_and(lane >= RANK, lane < 2 * RANK), p - high, high)
        stacked = jnp.concatenate([jnp.where(kind == k, mixed, 0.0).astype(BF16) for k in range(2 * halves)], axis=1)
        s_ref[steps] = dot(stacked, step_ref[...]).reshape(piece // SLOTS, SLOTS, chunk)

    def soften(lap, _):
        for sub in range(4):
            t = lap * 4 + sub
            for g in range(chunk // LANES):
                cells = slice(g * LANES, (g + 1) * LANES)
                before = s_ref[t, :, cells] + bias_ref[:, cells]
                small = jnp.exp(-jnp.abs(before))
                series = small * (1.0 + small * (-0.5 + small * (1.0 / 3.0 - 0.25 * small)))
                step = jnp.maximum(before, 0.0) + jnp.where(small < 0.01, series, jnp.log(1.0 + small))
                u = v_ref[t, :, cells]
                s_ref[t, :, cells] = step
                v_ref[t, :, cells] = step * u
                y_ref[t, :, cells] = skip_ref[:, cells] * u
        return 0

    lax.fori_loop(0, time // 4, soften, 0)

    groups = chunk // LANES
    at_once = max(1, 12 // groups)
    unroll = 8
    laps = time // unroll
    place = lax.broadcasted_iota(jnp.int32, (SLOTS, LANES), 0)
    for first in range(0, states, at_once):
        rates = []
        for n in range(first, first + at_once):
            rates.append([])
            for g in range(groups):
                rate = by_slot(
                    lambda half, way: decay_ref[way, n : n + 1, half * chunk + g * LANES : half * chunk + (g + 1) * LANES]
                )
                rates[-1].append(-LOG2E * jnp.exp(rate))

        def spread(lap):
            found = []
            for sub in range(unroll):
                coefs = proj_out_ref[lap * unroll + sub]
                for kind in range(2):
                    for n in range(at_once):
                        lane = 3 * RANK + kind * states + first + n
                        found.append(jnp.broadcast_to(coefs[:, lane : lane + 1], (SLOTS, LANES)))
            return found

        def keep(slot, found):
            for k, value in enumerate(found):
                spread_ref[slot, k] = value

        def advance(lap, hidden):
            hidden = list(hidden)
            slot = lap & 1
            ahead = spread(jnp.minimum(lap + 1, laps - 1))
            for sub in range(unroll):
                t = lap * unroll + sub
                enter = [spread_ref[slot, sub * 2 * at_once + n] for n in range(at_once)]
                leave = [spread_ref[slot, sub * 2 * at_once + at_once + n] for n in range(at_once)]
                for g in range(groups):
                    cells = pl.ds(g * LANES, LANES)
                    step = s_ref[t, :, cells]
                    value = v_ref[t, :, cells]
                    y = y_ref[t, :, cells]
                    for n in range(at_once):
                        k = n * groups + g
                        h = jnp.exp2(step * rates[n][g]) * hidden[k] + value * enter[n]
                        hidden[k] = h
                        y = y + h * leave[n]
                    y_ref[t, :, cells] = y
            keep(1 - slot, ahead)
            return tuple(hidden)

        keep(0, spread(0))
        zero = jnp.zeros((SLOTS, LANES), F32)
        lax.fori_loop(0, laps, advance, (zero,) * (at_once * groups))

    out_ref[...] = y_ref[...].reshape(time * SLOTS, chunk).astype(BF16)


def join_kernel(parts, lines, after_ref, scanned_ref, out_ref):
    length = out_ref.shape[0] // (parts * lines)
    time = parts * length
    chunk = scanned_ref.shape[1]
    halves = out_ref.shape[1] // chunk
    slot_lines = SLOTS // (2 * halves)
    row = rows_of(lines * time)
    line = (row >> bits(length)) & (lines - 1)
    now = ((row >> bits(lines * length)) << bits(length)) + (row & (length - 1))
    for half in range(halves):
        ahead = now * SLOTS + (half * 2 * slot_lines) + line
        behind = (time - 1 - now) * SLOTS + (half * 2 * slot_lines + slot_lines) + line
        joined = dot(one_hot([ahead, behind], time * SLOTS), scanned_ref[...])
        out_ref[:, half * chunk : (half + 1) * chunk] = joined.astype(BF16)


def join(scanned, parts, lines, length, width, after):
    return pl.pallas_call(
        functools.partial(join_kernel, parts, lines),
        out_shape=jax.ShapeDtypeStruct((parts * lines * length, width), BF16),
        in_specs=[pl.BlockSpec(memory_space=pl.ANY), pl.BlockSpec(memory_space=pltpu.VMEM)],
        out_specs=pl.BlockSpec(memory_space=pltpu.VMEM),
        compiler_params=pltpu.CompilerParams(vmem_limit_bytes=50 * 1024 * 1024),
    )(after, scanned)


RANK = 24


def lines_of(axis, after, x, seam, in_weight, conv, conv_bias, proj, step_weight, step_bias, decay_log, skip):
    parts, reach, length, channels = x.shape
    lines = reach - 2
    time = parts * length
    width = conv.shape[2]
    states = decay_log.shape[2]
    assert step_weight.shape[1] == RANK
    halves = 1 if lines >= 4 else 2
    assert lines <= SLOTS // (2 * halves)
    chunk = width // halves
    way = 0 if axis == "col" else 1
    at_once = max(1, 12 // (chunk // LANES))

    def all_of(*shape):
        return pl.BlockSpec(shape, lambda i: (0,) * len(shape))

    def pair(*shape):
        return pl.BlockSpec((2,) + shape, lambda i: (way,) + (0,) * len(shape))

    flops = 2 * time * (reach * channels * width + SLOTS * width * 256)
    return pl.pallas_call(
        functools.partial(line_kernel, lines, axis),
        out_shape=jax.ShapeDtypeStruct((time * SLOTS, chunk), BF16),
        grid=(1,),
        in_specs=[
            pl.BlockSpec(memory_space=pl.ANY),
            all_of(parts, reach, length, channels),
            all_of(parts, length, channels),
            all_of(channels, width),
            all_of(3, 3, width),
            all_of(1, width),
            pair(RANK + 2 * states, width),
            pair(RANK, width),
            pl.BlockSpec((None, 2, width), lambda i: (way, 0, 0)),
            pair(states, width),
            pl.BlockSpec((None, 2, width), lambda i: (way, 0, 0)),
        ],
        out_specs=all_of(time * SLOTS, chunk),
        scratch_shapes=[
            pltpu.VMEM((reach * time, channels), BF16),
            pltpu.VMEM((reach, time // SLOTS + 2, SLOTS, width), F32),
            pltpu.VMEM((halves * lines * time, chunk), BF16),
            pltpu.VMEM((chunk, halves * 2 * LANES), BF16),
            pltpu.VMEM((halves * 2 * LANES, chunk), BF16),
            pltpu.VMEM((SLOTS, chunk), F32),
            pltpu.VMEM((SLOTS, chunk), F32),
            pltpu.VMEM((time, SLOTS, LANES), F32),
            pltpu.VMEM((time, SLOTS, chunk), F32),
            pltpu.VMEM((time, SLOTS, chunk), F32),
            pltpu.VMEM((time, SLOTS, chunk), F32),
            pltpu.VMEM((2, 8 * 2 * at_once, SLOTS, LANES), F32),
        ],
        compiler_params=pltpu.CompilerParams(vmem_limit_bytes=50 * 1024 * 1024),
        cost_estimate=pl.CostEstimate(
            flops=flops, bytes_accessed=4 * 1024 * 1024, transcendentals=time * SLOTS * chunk * states
        ),
    )(
        after,
        x,
        seam,
        in_weight,
        conv,
        conv_bias.reshape(1, width),
        jnp.swapaxes(proj, 1, 2),
        step_weight,
        step_bias.reshape(2, 2, width),
        jnp.swapaxes(decay_log, 1, 2),
        skip.reshape(2, 2, width),
    )


def end_kernel(rows_ref, cols_ref, gate_ref, gain_ref, weight_ref, out_ref):
    height, width, channels = out_ref.shape
    row = rows_of(height * width)
    source = ((row & (width - 1)) << bits(height)) + (row >> bits(width))
    combined = rows_ref[...].astype(F32) + dot(one_hot([source], height * width), cols_ref[...])
    gate = gate_ref[...].astype(F32)
    gated = layer_norm(combined, gain_ref[...]) * (gate / (1.0 + jnp.exp(-gate)))
    out = dot(gated.astype(BF16), weight_ref[...]).astype(BF16)
    out_ref[...] = out.reshape(height, width, channels)


def send_lines(send, axis):
    x = lax.all_to_all(send, axis, 0, 0, tiled=True)
    count, place = lax.axis_size(axis), lax.axis_index(axis)
    height, breadth = lax.axis_size("row"), lax.axis_size("col")
    if axis == "row":
        ends = [((count - 1) * breadth + c, c + 1) for c in range(breadth - 1)]
    else:
        ends = [(r * breadth + count - 1, (r + 1) * breadth) for r in range(height - 1)]
    pairs = ends + [(b, a) for a, b in ends]
    seam = lax.ppermute(jnp.where(place == 0, x[:, 1], x[:, -2]), ("row", "col"), pairs)
    return x, seam


def local(
    features,
    norm_gain,
    in_weight,
    conv_weight,
    conv_bias,
    proj_weight,
    step_weight,
    step_bias,
    decay_log,
    skip_gain,
    out_gain,
    out_weight,
):
    height, width, channels = features.shape
    inner = out_weight.shape[0]
    tokens = height * width
    row_lines = height // lax.axis_size("col")
    col_lines = width // lax.axis_size("row")

    normed, row_send, col_send = pl.pallas_call(
        cut_kernel,
        out_shape=(
            jax.ShapeDtypeStruct((tokens, channels), BF16),
            jax.ShapeDtypeStruct((lax.axis_size("col"), row_lines + 2, width, channels), BF16),
            jax.ShapeDtypeStruct((lax.axis_size("row"), col_lines + 2, height, channels), BF16),
        ),
    )(features, norm_gain.reshape(1, channels))
    weights = (in_weight, conv_weight, conv_bias, proj_weight, step_weight, step_bias, decay_log, skip_gain)
    col_sent = send_lines(col_send, "row")
    row_sent = send_lines(row_send, "col")
    gate = pl.pallas_call(
        gate_kernel,
        out_shape=jax.ShapeDtypeStruct((tokens, inner), BF16),
        grid=(1,),
        in_specs=[
            pl.BlockSpec((tokens, channels), lambda i: (0, 0)),
            pl.BlockSpec((channels, inner), lambda i: (0, 1)),
        ],
        out_specs=pl.BlockSpec((tokens, inner), lambda i: (0, 0)),
        cost_estimate=pl.CostEstimate(flops=2 * tokens * channels * inner, bytes_accessed=1 << 20, transcendentals=0),
    )(normed, in_weight)
    parts = lax.axis_size("row")
    col_y = lines_of("row", normed, *col_sent, *weights)
    joined = join(col_y, parts, col_lines, height, inner, normed)
    col_y = lax.all_to_all(joined.reshape(parts, -1, inner), "row", 0, 0, tiled=True)
    parts = lax.axis_size("col")
    row_y = lines_of("col", joined, *row_sent, *weights)
    row_y = join(row_y, parts, row_lines, width, inner, col_y)
    row_y = lax.all_to_all(row_y.reshape(parts, -1, inner), "col", 0, 0, tiled=True)
    return pl.pallas_call(
        end_kernel,
        out_shape=jax.ShapeDtypeStruct(features.shape, BF16),
    )(row_y.reshape(tokens, inner), col_y.reshape(tokens, inner), gate, out_gain.reshape(1, inner), out_weight)


def solution(mesh):
    in_specs = (P("row", "col", None), P(), P(), P(), P(), P(), P(), P(), P(), P(), P(), P())
    out_specs = P("row", "col", None)
    return jax.shard_map(local, mesh=mesh, in_specs=in_specs, out_specs=out_specs, check_vma=False)
```

```python
import functools

import jax
import jax.numpy as jnp
from jax import lax
from jax.experimental import pallas as pl
from jax.experimental.pallas import tpu as pltpu
from jax.sharding import PartitionSpec as P

F32 = jnp.float32
BF16 = jnp.bfloat16
LANES = 128
SLOTS = 8
LOG2E = 1.4426950408889634


def bits(value):
    assert value & (value - 1) == 0
    return value.bit_length() - 1


def one_hot(targets, width):
    lane = lax.broadcasted_iota(jnp.int32, targets[0].shape, 1)
    blocks = []
    for block in range(pl.cdiv(width, LANES)):
        hit = targets[0] == lane + block * LANES
        for other in targets[1:]:
            hit = jnp.logical_or(hit, other == lane + block * LANES)
        blocks.append(jnp.where(hit, 1.0, 0.0).astype(BF16))
    return jnp.concatenate(blocks, axis=1)[:, :width]


def rows_of(count, start=0):
    return lax.broadcasted_iota(jnp.int32, (count, LANES), 0) + start


def dot(a, b):
    return jnp.dot(a, b, preferred_element_type=F32)


def layer_norm(values, scale_gain):
    centred = values - jnp.mean(values, axis=-1, keepdims=True)
    spread = jnp.mean(centred * centred, axis=-1, keepdims=True)
    return centred * lax.rsqrt(spread + 1e-05) * scale_gain


def flip(axis):
    other = "col" if axis == "row" else "row"
    return (lax.axis_index(other) & 1) * (lax.axis_size(axis) - 1)


def cut_kernel(feat_ref, gain_ref, norm_ref, rows_ref, cols_ref):
    height, width, channels = feat_ref.shape
    tile = layer_norm(feat_ref[...].reshape(height * width, channels).astype(F32), gain_ref[...][None]).astype(BF16)
    norm_ref[...] = tile
    row = rows_of(height * width)
    turned = dot(one_hot([((row & (height - 1)) << bits(width)) + (row >> bits(height))], height * width), tile).astype(
        BF16
    )

    def cut(axis, out_ref, body, lines, length):
        parts, reach = out_ref.shape[0], out_ref.shape[1]
        turn = flip(axis)
        for part in range(parts):
            to = part ^ turn
            for line in range(reach):
                at = part * (reach - 2) + line - 1
                if 0 <= at < lines:
                    out_ref[to, line] = body[at * length : (at + 1) * length]
                else:
                    out_ref[to, line] = jnp.zeros((length, channels), BF16)

    cut("col", rows_ref, tile, height, width)
    cut("row", cols_ref, turned, width, height)


def gate_kernel(norm_ref, weight_ref, gate_ref):
    gate_ref[...] = dot(norm_ref[...], weight_ref[...]).astype(BF16)


def line_kernel(
    lines,
    axis,
    after_ref,
    x_ref,
    seam_ref,
    weight_ref,
    conv_ref,
    conv_bias_ref,
    proj_raw_ref,
    step_raw_ref,
    bias_raw_ref,
    decay_ref,
    skip_raw_ref,
    out_ref,
    token_ref,
    inner_ref,
    active_ref,
    proj_ref,
    step_ref,
    bias_ref,
    skip_ref,
    proj_out_ref,
    s_ref,
    v_ref,
    y_ref,
):
    parts, reach, length, channels = x_ref.shape
    time = parts * length
    low = time // SLOTS
    width = weight_ref.shape[1]
    chunk = s_ref.shape[2]
    halves = width // chunk
    slot_lines = SLOTS // (2 * halves)
    states = decay_ref.shape[1]
    if axis == "row":
        across_first = lambda across, along: (along, across)
    else:
        across_first = lambda across, along: (across, along)

    place = lax.broadcasted_iota(jnp.int32, (SLOTS, chunk), 0)

    def by_slot(rows):
        found = None
        for half in range(halves):
            for way in range(2):
                row = rows(half, way)
                row = jnp.broadcast_to(row, (SLOTS, row.shape[1]))
                kind = half * 2 + way
                found = row if found is None else jnp.where(place[:, : row.shape[1]] >= kind * slot_lines, row, found)
        return found

    bias_ref[...] = by_slot(lambda half, way: bias_raw_ref[way : way + 1, half * chunk : (half + 1) * chunk])
    skip_ref[...] = by_slot(lambda half, way: skip_raw_ref[way : way + 1, half * chunk : (half + 1) * chunk])
    for half in range(halves):
        cells = slice(half * chunk, (half + 1) * chunk)
        for way in range(2):
            kind = slice((half * 2 + way) * LANES, (half * 2 + way + 1) * LANES)
            w = proj_raw_ref[way, :, cells].astype(F32)
            ranks = w[:RANK]
            rest = jnp.zeros((LANES - 3 * RANK - 2 * states, chunk), F32)
            w = jnp.concatenate([ranks, ranks, ranks, w[RANK:], rest], axis=0)
            proj_ref[:, kind] = w.T.astype(BF16)
            w = step_raw_ref[way, :, cells]
            high = w.astype(BF16).astype(F32)
            rest = jnp.zeros((LANES - 3 * RANK, chunk), F32)
            step_ref[kind, :] = jnp.concatenate([high, high, w - high, rest], axis=0).astype(BF16)

    row = rows_of(time)
    order = one_hot([((row & 7) << bits(low)) + (row >> 3)], time)
    for line in range(reach):
        x = x_ref[:, line].reshape(time, channels)
        if line == 0 or line == reach - 1:
            place = lax.axis_index(axis) ^ flip(axis)
            missing = place == (0 if line == 0 else lax.axis_size(axis) - 1)
            x = jnp.where(missing, seam_ref[...].reshape(time, channels), x)
        token_ref[line * time : (line + 1) * time] = dot(order, x).astype(BF16)
    inner = dot(token_ref[...], weight_ref[...]).astype(BF16).astype(F32)
    inner_ref[:, 1 : low + 1] = inner.reshape(reach, low, SLOTS, width)
    place = lax.broadcasted_iota(jnp.int32, (SLOTS, width), 0)
    for line in range(reach):
        inner_ref[line, 0] = jnp.where(place == 0, 0.0, pltpu.roll(inner_ref[line, low], 1, 0))
        inner_ref[line, low + 1] = jnp.where(place == SLOTS - 1, 0.0, pltpu.roll(inner_ref[line, 1], SLOTS - 1, 0))

    def convolve(pair, _):
        for group in range(width // (2 * LANES)):
            cells = slice(group * 2 * LANES, (group + 1) * 2 * LANES)
            half = (group * 2 * LANES) // chunk
            base = group * 2 * LANES - half * chunk
            bias = jnp.broadcast_to(conv_bias_ref[:, cells], (SLOTS, 2 * LANES))
            totals = [[bias for _ in range(2)] for _ in range(lines)]
            for across in range(3):
                for along in range(3):
                    first, second = across_first(across, along)
                    tap = jnp.broadcast_to(conv_ref[first, second : second + 1, cells], (SLOTS, 2 * LANES))
                    for line in range(lines):
                        for sub in range(2):
                            totals[line][sub] += inner_ref[line + across, 2 * pair + sub + along, :, cells] * tap
            for line in range(lines):
                value = jnp.concatenate(totals[line], axis=0)
                value = 0.5 * value
                value = value * jnp.tanh(value) + value
                value = value.astype(BF16)
                for piece in range(2):
                    at = base + piece * LANES
                    start = ((half + at // chunk) * lines + line) * time
                    start = pl.multiple_of(start + pair * (2 * SLOTS), 2 * SLOTS)
                    active_ref[pl.ds(start, 2 * SLOTS), at % chunk : at % chunk + LANES] = value[
                        :, piece * LANES : (piece + 1) * LANES
                    ]
        return 0

    lax.fori_loop(0, low // 2, convolve, 0)

    piece = 256
    for first in range(0, time * SLOTS, piece):
        row = rows_of(piece, first)
        now = row >> 3
        slot = row & 7
        line = slot & (slot_lines - 1)
        back = (slot >> bits(slot_lines)) & 1
        half = slot >> bits(2 * slot_lines)
        when = jnp.where(back == 1, time - 1 - now, now)
        source = half * (lines * time) + line * time + ((when & (low - 1)) << 3) + (when >> bits(low))
        if slot_lines > lines:
            source = jnp.where(line < lines, source, -1)
        u = dot(one_hot([source], halves * lines * time), active_ref[...])
        steps = pl.ds(first // SLOTS, piece // SLOTS)
        v_ref[steps] = u.reshape(piece // SLOTS, SLOTS, chunk)
        kind = slot >> bits(slot_lines)
        projected = dot(u.astype(BF16), proj_ref[...])
        p = projected[:, :LANES]
        for other in range(1, 2 * halves):
            p = jnp.where(kind == other, projected[:, other * LANES : (other + 1) * LANES], p)
        if halves == 2:
            p = p.reshape(piece // SLOTS, SLOTS, LANES)
            p = p + pltpu.roll(p, SLOTS // 2, 1)
            p = p.reshape(piece, LANES)
        proj_out_ref[steps] = p.reshape(piece // SLOTS, SLOTS, LANES)
        high = p.astype(BF16).astype(F32)
        lane = lax.broadcasted_iota(jnp.int32, p.shape, 1)
        mixed = jnp.where(jnp.logical_and(lane >= RANK, lane < 2 * RANK), p - high, high)
        stacked = jnp.concatenate([jnp.where(kind == k, mixed, 0.0).astype(BF16) for k in range(2 * halves)], axis=1)
        s_ref[steps] = dot(stacked, step_ref[...]).reshape(piece // SLOTS, SLOTS, chunk)

    def soften(lap, _):
        for sub in range(8):
            t = lap * 8 + sub
            for g in range(chunk // LANES):
                cells = slice(g * LANES, (g + 1) * LANES)
                before = s_ref[t, :, cells] + bias_ref[:, cells]
                small = jnp.exp(-jnp.abs(before))
                log1p = jnp.where(small < 0.001, small - 0.5 * small * small, jnp.log(1.0 + small))
                step = jnp.maximum(before, 0.0) + log1p
                u = v_ref[t, :, cells]
                s_ref[t, :, cells] = step
                v_ref[t, :, cells] = step * u
                y_ref[t, :, cells] = skip_ref[:, cells] * u
        return 0

    lax.fori_loop(0, time // 8, soften, 0)

    groups = chunk // LANES
    at_once = max(1, 12 // groups)
    unroll = 8
    laps = time // unroll
    place = lax.broadcasted_iota(jnp.int32, (SLOTS, LANES), 0)
    for first in range(0, states, at_once):
        rates = []
        for n in range(first, first + at_once):
            rates.append([])
            for g in range(groups):
                rate = by_slot(
                    lambda half, way: decay_ref[way, n : n + 1, half * chunk + g * LANES : half * chunk + (g + 1) * LANES]
                )
                rates[-1].append(-LOG2E * jnp.exp(rate))

        def advance(lap, hidden):
            hidden = list(hidden)
            for sub in range(unroll):
                t = lap * unroll + sub
                coefs = proj_out_ref[t]

                def spread(lane):
                    return jnp.broadcast_to(coefs[:, lane : lane + 1], (SLOTS, LANES))

                enter = [spread(3 * RANK + first + n) for n in range(at_once)]
                leave = [spread(3 * RANK + states + first + n) for n in range(at_once)]
                for g in range(groups):
                    cells = pl.ds(g * LANES, LANES)
                    step = s_ref[t, :, cells]
                    value = v_ref[t, :, cells]
                    y = y_ref[t, :, cells]
                    for n in range(at_once):
                        k = n * groups + g
                        h = jnp.exp2(step * rates[n][g]) * hidden[k] + value * enter[n]
                        hidden[k] = h
                        y = y + h * leave[n]
                    y_ref[t, :, cells] = y
            return tuple(hidden)

        zero = jnp.zeros((SLOTS, LANES), F32)
        lax.fori_loop(0, laps, advance, (zero,) * (at_once * groups))

    out_ref[...] = y_ref[...].reshape(time * SLOTS, chunk).astype(BF16)


def join_kernel(parts, lines, after_ref, scanned_ref, out_ref):
    length = out_ref.shape[0] // (parts * lines)
    time = parts * length
    chunk = scanned_ref.shape[1]
    halves = out_ref.shape[1] // chunk
    slot_lines = SLOTS // (2 * halves)
    row = rows_of(lines * time)
    line = (row >> bits(length)) & (lines - 1)
    now = ((row >> bits(lines * length)) << bits(length)) + (row & (length - 1))
    for half in range(halves):
        ahead = now * SLOTS + (half * 2 * slot_lines) + line
        behind = (time - 1 - now) * SLOTS + (half * 2 * slot_lines + slot_lines) + line
        joined = dot(one_hot([ahead, behind], time * SLOTS), scanned_ref[...])
        out_ref[:, half * chunk : (half + 1) * chunk] = joined.astype(BF16)


def join(scanned, parts, lines, length, width, after):
    return pl.pallas_call(
        functools.partial(join_kernel, parts, lines),
        out_shape=jax.ShapeDtypeStruct((parts * lines * length, width), BF16),
        in_specs=[pl.BlockSpec(memory_space=pl.ANY), pl.BlockSpec(memory_space=pltpu.VMEM)],
        out_specs=pl.BlockSpec(memory_space=pltpu.VMEM),
        compiler_params=pltpu.CompilerParams(vmem_limit_bytes=50 * 1024 * 1024),
    )(after, scanned)


RANK = 24


def lines_of(axis, after, x, seam, in_weight, conv, conv_bias, proj, step_weight, step_bias, decay_log, skip):
    parts, reach, length, channels = x.shape
    lines = reach - 2
    time = parts * length
    width = conv.shape[2]
    states = decay_log.shape[2]
    assert step_weight.shape[1] == RANK
    halves = 1 if lines >= 4 else 2
    assert lines <= SLOTS // (2 * halves)
    chunk = width // halves
    way = 0 if axis == "col" else 1

    def all_of(*shape):
        return pl.BlockSpec(shape, lambda i: (0,) * len(shape))

    def pair(*shape):
        return pl.BlockSpec((2,) + shape, lambda i: (way,) + (0,) * len(shape))

    flops = 2 * time * (reach * channels * width + SLOTS * width * 256)
    return pl.pallas_call(
        functools.partial(line_kernel, lines, axis),
        out_shape=jax.ShapeDtypeStruct((time * SLOTS, chunk), BF16),
        grid=(1,),
        in_specs=[
            pl.BlockSpec(memory_space=pl.ANY),
            all_of(parts, reach, length, channels),
            all_of(parts, length, channels),
            all_of(channels, width),
            all_of(3, 3, width),
            all_of(1, width),
            pair(RANK + 2 * states, width),
            pair(RANK, width),
            pl.BlockSpec((None, 2, width), lambda i: (way, 0, 0)),
            pair(states, width),
            pl.BlockSpec((None, 2, width), lambda i: (way, 0, 0)),
        ],
        out_specs=all_of(time * SLOTS, chunk),
        scratch_shapes=[
            pltpu.VMEM((reach * time, channels), BF16),
            pltpu.VMEM((reach, time // SLOTS + 2, SLOTS, width), F32),
            pltpu.VMEM((halves * lines * time, chunk), BF16),
            pltpu.VMEM((chunk, halves * 2 * LANES), BF16),
            pltpu.VMEM((halves * 2 * LANES, chunk), BF16),
            pltpu.VMEM((SLOTS, chunk), F32),
            pltpu.VMEM((SLOTS, chunk), F32),
            pltpu.VMEM((time, SLOTS, LANES), F32),
            pltpu.VMEM((time, SLOTS, chunk), F32),
            pltpu.VMEM((time, SLOTS, chunk), F32),
            pltpu.VMEM((time, SLOTS, chunk), F32),
        ],
        compiler_params=pltpu.CompilerParams(vmem_limit_bytes=50 * 1024 * 1024),
        cost_estimate=pl.CostEstimate(
            flops=flops, bytes_accessed=4 * 1024 * 1024, transcendentals=time * SLOTS * chunk * states
        ),
    )(
        after,
        x,
        seam,
        in_weight,
        conv,
        conv_bias.reshape(1, width),
        jnp.swapaxes(proj, 1, 2),
        step_weight,
        step_bias.reshape(2, 2, width),
        jnp.swapaxes(decay_log, 1, 2),
        skip.reshape(2, 2, width),
    )


def end_kernel(rows_ref, cols_ref, gate_ref, gain_ref, weight_ref, out_ref):
    height, width, channels = out_ref.shape
    row = rows_of(height * width)
    turn = flip("row") * (width // lax.axis_size("row"))
    source = (((row & (width - 1)) ^ turn) << bits(height)) + (row >> bits(width))
    turn = flip("col")
    rows = jnp.concatenate([rows_ref[part ^ turn] for part in range(rows_ref.shape[0])], axis=0)
    combined = rows.astype(F32) + dot(one_hot([source], height * width), cols_ref[...])
    gate = gate_ref[...].astype(F32)
    gated = layer_norm(combined, gain_ref[...][None]) * (gate / (1.0 + jnp.exp(-gate)))
    out = dot(gated.astype(BF16), weight_ref[...]).astype(BF16)
    out_ref[...] = out.reshape(height, width, channels)


def send_lines(send, axis):
    x = lax.all_to_all(send, axis, 0, 0, tiled=True)
    count = lax.axis_size(axis)
    height, breadth = lax.axis_size("row"), lax.axis_size("col")
    if axis == "row":
        at = lambda group: (0 if group & 1 else count - 1) * breadth
        ends = [(at(c) + c, at(c) + c + 1) for c in range(breadth - 1)]
    else:
        at = lambda group: 0 if group & 1 else count - 1
        ends = [(at(r) + r * breadth, at(r) + (r + 1) * breadth) for r in range(height - 1)]
    pairs = ends + [(b, a) for a, b in ends]
    place = lax.axis_index(axis) ^ flip(axis)
    seam = lax.ppermute(jnp.where(place == 0, x[:, 1], x[:, -2]), ("row", "col"), pairs)
    return x, seam


def local(
    features,
    norm_gain,
    in_weight,
    conv_weight,
    conv_bias,
    proj_weight,
    step_weight,
    step_bias,
    decay_log,
    skip_gain,
    out_gain,
    out_weight,
):
    height, width, channels = features.shape
    inner = out_weight.shape[0]
    tokens = height * width
    row_lines = height // lax.axis_size("col")
    col_lines = width // lax.axis_size("row")

    normed, row_send, col_send = pl.pallas_call(
        cut_kernel,
        out_shape=(
            jax.ShapeDtypeStruct((tokens, channels), BF16),
            jax.ShapeDtypeStruct((lax.axis_size("col"), row_lines + 2, width, channels), BF16),
            jax.ShapeDtypeStruct((lax.axis_size("row"), col_lines + 2, height, channels), BF16),
        ),
    )(features, norm_gain)
    weights = (in_weight, conv_weight, conv_bias, proj_weight, step_weight, step_bias, decay_log, skip_gain)
    col_sent = send_lines(col_send, "row")
    row_sent = send_lines(row_send, "col")
    gate = pl.pallas_call(
        gate_kernel,
        out_shape=jax.ShapeDtypeStruct((tokens, inner), BF16),
        grid=(1,),
        in_specs=[
            pl.BlockSpec((tokens, channels), lambda i: (0, 0)),
            pl.BlockSpec((channels, inner), lambda i: (0, 1)),
        ],
        out_specs=pl.BlockSpec((tokens, inner), lambda i: (0, 0)),
        cost_estimate=pl.CostEstimate(flops=2 * tokens * channels * inner, bytes_accessed=1 << 20, transcendentals=0),
    )(normed, in_weight)
    parts = lax.axis_size("row")
    col_y = lines_of("row", normed, *col_sent, *weights)
    joined = join(col_y, parts, col_lines, height, inner, row_sent[1])
    col_y = lax.all_to_all(joined.reshape(parts, -1, inner), "row", 0, 0, tiled=True)
    parts = lax.axis_size("col")
    row_y = lines_of("col", joined, *row_sent, *weights)
    row_y = join(row_y, parts, row_lines, width, inner, col_y)
    row_y = lax.all_to_all(row_y.reshape(parts, -1, inner), "col", 0, 0, tiled=True)
    return pl.pallas_call(
        end_kernel,
        out_shape=jax.ShapeDtypeStruct(features.shape, BF16),
    )(row_y, col_y.reshape(tokens, inner), gate, out_gain, out_weight)


def solution(mesh):
    in_specs = (P("row", "col", None), P(), P(), P(), P(), P(), P(), P(), P(), P(), P(), P())
    out_specs = P("row", "col", None)
    return jax.shard_map(local, mesh=mesh, in_specs=in_specs, out_specs=out_specs, check_vma=False)
```

```python
import functools

import jax
import jax.numpy as jnp
from jax import lax
from jax.experimental import pallas as pl
from jax.experimental.pallas import tpu as pltpu
from jax.sharding import PartitionSpec as P

F32 = jnp.float32
BF16 = jnp.bfloat16
LANES = 128
SLOTS = 8
LOG2E = 1.4426950408889634


def bits(value):
    assert value & (value - 1) == 0
    return value.bit_length() - 1


def one_hot(targets, width):
    lane = lax.broadcasted_iota(jnp.int32, targets[0].shape, 1)
    blocks = []
    for block in range(pl.cdiv(width, LANES)):
        hit = targets[0] == lane + block * LANES
        for other in targets[1:]:
            hit = jnp.logical_or(hit, other == lane + block * LANES)
        blocks.append(jnp.where(hit, 1.0, 0.0).astype(BF16))
    return jnp.concatenate(blocks, axis=1)[:, :width]


def rows_of(count, start=0):
    return lax.broadcasted_iota(jnp.int32, (count, LANES), 0) + start


def dot(a, b):
    return jnp.dot(a, b, preferred_element_type=F32)


def layer_norm(values, scale_gain):
    centred = values - jnp.mean(values, axis=-1, keepdims=True)
    spread = jnp.mean(centred * centred, axis=-1, keepdims=True)
    return centred * lax.rsqrt(spread + 1e-05) * scale_gain


def flip(axis):
    other = "col" if axis == "row" else "row"
    return (lax.axis_index(other) & 1) * (lax.axis_size(axis) - 1)


def cut_kernel(feat_ref, gain_ref, norm_ref, cols_ref, *row_refs):
    height, width, channels = feat_ref.shape
    tile = layer_norm(feat_ref[...].reshape(height * width, channels).astype(F32), gain_ref[...][None]).astype(BF16)
    norm_ref[...] = tile
    reach = row_refs[0].shape[0]
    turn = flip("col") ^ lax.axis_index("col")
    for part, row_ref in enumerate(row_refs):
        for line in range(reach):
            at = jnp.clip((part ^ turn) * (reach - 2) + line - 1, 0, height - 1)
            row_ref[line] = norm_ref[pl.ds(pl.multiple_of(at * width, width), width)]
    row = rows_of(height * width)
    turned = dot(one_hot([((row & (height - 1)) << bits(width)) + (row >> bits(height))], height * width), tile).astype(
        BF16
    )
    reach = cols_ref.shape[1]
    turn = flip("row")
    for part in range(cols_ref.shape[0]):
        for line in range(reach):
            at = min(max(part * (reach - 2) + line - 1, 0), width - 1)
            cols_ref[part ^ turn, line] = turned[at * height : (at + 1) * height]


def gate_kernel(norm_ref, weight_ref, gate_ref):
    gate_ref[...] = dot(norm_ref[...], weight_ref[...]).astype(BF16)


def by_slot(halves, rows):
    found = None
    for kind in range(halves * 2):
        row = rows(kind >> 1, kind & 1)
        row = jnp.broadcast_to(row, (SLOTS, row.shape[1]))
        slot = lax.broadcasted_iota(jnp.int32, row.shape, 0)
        found = row if found is None else jnp.where(slot >= kind * (SLOTS // (halves * 2)), row, found)
    return found


def prepare_kernel(
    lines,
    axis,
    swapped,
    after_ref,
    *refs,
):
    x_refs, refs = refs[:-16], refs[-16:]
    (
    seam_ref,
    weight_ref,
    conv_ref,
    conv_bias_ref,
    proj_raw_ref,
    step_raw_ref,
    bias_raw_ref,
    proj_out_ref,
    s_ref,
    v_ref,
    token_ref,
    inner_ref,
    active_ref,
    proj_ref,
    step_ref,
    bias_ref,
    ) = refs
    parts, length, channels = seam_ref.shape
    reach = lines + 2
    states = (proj_raw_ref.shape[1] - RANK) // 2
    time = parts * length
    low = time // SLOTS
    width = weight_ref.shape[1]
    chunk = s_ref.shape[2]
    halves = width // chunk
    slot_lines = SLOTS // (2 * halves)
    if axis == "row":
        across_first = lambda across, along: (along, across)
    else:
        across_first = lambda across, along: (across, along)

    bias_ref[...] = by_slot(halves, lambda half, way: bias_raw_ref[way : way + 1, half * chunk : (half + 1) * chunk])
    for half in range(halves):
        cells = slice(half * chunk, (half + 1) * chunk)
        for way in range(2):
            kind = slice((half * 2 + way) * LANES, (half * 2 + way + 1) * LANES)
            w = proj_raw_ref[way, :, cells].astype(F32)
            ranks = w[:RANK]
            rest = jnp.zeros((LANES - 3 * RANK - 2 * states, chunk), F32)
            w = jnp.concatenate([ranks, ranks, ranks, w[RANK:], rest], axis=0)
            proj_ref[:, kind] = w.T.astype(BF16)
            w = step_raw_ref[way, :, cells]
            high = w.astype(BF16).astype(F32)
            rest = jnp.zeros((LANES - 3 * RANK, chunk), F32)
            step_ref[kind, :] = jnp.concatenate([high, high, w - high, rest], axis=0).astype(BF16)

    row = rows_of(time)
    source = ((row & 7) << bits(low)) + (row >> 3)
    if swapped:
        source = source ^ (lax.axis_index(axis) << bits(length))
    order = one_hot([source], time)
    for line in range(reach):
        if swapped:
            x = jnp.concatenate([x_ref[line] for x_ref in x_refs], axis=0)
        else:
            x = x_refs[0][:, line].reshape(time, channels)
        if line == 0 or line == reach - 1:
            place = lax.axis_index(axis) ^ flip(axis)
            missing = place == (0 if line == 0 else lax.axis_size(axis) - 1)
            x = jnp.where(missing, seam_ref[...].reshape(time, channels), x)
        token_ref[line * time : (line + 1) * time] = dot(order, x).astype(BF16)
    inner = dot(token_ref[...], weight_ref[...]).astype(BF16).astype(F32)
    inner_ref[:, 1 : low + 1] = inner.reshape(reach, low, SLOTS, width)
    place = lax.broadcasted_iota(jnp.int32, (SLOTS, width), 0)
    for line in range(reach):
        inner_ref[line, 0] = jnp.where(place == 0, 0.0, pltpu.roll(inner_ref[line, low], 1, 0))
        inner_ref[line, low + 1] = jnp.where(place == SLOTS - 1, 0.0, pltpu.roll(inner_ref[line, 1], SLOTS - 1, 0))

    def convolve(pair, _):
        for group in range(width // (2 * LANES)):
            cells = slice(group * 2 * LANES, (group + 1) * 2 * LANES)
            half = (group * 2 * LANES) // chunk
            base = group * 2 * LANES - half * chunk
            bias = jnp.broadcast_to(conv_bias_ref[:, cells], (SLOTS, 2 * LANES))
            totals = [[bias for _ in range(2)] for _ in range(lines)]
            for across in range(3):
                for along in range(3):
                    first, second = across_first(across, along)
                    tap = jnp.broadcast_to(conv_ref[first, second : second + 1, cells], (SLOTS, 2 * LANES))
                    for line in range(lines):
                        for sub in range(2):
                            totals[line][sub] += inner_ref[line + across, 2 * pair + sub + along, :, cells] * tap
            for line in range(lines):
                value = jnp.concatenate(totals[line], axis=0)
                value = 0.5 * value
                value = value * jnp.tanh(value) + value
                value = value.astype(BF16)
                for piece in range(2):
                    at = base + piece * LANES
                    start = ((half + at // chunk) * lines + line) * time
                    start = pl.multiple_of(start + pair * (2 * SLOTS), 2 * SLOTS)
                    active_ref[pl.ds(start, 2 * SLOTS), at % chunk : at % chunk + LANES] = value[
                        :, piece * LANES : (piece + 1) * LANES
                    ]
        return 0

    lax.fori_loop(0, low // 2, convolve, 0)

    piece = 256
    for first in range(0, time * SLOTS, piece):
        row = rows_of(piece, first)
        now = row >> 3
        slot = row & 7
        line = slot & (slot_lines - 1)
        back = (slot >> bits(slot_lines)) & 1
        half = slot >> bits(2 * slot_lines)
        when = jnp.where(back == 1, time - 1 - now, now)
        source = half * (lines * time) + line * time + ((when & (low - 1)) << 3) + (when >> bits(low))
        if slot_lines > lines:
            source = jnp.where(line < lines, source, -1)
        u = dot(one_hot([source], halves * lines * time), active_ref[...])
        steps = pl.ds(first // SLOTS, piece // SLOTS)
        v_ref[steps] = u.reshape(piece // SLOTS, SLOTS, chunk)
        kind = slot >> bits(slot_lines)
        projected = dot(u.astype(BF16), proj_ref[...])
        p = projected[:, :LANES]
        for other in range(1, 2 * halves):
            p = jnp.where(kind == other, projected[:, other * LANES : (other + 1) * LANES], p)
        if halves == 2:
            p = p.reshape(piece // SLOTS, SLOTS, LANES)
            p = p + pltpu.roll(p, SLOTS // 2, 1)
            p = p.reshape(piece, LANES)
        proj_out_ref[steps] = p.reshape(piece // SLOTS, SLOTS, LANES)
        high = p.astype(BF16).astype(F32)
        lane = lax.broadcasted_iota(jnp.int32, p.shape, 1)
        mixed = jnp.where(jnp.logical_and(lane >= RANK, lane < 2 * RANK), p - high, high)
        stacked = jnp.concatenate([jnp.where(kind == k, mixed, 0.0).astype(BF16) for k in range(2 * halves)], axis=1)
        s_ref[steps] = dot(stacked, step_ref[...]).reshape(piece // SLOTS, SLOTS, chunk)

    def soften(lap, _):
        for sub in range(8):
            t = lap * 8 + sub
            for g in range(chunk // LANES):
                cells = slice(g * LANES, (g + 1) * LANES)
                before = s_ref[t, :, cells] + bias_ref[:, cells]
                small = jnp.exp(-jnp.abs(before))
                log1p = jnp.where(small < 0.001, small - 0.5 * small * small, jnp.log(1.0 + small))
                step = jnp.maximum(before, 0.0) + log1p
                s_ref[t, :, cells] = step
        return 0

    lax.fori_loop(0, time // 8, soften, 0)


def scan_kernel(after_ref, coef_ref, s_ref, u_ref, decay_ref, skip_raw_ref, out_ref, v_ref, y_ref):
    time, _, chunk = s_ref.shape
    halves = decay_ref.shape[2] // chunk
    states = decay_ref.shape[1]
    groups = chunk // LANES
    at_once = max(1, 12 // groups)
    unroll = 8
    laps = time // unroll
    for first in range(0, states, at_once):
        rates = []
        for n in range(first, first + at_once):
            rates.append([])
            for g in range(groups):
                rate = by_slot(
                    halves,
                    lambda half, way: decay_ref[way, n : n + 1, half * chunk + g * LANES : half * chunk + (g + 1) * LANES],
                )
                rates[-1].append(-LOG2E * jnp.exp(rate))
        if first == 0:
            skips = [
                by_slot(
                    halves,
                    lambda half, way: skip_raw_ref[
                        way : way + 1, half * chunk + g * LANES : half * chunk + (g + 1) * LANES
                    ],
                )
                for g in range(groups)
            ]

        def advance(lap, hidden):
            hidden = list(hidden)
            for sub in range(unroll):
                t = lap * unroll + sub
                coefs = coef_ref[t]

                def spread(lane):
                    return jnp.broadcast_to(coefs[:, lane : lane + 1], (SLOTS, LANES))

                enter = [spread(3 * RANK + first + n) for n in range(at_once)]
                leave = [spread(3 * RANK + states + first + n) for n in range(at_once)]
                for g in range(groups):
                    cells = pl.ds(g * LANES, LANES)
                    step = s_ref[t, :, cells]
                    if first == 0:
                        u = u_ref[t, :, cells]
                        value = step * u
                        v_ref[t, :, cells] = value
                        y = skips[g] * u
                    else:
                        value = v_ref[t, :, cells]
                        y = y_ref[t, :, cells]
                    for n in range(at_once):
                        k = n * groups + g
                        h = jnp.exp2(step * rates[n][g]) * hidden[k] + value * enter[n]
                        hidden[k] = h
                        y = y + h * leave[n]
                    y_ref[t, :, cells] = y
            return tuple(hidden)

        zero = jnp.zeros((SLOTS, LANES), F32)
        lax.fori_loop(0, laps, advance, (zero,) * (at_once * groups))

    out_ref[...] = y_ref[...].reshape(time * SLOTS, chunk).astype(BF16)


def join_kernel(parts, lines, axis, after_ref, scanned_ref, *out_refs):
    length = sum(out_ref.shape[0] for out_ref in out_refs) // (parts * lines)
    time = parts * length
    chunk = scanned_ref.shape[1]
    halves = out_refs[0].shape[1] // chunk
    slot_lines = SLOTS // (2 * halves)
    row = rows_of(lines * time)
    line = (row >> bits(length)) & (lines - 1)
    part = row >> bits(lines * length)
    if len(out_refs) > 1:
        part = part ^ lax.axis_index(axis)
    now = (part << bits(length)) + (row & (length - 1))
    for half in range(halves):
        ahead = now * SLOTS + (half * 2 * slot_lines) + line
        behind = (time - 1 - now) * SLOTS + (half * 2 * slot_lines + slot_lines) + line
        joined = dot(one_hot([ahead, behind], time * SLOTS), scanned_ref[...]).astype(BF16)
        at = 0
        for out_ref in out_refs:
            out_ref[:, half * chunk : (half + 1) * chunk] = joined[at : at + out_ref.shape[0]]
            at += out_ref.shape[0]


def join(axis, scanned, parts, lines, length, width, after, apart):
    count = parts if apart else 1
    return pl.pallas_call(
        functools.partial(join_kernel, parts, lines, axis),
        out_shape=[jax.ShapeDtypeStruct((parts * lines * length // count, width), BF16)] * count,
        in_specs=[pl.BlockSpec(memory_space=pl.ANY), pl.BlockSpec(memory_space=pltpu.VMEM)],
        out_specs=[pl.BlockSpec(memory_space=pltpu.VMEM)] * count,
        compiler_params=pltpu.CompilerParams(vmem_limit_bytes=24 * 1024 * 1024),
    )(after, scanned)


RANK = 24


def prepare(axis, after, xs, seam, in_weight, conv, conv_bias, proj, step_weight, step_bias, decay_log, skip):
    swapped = len(xs) > 1
    parts, length, channels = seam.shape
    reach = xs[0].shape[-3]
    lines = reach - 2
    time = parts * length
    width = conv.shape[2]
    states = decay_log.shape[2]
    assert step_weight.shape[1] == RANK
    halves = 1 if lines >= 4 else 2
    assert lines <= SLOTS // (2 * halves)
    chunk = width // halves
    way = 0 if axis == "col" else 1

    def all_of(*shape):
        return pl.BlockSpec(shape, lambda i: (0,) * len(shape))

    def pair(*shape):
        return pl.BlockSpec((2,) + shape, lambda i: (way,) + (0,) * len(shape))

    vmem = pl.BlockSpec(memory_space=pltpu.VMEM)
    flops = 2 * time * (reach * channels * width + SLOTS * width * 256)
    return pl.pallas_call(
        functools.partial(prepare_kernel, lines, axis, swapped),
        out_shape=[
            jax.ShapeDtypeStruct((time, SLOTS, LANES), F32),
            jax.ShapeDtypeStruct((time, SLOTS, chunk), F32),
            jax.ShapeDtypeStruct((time, SLOTS, chunk), F32),
        ],
        grid=(1,),
        in_specs=[pl.BlockSpec(memory_space=pl.ANY)]
        + [all_of(*x.shape) for x in xs]
        + [
            all_of(parts, length, channels),
            all_of(channels, width),
            all_of(3, 3, width),
            all_of(1, width),
            pair(RANK + 2 * states, width),
            pair(RANK, width),
            pl.BlockSpec((None, 2, width), lambda i: (way, 0, 0)),
        ],
        out_specs=[vmem, vmem, vmem],
        scratch_shapes=[
            pltpu.VMEM((reach * time, channels), BF16),
            pltpu.VMEM((reach, time // SLOTS + 2, SLOTS, width), F32),
            pltpu.VMEM((halves * lines * time, chunk), BF16),
            pltpu.VMEM((chunk, halves * 2 * LANES), BF16),
            pltpu.VMEM((halves * 2 * LANES, chunk), BF16),
            pltpu.VMEM((SLOTS, chunk), F32),
        ],
        compiler_params=pltpu.CompilerParams(vmem_limit_bytes=24 * 1024 * 1024),
        cost_estimate=pl.CostEstimate(flops=4 * flops, bytes_accessed=4 * 1024 * 1024, transcendentals=time * SLOTS * chunk),
    )(
        after,
        *xs,
        seam,
        in_weight,
        conv,
        conv_bias.reshape(1, width),
        jnp.swapaxes(proj, 1, 2),
        step_weight,
        step_bias.reshape(2, 2, width),
    )


def scan(axis, after, coefs, steps, u, decay_log, skip):
    time, _, chunk = steps.shape
    width, states = decay_log.shape[1:]
    way = 0 if axis == "col" else 1
    vmem = pl.BlockSpec(memory_space=pltpu.VMEM)
    return pl.pallas_call(
        scan_kernel,
        out_shape=jax.ShapeDtypeStruct((time * SLOTS, chunk), BF16),
        grid=(1,),
        in_specs=[
            pl.BlockSpec(memory_space=pl.ANY),
            vmem,
            vmem,
            vmem,
            pl.BlockSpec((2, states, width), lambda i: (way, 0, 0)),
            pl.BlockSpec((None, 2, width), lambda i: (way, 0, 0)),
        ],
        out_specs=vmem,
        scratch_shapes=[pltpu.VMEM((time, SLOTS, chunk), F32), pltpu.VMEM((time, SLOTS, chunk), F32)],
        compiler_params=pltpu.CompilerParams(vmem_limit_bytes=24 * 1024 * 1024),
        cost_estimate=pl.CostEstimate(
            flops=8 * time * SLOTS * chunk * states,
            bytes_accessed=4 * 1024 * 1024,
            transcendentals=time * SLOTS * chunk * states,
        ),
    )(after, coefs, steps, u, jnp.swapaxes(decay_log, 1, 2), skip.reshape(2, 2, width))


def end_kernel(cols_ref, gate_ref, gain_ref, weight_ref, *refs):
    row_refs, out_ref, gated_ref = refs[:-2], refs[-2], refs[-1]
    height, width, channels = out_ref.shape
    size = row_refs[0].shape[0]
    lines = size // width
    swap = flip("col") ^ lax.axis_index("col")
    turn = flip("row") * (width // lax.axis_size("row"))
    row = rows_of(height * width)
    line = (row >> bits(width)) ^ (swap * lines)
    source = (((row & (width - 1)) ^ turn) << bits(height)) + line
    rows = jnp.concatenate([row_ref[...] for row_ref in row_refs], axis=0)
    combined = layer_norm(rows.astype(F32) + dot(one_hot([source], height * width), cols_ref[...]), gain_ref[...][None])
    for part in range(len(row_refs)):
        cells = pl.ds(pl.multiple_of((part ^ swap) * size, size), size)
        gate = gate_ref[cells].astype(F32)
        gated_ref[cells] = (combined[part * size : (part + 1) * size] * (gate / (1.0 + jnp.exp(-gate)))).astype(BF16)
    out = dot(gated_ref[...], weight_ref[...]).astype(BF16)
    out_ref[...] = out.reshape(height, width, channels)


def swap_blocks(blocks, axis):
    count = lax.axis_size(axis)
    blocks = list(blocks)
    return blocks[:1] + [lax.ppermute(blocks[k], axis, [(i, i ^ k) for i in range(count)]) for k in range(1, count)]


def pick_kernel(axis, after_ref, x_ref, out_ref):
    place = lax.axis_index(axis) ^ flip(axis)
    out_ref[...] = x_ref[:, jnp.where(place == 0, 1, x_ref.shape[1] - 2)]


def pick(axis, after, x):
    return pl.pallas_call(
        functools.partial(pick_kernel, axis),
        out_shape=jax.ShapeDtypeStruct((x.shape[0],) + x.shape[2:], x.dtype),
        in_specs=[pl.BlockSpec(memory_space=pl.ANY), pl.BlockSpec(memory_space=pltpu.VMEM)],
        out_specs=pl.BlockSpec(memory_space=pltpu.VMEM),
    )(after, x)


def seam_of(axis, line):
    count = lax.axis_size(axis)
    height, breadth = lax.axis_size("row"), lax.axis_size("col")
    if axis == "row":
        at = lambda group: (0 if group & 1 else count - 1) * breadth
        ends = [(at(c) + c, at(c) + c + 1) for c in range(breadth - 1)]
    else:
        at = lambda group: 0 if group & 1 else count - 1
        ends = [(at(r) + r * breadth, at(r) + (r + 1) * breadth) for r in range(height - 1)]
    pairs = ends + [(b, a) for a, b in ends]
    return lax.ppermute(line, ("row", "col"), pairs)


def local(
    features,
    norm_gain,
    in_weight,
    conv_weight,
    conv_bias,
    proj_weight,
    step_weight,
    step_bias,
    decay_log,
    skip_gain,
    out_gain,
    out_weight,
):
    height, width, channels = features.shape
    inner = out_weight.shape[0]
    tokens = height * width
    row_lines = height // lax.axis_size("col")
    col_lines = width // lax.axis_size("row")

    rows, cols = lax.axis_size("row"), lax.axis_size("col")
    normed, col_send, *row_send = pl.pallas_call(
        cut_kernel,
        out_shape=[
            jax.ShapeDtypeStruct((tokens, channels), BF16),
            jax.ShapeDtypeStruct((rows, col_lines + 2, height, channels), BF16),
        ]
        + [jax.ShapeDtypeStruct((row_lines + 2, width, channels), BF16)] * cols,
    )(features, norm_gain)
    weights = (in_weight, conv_weight, conv_bias, proj_weight, step_weight, step_bias, decay_log, skip_gain)
    gate = pl.pallas_call(
        gate_kernel,
        out_shape=jax.ShapeDtypeStruct((tokens, inner), BF16),
        grid=(1,),
        in_specs=[
            pl.BlockSpec((tokens, channels), lambda i: (0, 0)),
            pl.BlockSpec((channels, inner), lambda i: (0, 1)),
        ],
        out_specs=pl.BlockSpec((tokens, inner), lambda i: (0, 0)),
        cost_estimate=pl.CostEstimate(flops=2 * tokens * channels * inner, bytes_accessed=1 << 20, transcendentals=0),
    )(normed, in_weight)

    row_x = swap_blocks(row_send, "col")
    col_x = lax.all_to_all(col_send, "row", 0, 0, tiled=True)
    start = lax.axis_index("col") == flip("col")
    row_seam = seam_of("col", jnp.stack([jnp.where(start, x[1], x[-2]) for x in row_x]))
    row_steps = prepare("col", normed, row_x, row_seam, *weights)
    col_seam = seam_of("row", pick("row", row_steps[0], col_x))
    col_steps = prepare("row", row_steps[0], [col_x], col_seam, *weights)
    col_y = scan("row", normed, *col_steps, decay_log, skip_gain)
    (joined,) = join("row", col_y, rows, col_lines, height, inner, normed, False)
    col_y = lax.all_to_all(joined.reshape(rows, -1, inner), "row", 0, 0, tiled=True)
    row_y = scan("col", joined, *row_steps, decay_log, skip_gain)
    row_y = swap_blocks(join("col", row_y, cols, row_lines, width, inner, col_y, True), "col")
    return pl.pallas_call(
        end_kernel,
        out_shape=jax.ShapeDtypeStruct(features.shape, BF16),
        scratch_shapes=[pltpu.VMEM((tokens, inner), BF16)],
    )(col_y.reshape(tokens, inner), gate, out_gain, out_weight, *row_y)


def solution(mesh):
    in_specs = (P("row", "col", None), P(), P(), P(), P(), P(), P(), P(), P(), P(), P(), P())
    out_specs = P("row", "col", None)
    return jax.shard_map(local, mesh=mesh, in_specs=in_specs, out_specs=out_specs, check_vma=False)
```

```python
import functools

import jax
import jax.numpy as jnp
from jax import lax
from jax.experimental import pallas as pl
from jax.experimental.pallas import tpu as pltpu
from jax.sharding import PartitionSpec as P

F32 = jnp.float32
BF16 = jnp.bfloat16
LANES = 128
SLOTS = 8
LOG2E = 1.4426950408889634


def bits(value):
    assert value & (value - 1) == 0
    return value.bit_length() - 1


def one_hot(targets, width):
    lane = lax.broadcasted_iota(jnp.int32, targets[0].shape, 1)
    blocks = []
    for block in range(pl.cdiv(width, LANES)):
        hit = targets[0] == lane + block * LANES
        for other in targets[1:]:
            hit = jnp.logical_or(hit, other == lane + block * LANES)
        blocks.append(jnp.where(hit, 1.0, 0.0).astype(BF16))
    return jnp.concatenate(blocks, axis=1)[:, :width]


def rows_of(count, start=0):
    return lax.broadcasted_iota(jnp.int32, (count, LANES), 0) + start


def dot(a, b):
    return jnp.dot(a, b, preferred_element_type=F32)


def layer_norm(values, scale_gain):
    centred = values - jnp.mean(values, axis=-1, keepdims=True)
    spread = jnp.mean(centred * centred, axis=-1, keepdims=True)
    return centred * lax.rsqrt(spread + 1e-05) * scale_gain


def flip(axis):
    other = "col" if axis == "row" else "row"
    return (lax.axis_index(other) & 1) * (lax.axis_size(axis) - 1)


def cut_kernel(columns, feat_ref, gain_ref, norm_ref, *refs):
    col_refs, row_refs, turned_ref = refs[:columns], refs[columns:-1], refs[-1]
    height, width, channels = feat_ref.shape
    tile = layer_norm(feat_ref[...].reshape(height * width, channels).astype(F32), gain_ref[...][None]).astype(BF16)
    norm_ref[...] = tile
    reach = row_refs[0].shape[0]
    turn = flip("col") ^ lax.axis_index("col")
    for part, row_ref in enumerate(row_refs):
        for line in range(reach):
            at = jnp.clip((part ^ turn) * (reach - 2) + line - 1, 0, height - 1)
            row_ref[line] = norm_ref[pl.ds(pl.multiple_of(at * width, width), width)]
    row = rows_of(height * width)
    turned = dot(one_hot([((row & (height - 1)) << bits(width)) + (row >> bits(height))], height * width), tile).astype(
        BF16
    )
    turned_ref[...] = turned
    reach = col_refs[0].shape[0]
    turn = flip("row") ^ lax.axis_index("row")
    for part, col_ref in enumerate(col_refs):
        for line in range(reach):
            at = jnp.clip((part ^ turn) * (reach - 2) + line - 1, 0, width - 1)
            col_ref[line] = turned_ref[pl.ds(pl.multiple_of(at * height, height), height)]


def gate_kernel(norm_ref, weight_ref, gate_ref):
    gate_ref[...] = dot(norm_ref[...], weight_ref[...]).astype(BF16)


def by_slot(halves, rows):
    found = None
    for kind in range(halves * 2):
        row = rows(kind >> 1, kind & 1)
        row = jnp.broadcast_to(row, (SLOTS, row.shape[1]))
        slot = lax.broadcasted_iota(jnp.int32, row.shape, 0)
        found = row if found is None else jnp.where(slot >= kind * (SLOTS // (halves * 2)), row, found)
    return found


def prepare_kernel(
    lines,
    axis,
    after_ref,
    *refs,
):
    x_refs, refs = refs[:-23], refs[-23:]
    (
        seam_ref,
        weight_hbm,
        conv_hbm,
        conv_bias_hbm,
        proj_hbm,
        step_hbm,
        bias_hbm,
        proj_out_ref,
        s_ref,
        v_ref,
        weight_ref,
        conv_ref,
        conv_bias_ref,
        proj_raw_ref,
        step_raw_ref,
        bias_raw_ref,
        token_ref,
        inner_ref,
        active_ref,
        proj_ref,
        step_ref,
        bias_ref,
        copied,
    ) = refs
    pair = pl.ds(0 if axis == "col" else 2, 2)
    copies = [
        pltpu.make_async_copy(source, to, copied.at[k])
        for k, (source, to) in enumerate(
            [
                (weight_hbm.at[:, pl.ds(0, weight_ref.shape[1])], weight_ref),
                (conv_hbm, conv_ref),
                (conv_bias_hbm, conv_bias_ref),
                (proj_hbm.at[pair], proj_raw_ref),
                (step_hbm.at[pair], step_raw_ref),
                (bias_hbm, bias_raw_ref),
            ]
        )
    ]
    for copy in copies:
        copy.start()
    parts, length, channels = seam_ref.shape
    reach = lines + 2
    states = (proj_raw_ref.shape[1] - RANK) // 2
    time = parts * length
    low = time // SLOTS
    width = weight_ref.shape[1]
    chunk = s_ref.shape[2]
    halves = width // chunk
    slot_lines = SLOTS // (2 * halves)
    if axis == "row":
        across_first = lambda across, along: (along, across)
    else:
        across_first = lambda across, along: (across, along)

    row = rows_of(time)
    source = ((row & 7) << bits(low)) + (row >> 3)
    source = source ^ (lax.axis_index(axis) << bits(length))
    order = one_hot([source], time)
    for line in range(reach):
        x = jnp.concatenate([x_ref[line] for x_ref in x_refs], axis=0)
        if line == 0 or line == reach - 1:
            place = lax.axis_index(axis) ^ flip(axis)
            missing = place == (0 if line == 0 else lax.axis_size(axis) - 1)
            x = jnp.where(missing, seam_ref[...].reshape(time, channels), x)
        token_ref[line * time : (line + 1) * time] = dot(order, x).astype(BF16)
    for copy in copies:
        copy.wait()
    inner = dot(token_ref[...], weight_ref[...]).astype(BF16).astype(F32)
    inner_ref[:, 1 : low + 1] = inner.reshape(reach, low, SLOTS, width)
    place = lax.broadcasted_iota(jnp.int32, (SLOTS, width), 0)
    for line in range(reach):
        inner_ref[line, 0] = jnp.where(place == 0, 0.0, pltpu.roll(inner_ref[line, low], 1, 0))
        inner_ref[line, low + 1] = jnp.where(place == SLOTS - 1, 0.0, pltpu.roll(inner_ref[line, 1], SLOTS - 1, 0))

    conv_bias = conv_bias_ref[...][None]

    def convolve(pair, _):
        for group in range(width // (2 * LANES)):
            cells = slice(group * 2 * LANES, (group + 1) * 2 * LANES)
            half = (group * 2 * LANES) // chunk
            base = group * 2 * LANES - half * chunk
            bias = jnp.broadcast_to(conv_bias[:, cells], (SLOTS, 2 * LANES))
            totals = [[bias for _ in range(2)] for _ in range(lines)]
            for across in range(3):
                for along in range(3):
                    first, second = across_first(across, along)
                    tap = jnp.broadcast_to(conv_ref[first, second : second + 1, cells], (SLOTS, 2 * LANES))
                    for line in range(lines):
                        for sub in range(2):
                            totals[line][sub] += inner_ref[line + across, 2 * pair + sub + along, :, cells] * tap
            for line in range(lines):
                value = jnp.concatenate(totals[line], axis=0)
                value = 0.5 * value
                value = value * jnp.tanh(value) + value
                value = value.astype(BF16)
                for piece in range(2):
                    at = base + piece * LANES
                    start = ((half + at // chunk) * lines + line) * time
                    start = pl.multiple_of(start + pair * (2 * SLOTS), 2 * SLOTS)
                    active_ref[pl.ds(start, 2 * SLOTS), at % chunk : at % chunk + LANES] = value[
                        :, piece * LANES : (piece + 1) * LANES
                    ]
        return 0

    lax.fori_loop(0, low // 2, convolve, 0)

    bias_ref[...] = by_slot(halves, lambda half, way: bias_raw_ref[pair.start + way : pair.start + way + 1, half * chunk : (half + 1) * chunk])
    for half in range(halves):
        cells = slice(half * chunk, (half + 1) * chunk)
        for way in range(2):
            kind = slice((half * 2 + way) * LANES, (half * 2 + way + 1) * LANES)
            w = proj_raw_ref[way, :, cells].astype(F32)
            ranks = w[:RANK]
            rest = jnp.zeros((LANES - 3 * RANK - 2 * states, chunk), F32)
            w = jnp.concatenate([ranks, ranks, ranks, w[RANK:], rest], axis=0)
            proj_ref[:, kind] = w.T.astype(BF16)
            w = step_raw_ref[way, :, cells]
            high = w.astype(BF16).astype(F32)
            rest = jnp.zeros((LANES - 3 * RANK, chunk), F32)
            step_ref[kind, :] = jnp.concatenate([high, high, w - high, rest], axis=0).astype(BF16)

    piece = 256
    for first in range(0, time * SLOTS, piece):
        row = rows_of(piece, first)
        now = row >> 3
        slot = row & 7
        line = slot & (slot_lines - 1)
        back = (slot >> bits(slot_lines)) & 1
        half = slot >> bits(2 * slot_lines)
        when = jnp.where(back == 1, time - 1 - now, now)
        source = half * (lines * time) + line * time + ((when & (low - 1)) << 3) + (when >> bits(low))
        if slot_lines > lines:
            source = jnp.where(line < lines, source, -1)
        u = dot(one_hot([source], halves * lines * time), active_ref[...])
        steps = pl.ds(first // SLOTS, piece // SLOTS)
        v_ref[steps] = u.reshape(piece // SLOTS, SLOTS, chunk)
        kind = slot >> bits(slot_lines)
        projected = dot(u.astype(BF16), proj_ref[...])
        p = projected[:, :LANES]
        for other in range(1, 2 * halves):
            p = jnp.where(kind == other, projected[:, other * LANES : (other + 1) * LANES], p)
        if halves == 2:
            p = p.reshape(piece // SLOTS, SLOTS, LANES)
            p = p + pltpu.roll(p, SLOTS // 2, 1)
            p = p.reshape(piece, LANES)
        proj_out_ref[steps] = p.reshape(piece // SLOTS, SLOTS, LANES)
        high = p.astype(BF16).astype(F32)
        lane = lax.broadcasted_iota(jnp.int32, p.shape, 1)
        mixed = jnp.where(jnp.logical_and(lane >= RANK, lane < 2 * RANK), p - high, high)
        stacked = jnp.concatenate([jnp.where(kind == k, mixed, 0.0).astype(BF16) for k in range(2 * halves)], axis=1)
        s_ref[steps] = dot(stacked, step_ref[...]).reshape(piece // SLOTS, SLOTS, chunk)

    def soften(lap, _):
        for sub in range(8):
            t = lap * 8 + sub
            for g in range(chunk // LANES):
                cells = slice(g * LANES, (g + 1) * LANES)
                before = s_ref[t, :, cells] + bias_ref[:, cells]
                small = jnp.exp(-jnp.abs(before))
                log1p = jnp.where(small < 0.001, small - 0.5 * small * small, jnp.log(1.0 + small))
                step = jnp.maximum(before, 0.0) + log1p
                s_ref[t, :, cells] = step
        return 0

    lax.fori_loop(0, time // 8, soften, 0)


def scan_kernel(
    axis,
    after_ref,
    coef_ref,
    s_ref,
    u_ref,
    decay_hbm,
    skip_hbm,
    out_ref,
    v_ref,
    y_ref,
    spread_ref,
    decay_ref,
    skip_raw_ref,
    copied,
):
    time, _, chunk = s_ref.shape
    halves = decay_ref.shape[2] // chunk
    states = decay_ref.shape[1]
    groups = chunk // LANES
    at_once = max(1, 12 // groups)
    unroll = 8
    laps = time // unroll

    pair = pl.ds(0 if axis == "col" else 2, 2)
    copies = [
        pltpu.make_async_copy(decay_hbm.at[pair], decay_ref, copied.at[0]),
        pltpu.make_async_copy(skip_hbm, skip_raw_ref, copied.at[1]),
    ]
    for copy in copies:
        copy.start()

    piece = 32
    row = lax.broadcasted_iota(jnp.int32, (2 * LANES, LANES), 0) & (LANES - 1)
    taken = [jnp.where(row == 3 * RANK + n, 1.0, 0.0).astype(BF16) for n in range(2 * states)]

    def spread(lap, _):
        steps = pl.ds(lap * piece, piece)
        coefs = coef_ref[steps].reshape(piece * SLOTS, LANES)
        high = coefs.astype(BF16)
        both = jnp.concatenate([high, (coefs - high.astype(F32)).astype(BF16)], axis=1)
        for n in range(0, 2 * states, 4):
            found = dot(both, jnp.concatenate(taken[n : n + 4], axis=1))
            for k in range(4):
                spread_ref[steps, n + k] = found[:, k * LANES : (k + 1) * LANES].reshape(piece, SLOTS, LANES)
        return 0

    lax.fori_loop(0, time // piece, spread, 0)
    for copy in copies:
        copy.wait()
    for first in range(0, states, at_once):
        rates = []
        for n in range(first, first + at_once):
            rates.append([])
            for g in range(groups):
                rate = by_slot(
                    halves,
                    lambda half, way: decay_ref[way, n : n + 1, half * chunk + g * LANES : half * chunk + (g + 1) * LANES],
                )
                rates[-1].append(-LOG2E * jnp.exp(rate))
        if first == 0:
            skips = [
                by_slot(
                    halves,
                    lambda half, way: skip_raw_ref[
                        pair.start + way : pair.start + way + 1, half * chunk + g * LANES : half * chunk + (g + 1) * LANES
                    ],
                )
                for g in range(groups)
            ]

        def advance(lap, hidden):
            hidden = list(hidden)
            for sub in range(unroll):
                t = lap * unroll + sub
                enter = [spread_ref[t, first + n] for n in range(at_once)]
                leave = [spread_ref[t, states + first + n] for n in range(at_once)]
                for g in range(groups):
                    cells = pl.ds(g * LANES, LANES)
                    step = s_ref[t, :, cells]
                    if first == 0:
                        u = u_ref[t, :, cells]
                        value = step * u
                        v_ref[t, :, cells] = value
                        y = skips[g] * u
                    else:
                        value = v_ref[t, :, cells]
                        y = y_ref[t, :, cells]
                    for n in range(at_once):
                        k = n * groups + g
                        h = jnp.exp2(step * rates[n][g]) * hidden[k] + value * enter[n]
                        hidden[k] = h
                        y = y + h * leave[n]
                    y_ref[t, :, cells] = y
            return tuple(hidden)

        zero = jnp.zeros((SLOTS, LANES), F32)
        lax.fori_loop(0, laps, advance, (zero,) * (at_once * groups))

    out_ref[...] = y_ref[...].reshape(time * SLOTS, chunk).astype(BF16)


def join_kernel(parts, lines, axis, after_ref, scanned_ref, *out_refs):
    length = sum(out_ref.shape[0] for out_ref in out_refs) // (parts * lines)
    time = parts * length
    chunk = scanned_ref.shape[1]
    halves = out_refs[0].shape[1] // chunk
    slot_lines = SLOTS // (2 * halves)
    row = rows_of(lines * time)
    line = (row >> bits(length)) & (lines - 1)
    part = row >> bits(lines * length)
    part = part ^ lax.axis_index(axis)
    now = (part << bits(length)) + (row & (length - 1))
    for half in range(halves):
        ahead = now * SLOTS + (half * 2 * slot_lines) + line
        behind = (time - 1 - now) * SLOTS + (half * 2 * slot_lines + slot_lines) + line
        joined = dot(one_hot([ahead, behind], time * SLOTS), scanned_ref[...]).astype(BF16)
        at = 0
        for out_ref in out_refs:
            out_ref[:, half * chunk : (half + 1) * chunk] = joined[at : at + out_ref.shape[0]]
            at += out_ref.shape[0]


def join(axis, scanned, parts, lines, length, width, after):
    return pl.pallas_call(
        functools.partial(join_kernel, parts, lines, axis),
        out_shape=[jax.ShapeDtypeStruct((lines * length, width), BF16)] * parts,
        in_specs=[pl.BlockSpec(memory_space=pl.ANY), pl.BlockSpec(memory_space=pltpu.VMEM)],
        out_specs=[pl.BlockSpec(memory_space=pltpu.VMEM)] * parts,
        compiler_params=pltpu.CompilerParams(vmem_limit_bytes=24 * 1024 * 1024),
    )(after, scanned)


RANK = 24


def prepare(axis, after, xs, seam, in_weight, conv, conv_bias, proj, step_weight, step_bias, decay_log, skip):
    parts, length, channels = seam.shape
    reach = xs[0].shape[-3]
    lines = reach - 2
    time = parts * length
    width = conv.shape[2]
    states = decay_log.shape[2]
    assert step_weight.shape[1] == RANK
    halves = 1 if lines >= 4 else 2
    assert lines <= SLOTS // (2 * halves)
    chunk = width // halves
    vmem = pl.BlockSpec(memory_space=pltpu.VMEM)
    hbm = pl.BlockSpec(memory_space=pltpu.HBM)
    flops = 2 * time * (reach * channels * width + SLOTS * width * 256)
    return pl.pallas_call(
        functools.partial(prepare_kernel, lines, axis),
        out_shape=[
            jax.ShapeDtypeStruct((time, SLOTS, LANES), F32),
            jax.ShapeDtypeStruct((time, SLOTS, chunk), F32),
            jax.ShapeDtypeStruct((time, SLOTS, chunk), F32),
        ],
        in_specs=[pl.BlockSpec(memory_space=pl.ANY)] + [vmem] * (len(xs) + 1) + [hbm] * 6,
        out_specs=[vmem, vmem, vmem],
        scratch_shapes=[
            pltpu.VMEM((channels, width), in_weight.dtype),
            pltpu.VMEM(conv.shape, conv.dtype),
            pltpu.VMEM(conv_bias.shape, conv_bias.dtype),
            pltpu.VMEM((2, RANK + 2 * states, width), proj.dtype),
            pltpu.VMEM((2, RANK, width), step_weight.dtype),
            pltpu.VMEM(step_bias.shape, step_bias.dtype),
            pltpu.VMEM((reach * time, channels), BF16),
            pltpu.VMEM((reach, time // SLOTS + 2, SLOTS, width), F32),
            pltpu.VMEM((halves * lines * time, chunk), BF16),
            pltpu.VMEM((chunk, halves * 2 * LANES), BF16),
            pltpu.VMEM((halves * 2 * LANES, chunk), BF16),
            pltpu.VMEM((SLOTS, chunk), F32),
            pltpu.SemaphoreType.DMA((6,)),
        ],
        compiler_params=pltpu.CompilerParams(vmem_limit_bytes=24 * 1024 * 1024),
        cost_estimate=pl.CostEstimate(flops=4 * flops, bytes_accessed=4 * 1024 * 1024, transcendentals=time * SLOTS * chunk),
    )(
        after,
        *xs,
        seam,
        in_weight,
        conv,
        conv_bias,
        jnp.swapaxes(proj, 1, 2),
        step_weight,
        step_bias,
    )


def scan(axis, after, coefs, steps, u, decay_log, skip):
    time, _, chunk = steps.shape
    width, states = decay_log.shape[1:]
    vmem = pl.BlockSpec(memory_space=pltpu.VMEM)
    hbm = pl.BlockSpec(memory_space=pltpu.HBM)
    return pl.pallas_call(
        functools.partial(scan_kernel, axis),
        out_shape=jax.ShapeDtypeStruct((time * SLOTS, chunk), BF16),
        in_specs=[pl.BlockSpec(memory_space=pl.ANY), vmem, vmem, vmem, hbm, hbm],
        out_specs=vmem,
        scratch_shapes=[
            pltpu.VMEM((time, SLOTS, chunk), F32),
            pltpu.VMEM((time, SLOTS, chunk), F32),
            pltpu.VMEM((time, 2 * states, SLOTS, LANES), F32),
            pltpu.VMEM((2, states, width), decay_log.dtype),
            pltpu.VMEM(skip.shape, skip.dtype),
            pltpu.SemaphoreType.DMA((2,)),
        ],
        compiler_params=pltpu.CompilerParams(vmem_limit_bytes=(8 << 20) + time * (136 << 10) + time * 20 * chunk),
        cost_estimate=pl.CostEstimate(
            flops=8 * time * SLOTS * chunk * states,
            bytes_accessed=4 * 1024 * 1024,
            transcendentals=time * SLOTS * chunk * states,
        ),
    )(after, coefs, steps, u, jnp.swapaxes(decay_log, 1, 2), skip)


def end_kernel(columns, gate_ref, gain_ref, weight_ref, *refs):
    col_refs, row_refs, out_ref, gated_ref = refs[:columns], refs[columns:-2], refs[-2], refs[-1]
    height, width, channels = out_ref.shape
    size = row_refs[0].shape[0]
    lines = size // width
    swap = flip("col") ^ lax.axis_index("col")
    turn = (flip("row") ^ lax.axis_index("row")) * (width // lax.axis_size("row"))
    row = rows_of(height * width)
    line = (row >> bits(width)) ^ (swap * lines)
    source = (((row & (width - 1)) ^ turn) << bits(height)) + line
    rows = jnp.concatenate([row_ref[...] for row_ref in row_refs], axis=0)
    columns = jnp.concatenate([col_ref[...] for col_ref in col_refs], axis=0)
    combined = layer_norm(rows.astype(F32) + dot(one_hot([source], height * width), columns), gain_ref[...][None])
    for part in range(len(row_refs)):
        cells = pl.ds(pl.multiple_of((part ^ swap) * size, size), size)
        gate = gate_ref[cells].astype(F32)
        gated_ref[cells] = (combined[part * size : (part + 1) * size] * (gate / (1.0 + jnp.exp(-gate)))).astype(BF16)
    out = dot(gated_ref[...], weight_ref[...]).astype(BF16)
    out_ref[...] = out.reshape(height, width, channels)


def swap_blocks(blocks, axis):
    count = lax.axis_size(axis)
    found = {k: lax.ppermute(blocks[k], axis, [(i, i ^ k) for i in range(count)]) for k in range(count - 1, 0, -1)}
    return [blocks[0]] + [found[k] for k in range(1, count)]


def pick_kernel(axis, after_ref, *refs):
    x_refs, out_ref = refs[:-1], refs[-1]
    place = lax.axis_index(axis) ^ flip(axis)
    line = jnp.where(place == 0, 1, x_refs[0].shape[0] - 2)
    for part, x_ref in enumerate(x_refs):
        out_ref[part] = x_ref[line]


def pick(axis, after, xs):
    return pl.pallas_call(
        functools.partial(pick_kernel, axis),
        out_shape=jax.ShapeDtypeStruct((len(xs),) + xs[0].shape[1:], xs[0].dtype),
        in_specs=[pl.BlockSpec(memory_space=pl.ANY)] + [pl.BlockSpec(memory_space=pltpu.VMEM)] * len(xs),
        out_specs=pl.BlockSpec(memory_space=pltpu.VMEM),
        compiler_params=pltpu.CompilerParams(vmem_limit_bytes=4 * 1024 * 1024),
    )(after, *xs)


def seam_of(axis, line):
    count = lax.axis_size(axis)
    height, breadth = lax.axis_size("row"), lax.axis_size("col")
    if axis == "row":
        at = lambda group: (0 if group & 1 else count - 1) * breadth
        ends = [(at(c) + c, at(c) + c + 1) for c in range(breadth - 1)]
    else:
        at = lambda group: 0 if group & 1 else count - 1
        ends = [(at(r) + r * breadth, at(r) + (r + 1) * breadth) for r in range(height - 1)]
    pairs = ends + [(b, a) for a, b in ends]
    return lax.ppermute(line, ("row", "col"), pairs)


def local(
    features,
    norm_gain,
    in_weight,
    conv_weight,
    conv_bias,
    proj_weight,
    step_weight,
    step_bias,
    decay_log,
    skip_gain,
    out_gain,
    out_weight,
):
    height, width, channels = features.shape
    inner = out_weight.shape[0]
    tokens = height * width
    row_lines = height // lax.axis_size("col")
    col_lines = width // lax.axis_size("row")

    rows, cols = lax.axis_size("row"), lax.axis_size("col")
    vmem = pl.BlockSpec(memory_space=pltpu.VMEM)
    normed, *sends = pl.pallas_call(
        functools.partial(cut_kernel, rows),
        out_shape=[jax.ShapeDtypeStruct((tokens, channels), BF16)]
        + [jax.ShapeDtypeStruct((col_lines + 2, height, channels), BF16)] * rows
        + [jax.ShapeDtypeStruct((row_lines + 2, width, channels), BF16)] * cols,
        in_specs=[pl.BlockSpec(features.shape, lambda: (0, 0, 0)), pl.BlockSpec((channels,), lambda: (0,))],
        out_specs=[vmem] * (1 + rows + cols),
        scratch_shapes=[pltpu.VMEM((tokens, channels), BF16)],
        compiler_params=pltpu.CompilerParams(vmem_limit_bytes=12 * 1024 * 1024),
        cost_estimate=pl.CostEstimate(flops=6_000_000_000, bytes_accessed=2 << 20, transcendentals=tokens),
    )(features, norm_gain)
    weights = (in_weight, conv_weight, conv_bias, proj_weight, step_weight, step_bias, decay_log, skip_gain)
    gate = pl.pallas_call(
        gate_kernel,
        out_shape=jax.ShapeDtypeStruct((tokens, inner), BF16),
        grid=(1,),
        in_specs=[
            pl.BlockSpec((tokens, channels), lambda i: (0, 0)),
            pl.BlockSpec((channels, inner), lambda i: (0, 1)),
        ],
        out_specs=pl.BlockSpec((tokens, inner), lambda i: (0, 0)),
        compiler_params=pltpu.CompilerParams(vmem_limit_bytes=12 * 1024 * 1024),
        cost_estimate=pl.CostEstimate(flops=2 * tokens * channels * inner, bytes_accessed=1 << 20, transcendentals=0),
    )(normed, in_weight)

    row_x = swap_blocks(sends[rows:], "col")
    col_x = swap_blocks(sends[:rows], "row")
    row_seam = seam_of("col", pick("col", normed, row_x))
    row_steps = prepare("col", normed, row_x, row_seam, *weights)
    col_seam = seam_of("row", pick("row", row_steps[0], col_x))
    col_steps = prepare("row", row_steps[0], col_x, col_seam, *weights)
    col_y = scan("row", normed, *col_steps, decay_log, skip_gain)
    joined = join("row", col_y, rows, col_lines, height, inner, normed)
    col_y = swap_blocks(joined, "row")
    row_y = scan("col", joined[0], *row_steps, decay_log, skip_gain)
    row_y = swap_blocks(join("col", row_y, cols, row_lines, width, inner, col_y[-1]), "col")
    return pl.pallas_call(
        functools.partial(end_kernel, rows),
        out_shape=jax.ShapeDtypeStruct(features.shape, BF16),
        scratch_shapes=[pltpu.VMEM((tokens, inner), BF16)],
        compiler_params=pltpu.CompilerParams(vmem_limit_bytes=16 * 1024 * 1024),
    )(gate, out_gain, out_weight, *col_y, *row_y)


def solution(mesh):
    in_specs = (P("row", "col", None), P(), P(), P(), P(), P(), P(), P(), P(), P(), P(), P())
    out_specs = P("row", "col", None)
    return jax.shard_map(local, mesh=mesh, in_specs=in_specs, out_specs=out_specs, check_vma=False)
```

```python
import functools

import jax
import jax.numpy as jnp
from jax import lax
from jax.experimental import pallas as pl
from jax.experimental.pallas import tpu as pltpu
from jax.sharding import PartitionSpec as P

F32 = jnp.float32
BF16 = jnp.bfloat16
LANES = 128
SLOTS = 8
LOG2E = 1.4426950408889634


def bits(value):
    assert value & (value - 1) == 0
    return value.bit_length() - 1


def one_hot(targets, width):
    lane = lax.broadcasted_iota(jnp.int32, targets[0].shape, 1)
    blocks = []
    for block in range(pl.cdiv(width, LANES)):
        hit = targets[0] == lane + block * LANES
        for other in targets[1:]:
            hit = jnp.logical_or(hit, other == lane + block * LANES)
        blocks.append(jnp.where(hit, 1.0, 0.0).astype(BF16))
    return jnp.concatenate(blocks, axis=1)[:, :width]


def rows_of(count, start=0):
    return lax.broadcasted_iota(jnp.int32, (count, LANES), 0) + start


def dot(a, b):
    return jnp.dot(a, b, preferred_element_type=F32)


def layer_norm(values, scale_gain):
    centred = values - jnp.mean(values, axis=-1, keepdims=True)
    spread = jnp.mean(centred * centred, axis=-1, keepdims=True)
    return centred * lax.rsqrt(spread + 1e-05) * scale_gain


def flip(axis):
    other = "col" if axis == "row" else "row"
    return (lax.axis_index(other) & 1) * (lax.axis_size(axis) - 1)


def cut_kernel(columns, feat_ref, gain_ref, norm_ref, *refs):
    col_refs, beside_ref, row_refs, turned_ref = refs[: columns // 2], refs[columns // 2], refs[columns // 2 + 1 : -1], refs[-1]
    height, width, channels = feat_ref.shape
    tile = layer_norm(feat_ref[...].reshape(height * width, channels).astype(F32), gain_ref[...][None]).astype(BF16)
    norm_ref[...] = tile
    reach = row_refs[0].shape[0]
    turn = flip("col") ^ lax.axis_index("col")
    for part, row_ref in enumerate(row_refs):
        for line in range(reach):
            at = jnp.clip((part ^ turn) * (reach - 2) + line - 1, 0, height - 1)
            row_ref[line] = norm_ref[pl.ds(pl.multiple_of(at * width, width), width)]
    row = rows_of(height * width)
    turned = dot(one_hot([((row & (height - 1)) << bits(width)) + (row >> bits(height))], height * width), tile).astype(
        BF16
    )
    turned_ref[...] = turned
    reach = col_refs[0].shape[0]
    turn = flip("row") ^ lax.axis_index("row")
    for part in range(columns):
        for line in range(reach):
            at = jnp.clip((part ^ turn) * (reach - 2) + line - 1, 0, width - 1)
            found = turned_ref[pl.ds(pl.multiple_of(at * height, height), height)]
            if part & 1:
                beside_ref[part >> 1, line] = found
            else:
                col_refs[part >> 1][line] = found


def gate_kernel(norm_ref, weight_ref, gate_ref):
    gate_ref[...] = dot(norm_ref[...], weight_ref[...]).astype(BF16)


def views(refs, rank):
    found = []
    for ref in refs:
        found += [ref] if len(ref.shape) == rank else [ref.at[k] for k in range(ref.shape[0])]
    return found


def by_slot(halves, rows):
    found = None
    for kind in range(halves * 2):
        row = rows(kind >> 1, kind & 1)
        row = jnp.broadcast_to(row, (SLOTS, row.shape[1]))
        slot = lax.broadcasted_iota(jnp.int32, row.shape, 0)
        found = row if found is None else jnp.where(slot >= kind * (SLOTS // (halves * 2)), row, found)
    return found


def prepare_kernel(
    lines,
    axis,
    after_ref,
    *refs,
):
    x_refs, refs = views(refs[:-16], 3), refs[-16:]
    (
        seam_ref,
        weight_ref,
        conv_ref,
        conv_bias_ref,
        proj_raw_ref,
        step_raw_ref,
        bias_raw_ref,
        proj_out_ref,
        s_ref,
        v_ref,
        token_ref,
        inner_ref,
        active_ref,
        proj_ref,
        step_ref,
        bias_ref,
    ) = refs
    ks = (0, 1) if axis == "col" else (2, 3)
    parts, length, channels = seam_ref.shape
    reach = lines + 2
    states = (proj_raw_ref.shape[1] - RANK) // 2
    time = parts * length
    low = time // SLOTS
    width = weight_ref.shape[1] // 2
    chunk = s_ref.shape[2]
    halves = width // chunk
    slot_lines = SLOTS // (2 * halves)
    if axis == "row":
        across_first = lambda across, along: (along, across)
    else:
        across_first = lambda across, along: (across, along)

    row = rows_of(time)
    source = ((row & 7) << bits(low)) + (row >> 3)
    source = source ^ (lax.axis_index(axis) << bits(length))
    order = one_hot([source], time)
    for line in range(reach):
        x = jnp.concatenate([x_ref[line] for x_ref in x_refs], axis=0)
        if line == 0 or line == reach - 1:
            place = lax.axis_index(axis) ^ flip(axis)
            missing = place == (0 if line == 0 else lax.axis_size(axis) - 1)
            x = jnp.where(missing, seam_ref[...].reshape(time, channels), x)
        token_ref[line * time : (line + 1) * time] = dot(order, x).astype(BF16)
    inner = dot(token_ref[...], weight_ref[:, :width]).astype(BF16).astype(F32)
    inner_ref[:, 1 : low + 1] = inner.reshape(reach, low, SLOTS, width)
    place = lax.broadcasted_iota(jnp.int32, (SLOTS, width), 0)
    for line in range(reach):
        inner_ref[line, 0] = jnp.where(place == 0, 0.0, pltpu.roll(inner_ref[line, low], 1, 0))
        inner_ref[line, low + 1] = jnp.where(place == SLOTS - 1, 0.0, pltpu.roll(inner_ref[line, 1], SLOTS - 1, 0))

    conv_bias = conv_bias_ref[...][None]

    def convolve(pair, _):
        for group in range(width // (2 * LANES)):
            cells = slice(group * 2 * LANES, (group + 1) * 2 * LANES)
            half = (group * 2 * LANES) // chunk
            base = group * 2 * LANES - half * chunk
            bias = jnp.broadcast_to(conv_bias[:, cells], (SLOTS, 2 * LANES))
            totals = [[bias for _ in range(2)] for _ in range(lines)]
            for across in range(3):
                for along in range(3):
                    first, second = across_first(across, along)
                    tap = jnp.broadcast_to(conv_ref[first, second : second + 1, cells], (SLOTS, 2 * LANES))
                    for line in range(lines):
                        for sub in range(2):
                            totals[line][sub] += inner_ref[line + across, 2 * pair + sub + along, :, cells] * tap
            for line in range(lines):
                value = jnp.concatenate(totals[line], axis=0)
                value = 0.5 * value
                value = value * jnp.tanh(value) + value
                value = value.astype(BF16)
                for piece in range(2):
                    at = base + piece * LANES
                    start = ((half + at // chunk) * lines + line) * time
                    start = pl.multiple_of(start + pair * (2 * SLOTS), 2 * SLOTS)
                    active_ref[pl.ds(start, 2 * SLOTS), at % chunk : at % chunk + LANES] = value[
                        :, piece * LANES : (piece + 1) * LANES
                    ]
        return 0

    lax.fori_loop(0, low // 2, convolve, 0)

    bias_ref[...] = by_slot(halves, lambda half, way: bias_raw_ref[ks[way] : ks[way] + 1, half * chunk : (half + 1) * chunk])
    for half in range(halves):
        cells = slice(half * chunk, (half + 1) * chunk)
        for way in range(2):
            kind = slice((half * 2 + way) * LANES, (half * 2 + way + 1) * LANES)
            w = proj_raw_ref[ks[way], :, cells].astype(F32)
            ranks = w[:RANK]
            rest = jnp.zeros((LANES - 3 * RANK - 2 * states, chunk), F32)
            w = jnp.concatenate([ranks, ranks, ranks, w[RANK:], rest], axis=0)
            proj_ref[:, kind] = w.T.astype(BF16)
            w = step_raw_ref[ks[way], :, cells]
            high = w.astype(BF16).astype(F32)
            rest = jnp.zeros((LANES - 3 * RANK, chunk), F32)
            step_ref[kind, :] = jnp.concatenate([high, high, w - high, rest], axis=0).astype(BF16)

    piece = 256
    for first in range(0, time * SLOTS, piece):
        row = rows_of(piece, first)
        now = row >> 3
        slot = row & 7
        line = slot & (slot_lines - 1)
        back = (slot >> bits(slot_lines)) & 1
        half = slot >> bits(2 * slot_lines)
        when = jnp.where(back == 1, time - 1 - now, now)
        source = half * (lines * time) + line * time + ((when & (low - 1)) << 3) + (when >> bits(low))
        if slot_lines > lines:
            source = jnp.where(line < lines, source, -1)
        u = dot(one_hot([source], halves * lines * time), active_ref[...])
        steps = pl.ds(first // SLOTS, piece // SLOTS)
        v_ref[steps] = u.reshape(piece // SLOTS, SLOTS, chunk)
        kind = slot >> bits(slot_lines)
        projected = dot(u.astype(BF16), proj_ref[...])
        p = projected[:, :LANES]
        for other in range(1, 2 * halves):
            p = jnp.where(kind == other, projected[:, other * LANES : (other + 1) * LANES], p)
        if halves == 2:
            p = p.reshape(piece // SLOTS, SLOTS, LANES)
            p = p + pltpu.roll(p, SLOTS // 2, 1)
            p = p.reshape(piece, LANES)
        proj_out_ref[steps] = p.reshape(piece // SLOTS, SLOTS, LANES)
        high = p.astype(BF16).astype(F32)
        lane = lax.broadcasted_iota(jnp.int32, p.shape, 1)
        mixed = jnp.where(jnp.logical_and(lane >= RANK, lane < 2 * RANK), p - high, high)
        stacked = jnp.concatenate([jnp.where(kind == k, mixed, 0.0).astype(BF16) for k in range(2 * halves)], axis=1)
        s_ref[steps] = dot(stacked, step_ref[...]).reshape(piece // SLOTS, SLOTS, chunk)

    def soften(lap, _):
        for sub in range(8):
            t = lap * 8 + sub
            for g in range(chunk // LANES):
                cells = slice(g * LANES, (g + 1) * LANES)
                before = s_ref[t, :, cells] + bias_ref[:, cells]
                small = jnp.exp(-jnp.abs(before))
                log1p = jnp.where(small < 0.001, small - 0.5 * small * small, jnp.log(1.0 + small))
                step = jnp.maximum(before, 0.0) + log1p
                s_ref[t, :, cells] = step
        return 0

    lax.fori_loop(0, time // 8, soften, 0)


def scan_kernel(
    axis,
    after_ref,
    coef_ref,
    s_ref,
    u_ref,
    decay_ref,
    skip_raw_ref,
    out_ref,
    v_ref,
    y_ref,
    spread_ref,
):
    time, _, chunk = s_ref.shape
    halves = decay_ref.shape[2] // chunk
    states = decay_ref.shape[1]
    groups = chunk // LANES
    at_once = max(1, 12 // groups)
    unroll = 16 if axis == "col" else 8
    laps = time // unroll
    base2 = axis == "col"
    power = jnp.exp2 if base2 else jnp.exp

    ks = (0, 1) if axis == "col" else (2, 3)
    piece = 32
    row = lax.broadcasted_iota(jnp.int32, (2 * LANES, LANES), 0) & (LANES - 1)
    taken = [jnp.where(row == 3 * RANK + n, 1.0, 0.0).astype(BF16) for n in range(2 * states)]

    def spread(lap, _):
        steps = pl.ds(lap * piece, piece)
        coefs = coef_ref[steps].reshape(piece * SLOTS, LANES)
        high = coefs.astype(BF16)
        both = jnp.concatenate([high, (coefs - high.astype(F32)).astype(BF16)], axis=1)
        for n in range(0, 2 * states, 4):
            found = dot(both, jnp.concatenate(taken[n : n + 4], axis=1))
            for k in range(4):
                spread_ref[steps, n + k] = found[:, k * LANES : (k + 1) * LANES].reshape(piece, SLOTS, LANES)
        return 0

    lax.fori_loop(0, time // piece, spread, 0)
    for first in range(0, states, at_once):
        rates = []
        for n in range(first, first + at_once):
            rates.append([])
            for g in range(groups):
                rate = by_slot(
                    halves,
                    lambda half, way: decay_ref[ks[way], n : n + 1, half * chunk + g * LANES : half * chunk + (g + 1) * LANES],
                )
                rates[-1].append((-LOG2E if base2 else -1.0) * jnp.exp(rate))
        if first == 0:
            skips = [
                by_slot(
                    halves,
                    lambda half, way: skip_raw_ref[
                        ks[way] : ks[way] + 1, half * chunk + g * LANES : half * chunk + (g + 1) * LANES
                    ],
                )
                for g in range(groups)
            ]

        def advance(lap, hidden):
            hidden = list(hidden)
            for sub in range(unroll):
                t = lap * unroll + sub
                enter = [spread_ref[t, first + n] for n in range(at_once)]
                leave = [spread_ref[t, states + first + n] for n in range(at_once)]
                for g in range(groups):
                    cells = pl.ds(g * LANES, LANES)
                    step = s_ref[t, :, cells]
                    if first == 0:
                        u = u_ref[t, :, cells]
                        value = step * u
                        v_ref[t, :, cells] = value
                        y = skips[g] * u
                    else:
                        value = v_ref[t, :, cells]
                        y = y_ref[t, :, cells]
                    for n in range(at_once):
                        k = n * groups + g
                        h = power(step * rates[n][g]) * hidden[k] + value * enter[n]
                        hidden[k] = h
                        y = y + h * leave[n]
                    y_ref[t, :, cells] = y
            return tuple(hidden)

        zero = jnp.zeros((SLOTS, LANES), F32)
        lax.fori_loop(0, laps, advance, (zero,) * (at_once * groups))

    out_ref[...] = y_ref[...].reshape(time * SLOTS, chunk).astype(BF16)


def join_kernel(parts, lines, axis, after_ref, scanned_ref, *out_refs):
    length = out_refs[0].shape[-2] // lines
    time = parts * length
    chunk = scanned_ref.shape[1]
    halves = out_refs[0].shape[-1] // chunk
    slot_lines = SLOTS // (2 * halves)
    row = rows_of(lines * time)
    line = (row >> bits(length)) & (lines - 1)
    part = row >> bits(lines * length)
    part = part ^ lax.axis_index(axis)
    now = (part << bits(length)) + (row & (length - 1))
    for half in range(halves):
        ahead = now * SLOTS + (half * 2 * slot_lines) + line
        behind = (time - 1 - now) * SLOTS + (half * 2 * slot_lines + slot_lines) + line
        joined = dot(one_hot([ahead, behind], time * SLOTS), scanned_ref[...]).astype(BF16)
        size = lines * length
        for part in range(parts):
            found = joined[part * size : (part + 1) * size]
            if len(out_refs) < parts:
                out_refs[part >> 1][part & 1, :, half * chunk : (half + 1) * chunk] = found
            else:
                out_refs[part][:, half * chunk : (half + 1) * chunk] = found


def join(axis, scanned, parts, lines, length, width, after):
    size = (lines * length, width)
    shapes = [size] * parts if axis == "col" else [(2,) + size] * (parts // 2)
    return pl.pallas_call(
        functools.partial(join_kernel, parts, lines, axis),
        out_shape=[jax.ShapeDtypeStruct(shape, BF16) for shape in shapes],
        in_specs=[pl.BlockSpec(memory_space=pl.ANY), pl.BlockSpec(memory_space=pltpu.VMEM)],
        out_specs=[pl.BlockSpec(memory_space=pltpu.VMEM)] * len(shapes),
        compiler_params=pltpu.CompilerParams(vmem_limit_bytes=24 * 1024 * 1024),
    )(after, scanned)


RANK = 24


def prepare(axis, after, xs, seam, in_weight, conv, conv_bias, proj, step_weight, step_bias, decay_log, skip):
    parts, length, channels = seam.shape
    reach = xs[0].shape[-3]
    lines = reach - 2
    time = parts * length
    width = conv.shape[2]
    states = decay_log.shape[2]
    assert step_weight.shape[1] == RANK and in_weight.shape[1] == 2 * width
    halves = 1 if lines >= 4 else 2
    assert lines <= SLOTS // (2 * halves)
    chunk = width // halves
    vmem = pl.BlockSpec(memory_space=pltpu.VMEM)
    flops = 2 * time * (reach * channels * width + SLOTS * width * 256)
    return pl.pallas_call(
        functools.partial(prepare_kernel, lines, axis),
        out_shape=[
            jax.ShapeDtypeStruct((time, SLOTS, LANES), F32),
            jax.ShapeDtypeStruct((time, SLOTS, chunk), F32),
            jax.ShapeDtypeStruct((time, SLOTS, chunk), F32),
        ],
        in_specs=[pl.BlockSpec(memory_space=pl.ANY)] + [vmem] * (len(xs) + 7),
        out_specs=[vmem, vmem, vmem],
        scratch_shapes=[
            pltpu.VMEM((reach * time, channels), BF16),
            pltpu.VMEM((reach, time // SLOTS + 2, SLOTS, width), F32),
            pltpu.VMEM((halves * lines * time, chunk), BF16),
            pltpu.VMEM((chunk, halves * 2 * LANES), BF16),
            pltpu.VMEM((halves * 2 * LANES, chunk), BF16),
            pltpu.VMEM((SLOTS, chunk), F32),
        ],
        compiler_params=pltpu.CompilerParams(vmem_limit_bytes=24 * 1024 * 1024),
        cost_estimate=pl.CostEstimate(flops=4 * flops, bytes_accessed=4 * 1024 * 1024, transcendentals=time * SLOTS * chunk),
    )(
        after,
        *xs,
        seam,
        in_weight,
        conv,
        conv_bias,
        jnp.swapaxes(proj, 1, 2),
        step_weight,
        step_bias,
    )


def scan(axis, after, coefs, steps, u, decay_log, skip):
    time, _, chunk = steps.shape
    width, states = decay_log.shape[1:]
    vmem = pl.BlockSpec(memory_space=pltpu.VMEM)
    return pl.pallas_call(
        functools.partial(scan_kernel, axis),
        out_shape=jax.ShapeDtypeStruct((time * SLOTS, chunk), BF16),
        in_specs=[pl.BlockSpec(memory_space=pl.ANY), vmem, vmem, vmem, vmem, vmem],
        out_specs=vmem,
        scratch_shapes=[
            pltpu.VMEM((time, SLOTS, chunk), F32),
            pltpu.VMEM((time, SLOTS, chunk), F32),
            pltpu.VMEM((time, 2 * states, SLOTS, LANES), F32),
        ],
        compiler_params=pltpu.CompilerParams(vmem_limit_bytes=(8 << 20) + time * (136 << 10) + time * 20 * chunk),
        cost_estimate=pl.CostEstimate(
            flops=8 * time * SLOTS * chunk * states,
            bytes_accessed=4 * 1024 * 1024,
            transcendentals=time * SLOTS * chunk * states,
        ),
    )(after, coefs, steps, u, jnp.swapaxes(decay_log, 1, 2), skip)


def end_kernel(columns, gate_ref, gain_ref, weight_ref, *refs):
    pair_refs, beside_ref, row_refs, out_ref, gated_ref = refs[:columns], refs[columns], refs[columns + 1 : -2], refs[-2], refs[-1]
    height, width, channels = out_ref.shape
    size = row_refs[0].shape[0]
    lines = size // width
    swap = flip("col") ^ lax.axis_index("col")
    turn = (flip("row") ^ lax.axis_index("row")) * (width // lax.axis_size("row"))
    row = rows_of(height * width)
    line = (row >> bits(width)) ^ (swap * lines)
    source = (((row & (width - 1)) ^ turn) << bits(height)) + line
    rows = jnp.concatenate([row_ref[...] for row_ref in row_refs], axis=0)
    blocks = []
    for part in range(columns):
        blocks += [pair_refs[part][0], beside_ref[part]]
    columns = jnp.concatenate(blocks, axis=0)
    combined = layer_norm(rows.astype(F32) + dot(one_hot([source], height * width), columns), gain_ref[...][None])
    for part in range(len(row_refs)):
        cells = pl.ds(pl.multiple_of((part ^ swap) * size, size), size)
        gate = gate_ref[cells].astype(F32)
        gated_ref[cells] = (combined[part * size : (part + 1) * size] * (gate / (1.0 + jnp.exp(-gate)))).astype(BF16)
    out = dot(gated_ref[...], weight_ref[...]).astype(BF16)
    out_ref[...] = out.reshape(height, width, channels)


def pair_kernel(*refs):
    count = len(refs) // 2
    own_refs, beside_ref, out_refs = refs[:count], refs[count], refs[count + 1 :]
    for k in range(count):
        out_refs[k][0] = own_refs[k][...]
        out_refs[k][1] = beside_ref[k + 1]


def first_kernel(own_ref, beside_ref, out_ref):
    out_ref[0] = own_ref[...]
    out_ref[1] = beside_ref[0]


def collect_kernel(after_ref, *refs):
    out_ref = refs[-1]
    for k in range(len(refs) - 1):
        out_ref[k] = refs[k][1]


def simple(kernel, shapes, *arrays, after=None):
    vmem = pl.BlockSpec(memory_space=pltpu.VMEM)
    first = [] if after is None else [after]
    many = isinstance(shapes, list)
    return pl.pallas_call(
        kernel,
        out_shape=shapes,
        in_specs=[pl.BlockSpec(memory_space=pl.ANY)] * len(first) + [vmem] * len(arrays),
        out_specs=[vmem] * len(shapes) if many else vmem,
        compiler_params=pltpu.CompilerParams(vmem_limit_bytes=4 * 1024 * 1024),
        cost_estimate=pl.CostEstimate(flops=0, bytes_accessed=2 << 20, transcendentals=0),
    )(*first, *arrays)


def swap(block, axis, k):
    return lax.ppermute(block, axis, [(i, i ^ k) for i in range(lax.axis_size(axis))])


def swap_out(own, beside):
    beside = swap(beside, "row", 1)
    shape = jax.ShapeDtypeStruct((2,) + own[0].shape, own[0].dtype)
    pairs = simple(pair_kernel, [shape] * (len(own) - 1), *own[1:], beside)
    found = {k: swap(pairs[k - 1], "row", 2 * k) for k in range(len(own) - 1, 0, -1)}
    first = simple(first_kernel, jax.ShapeDtypeStruct((2,) + own[0].shape, own[0].dtype), own[0], beside)
    return [first] + [found[k] for k in range(1, len(own))]


def swap_back_far(pairs):
    found = {k: swap(pairs[k], "row", 2 * k) for k in range(len(pairs) - 1, 0, -1)}
    return [pairs[0]] + [found[k] for k in range(1, len(pairs))]


def swap_blocks(blocks, axis):
    count = lax.axis_size(axis)
    found = {k: lax.ppermute(blocks[k], axis, [(i, i ^ k) for i in range(count)]) for k in range(count - 1, 0, -1)}
    return [blocks[0]] + [found[k] for k in range(1, count)]


def pick_kernel(axis, after_ref, *refs):
    x_refs, out_ref = views(refs[:-1], 3), refs[-1]
    place = lax.axis_index(axis) ^ flip(axis)
    line = jnp.where(place == 0, 1, x_refs[0].shape[0] - 2)
    for part, x_ref in enumerate(x_refs):
        out_ref[part] = x_ref[line]


def pick(axis, after, xs):
    return pl.pallas_call(
        functools.partial(pick_kernel, axis),
        out_shape=jax.ShapeDtypeStruct((lax.axis_size("col" if axis == "col" else "row"),) + xs[-1].shape[-2:], xs[-1].dtype),
        in_specs=[pl.BlockSpec(memory_space=pl.ANY)] + [pl.BlockSpec(memory_space=pltpu.VMEM)] * len(xs),
        out_specs=pl.BlockSpec(memory_space=pltpu.VMEM),
        compiler_params=pltpu.CompilerParams(vmem_limit_bytes=4 * 1024 * 1024),
    )(after, *xs)


def seam_of(axis, line):
    count = lax.axis_size(axis)
    height, breadth = lax.axis_size("row"), lax.axis_size("col")
    if axis == "row":
        at = lambda group: (0 if group & 1 else count - 1) * breadth
        ends = [(at(c) + c, at(c) + c + 1) for c in range(breadth - 1)]
    else:
        at = lambda group: 0 if group & 1 else count - 1
        ends = [(at(r) + r * breadth, at(r) + (r + 1) * breadth) for r in range(height - 1)]
    pairs = ends + [(b, a) for a, b in ends]
    return lax.ppermute(line, ("row", "col"), pairs)


def local(
    features,
    norm_gain,
    in_weight,
    conv_weight,
    conv_bias,
    proj_weight,
    step_weight,
    step_bias,
    decay_log,
    skip_gain,
    out_gain,
    out_weight,
):
    height, width, channels = features.shape
    inner = out_weight.shape[0]
    tokens = height * width
    row_lines = height // lax.axis_size("col")
    col_lines = width // lax.axis_size("row")

    rows, cols = lax.axis_size("row"), lax.axis_size("col")
    vmem = pl.BlockSpec(memory_space=pltpu.VMEM)
    normed, *sends = pl.pallas_call(
        functools.partial(cut_kernel, rows),
        out_shape=[jax.ShapeDtypeStruct((tokens, channels), BF16)]
        + [jax.ShapeDtypeStruct((col_lines + 2, height, channels), BF16)] * (rows // 2)
        + [jax.ShapeDtypeStruct((rows // 2, col_lines + 2, height, channels), BF16)]
        + [jax.ShapeDtypeStruct((row_lines + 2, width, channels), BF16)] * cols,
        in_specs=[pl.BlockSpec(features.shape, lambda: (0, 0, 0)), pl.BlockSpec((channels,), lambda: (0,))],
        out_specs=[vmem] * (2 + rows // 2 + cols),
        scratch_shapes=[pltpu.VMEM((tokens, channels), BF16)],
        compiler_params=pltpu.CompilerParams(vmem_limit_bytes=12 * 1024 * 1024),
        cost_estimate=pl.CostEstimate(flops=6_000_000_000, bytes_accessed=2 << 20, transcendentals=tokens),
    )(features, norm_gain)
    weights = (in_weight, conv_weight, conv_bias, proj_weight, step_weight, step_bias, decay_log, skip_gain)
    gate = pl.pallas_call(
        gate_kernel,
        out_shape=jax.ShapeDtypeStruct((tokens, inner), BF16),
        grid=(1,),
        in_specs=[
            pl.BlockSpec((tokens, channels), lambda i: (0, 0)),
            pl.BlockSpec((channels, inner), lambda i: (0, 1)),
        ],
        out_specs=pl.BlockSpec((tokens, inner), lambda i: (0, 0)),
        compiler_params=pltpu.CompilerParams(vmem_limit_bytes=12 * 1024 * 1024),
        cost_estimate=pl.CostEstimate(flops=2 * tokens * channels * inner, bytes_accessed=1 << 20, transcendentals=0),
    )(normed, in_weight)

    half = rows // 2
    row_x = swap_blocks(sends[half + 1 :], "col")
    col_x = swap_out(sends[:half], sends[half])
    row_seam = seam_of("col", pick("col", normed, row_x))
    row_steps = prepare("col", normed, row_x, row_seam, *weights)
    col_seam = seam_of("row", pick("row", row_steps[0], col_x))
    col_steps = prepare("row", row_steps[0], col_x, col_seam, *weights)
    col_y = scan("row", normed, *col_steps, decay_log, skip_gain)
    joined = join("row", col_y, rows, col_lines, height, inner, normed)
    col_y = swap_back_far(joined)
    row_y = scan("col", joined[0], *row_steps, decay_log, skip_gain)
    beside = jax.ShapeDtypeStruct((half,) + joined[0].shape[1:], BF16)
    beside = simple(collect_kernel, beside, *col_y, after=row_y)
    row_y = swap_blocks(join("col", row_y, cols, row_lines, width, inner, beside), "col")
    beside = swap(beside, "row", 1)
    return pl.pallas_call(
        functools.partial(end_kernel, half),
        out_shape=jax.ShapeDtypeStruct(features.shape, BF16),
        scratch_shapes=[pltpu.VMEM((tokens, inner), BF16)],
        compiler_params=pltpu.CompilerParams(vmem_limit_bytes=16 * 1024 * 1024),
    )(gate, out_gain, out_weight, *col_y, beside, *row_y)


def solution(mesh):
    in_specs = (P("row", "col", None), P(), P(), P(), P(), P(), P(), P(), P(), P(), P(), P())
    out_specs = P("row", "col", None)
    return jax.shard_map(local, mesh=mesh, in_specs=in_specs, out_specs=out_specs, check_vma=False)
```

```python
import functools

import jax
import jax.numpy as jnp
from jax import lax
from jax.experimental import pallas as pl
from jax.experimental.pallas import tpu as pltpu
from jax.sharding import PartitionSpec as P

F32 = jnp.float32
BF16 = jnp.bfloat16
LANES = 128
SLOTS = 8
LOG2E = 1.4426950408889634


def bits(value):
    assert value & (value - 1) == 0
    return value.bit_length() - 1


def one_hot(targets, width):
    lane = lax.broadcasted_iota(jnp.int32, targets[0].shape, 1)
    blocks = []
    for block in range(pl.cdiv(width, LANES)):
        hit = targets[0] == lane + block * LANES
        for other in targets[1:]:
            hit = jnp.logical_or(hit, other == lane + block * LANES)
        blocks.append(jnp.where(hit, 1.0, 0.0).astype(BF16))
    return jnp.concatenate(blocks, axis=1)[:, :width]


def rows_of(count, start=0):
    return lax.broadcasted_iota(jnp.int32, (count, LANES), 0) + start


def dot(a, b):
    return jnp.dot(a, b, preferred_element_type=F32)


def layer_norm(values, scale_gain):
    centred = values - jnp.mean(values, axis=-1, keepdims=True)
    spread = jnp.mean(centred * centred, axis=-1, keepdims=True)
    return centred * lax.rsqrt(spread + 1e-05) * scale_gain


def flip(axis):
    other = "col" if axis == "row" else "row"
    return (lax.axis_index(other) & 1) * (lax.axis_size(axis) - 1)


def cut_kernel(columns, feat_ref, gain_ref, norm_ref, *refs):
    col_refs, beside_ref, row_refs, turned_ref = refs[: columns // 2], refs[columns // 2], refs[columns // 2 + 1 : -1], refs[-1]
    height, width, channels = feat_ref.shape
    tile = layer_norm(feat_ref[...].reshape(height * width, channels).astype(F32), gain_ref[...][None]).astype(BF16)
    norm_ref[...] = tile
    reach = row_refs[0].shape[0]
    turn = flip("col") ^ lax.axis_index("col")
    for part, row_ref in enumerate(row_refs):
        for line in range(reach):
            at = jnp.clip((part ^ turn) * (reach - 2) + line - 1, 0, height - 1)
            row_ref[line] = norm_ref[pl.ds(pl.multiple_of(at * width, width), width)]
    row = rows_of(height * width)
    turned = dot(one_hot([((row & (height - 1)) << bits(width)) + (row >> bits(height))], height * width), tile).astype(
        BF16
    )
    turned_ref[...] = turned
    reach = col_refs[0].shape[0]
    turn = flip("row") ^ lax.axis_index("row")
    for part in range(columns):
        for line in range(reach):
            at = jnp.clip((part ^ turn) * (reach - 2) + line - 1, 0, width - 1)
            found = turned_ref[pl.ds(pl.multiple_of(at * height, height), height)]
            if part & 1:
                beside_ref[part >> 1, line] = found
            else:
                col_refs[part >> 1][line] = found


def gate_kernel(norm_ref, weight_ref, gate_ref):
    gate_ref[...] = dot(norm_ref[...], weight_ref[...]).astype(BF16)


def views(refs, rank):
    found = []
    for ref in refs:
        found += [ref] if len(ref.shape) == rank else [ref.at[k] for k in range(ref.shape[0])]
    return found


def by_slot(halves, rows):
    found = None
    for kind in range(halves * 2):
        row = rows(kind >> 1, kind & 1)
        row = jnp.broadcast_to(row, (SLOTS, row.shape[1]))
        slot = lax.broadcasted_iota(jnp.int32, row.shape, 0)
        found = row if found is None else jnp.where(slot >= kind * (SLOTS // (halves * 2)), row, found)
    return found


def prepare_kernel(
    lines,
    axis,
    after_ref,
    *refs,
):
    x_refs, refs = views(refs[:-16], 3), refs[-16:]
    (
        seam_ref,
        weight_ref,
        conv_ref,
        conv_bias_ref,
        proj_raw_ref,
        step_raw_ref,
        bias_raw_ref,
        proj_out_ref,
        s_ref,
        v_ref,
        token_ref,
        inner_ref,
        active_ref,
        proj_ref,
        step_ref,
        bias_ref,
    ) = refs
    ks = (0, 1) if axis == "col" else (2, 3)
    parts, length, channels = seam_ref.shape
    reach = lines + 2
    states = (proj_raw_ref.shape[1] - RANK) // 2
    time = parts * length
    low = time // SLOTS
    width = weight_ref.shape[1] // 2
    chunk = s_ref.shape[2]
    halves = width // chunk
    slot_lines = SLOTS // (2 * halves)
    if axis == "row":
        across_first = lambda across, along: (along, across)
    else:
        across_first = lambda across, along: (across, along)

    row = rows_of(time)
    source = ((row & 7) << bits(low)) + (row >> 3)
    source = source ^ (lax.axis_index(axis) << bits(length))
    order = one_hot([source], time)
    for line in range(reach):
        x = jnp.concatenate([x_ref[line] for x_ref in x_refs], axis=0)
        if line == 0 or line == reach - 1:
            place = lax.axis_index(axis) ^ flip(axis)
            missing = place == (0 if line == 0 else lax.axis_size(axis) - 1)
            x = jnp.where(missing, seam_ref[...].reshape(time, channels), x)
        token_ref[line * time : (line + 1) * time] = dot(order, x).astype(BF16)
    inner = dot(token_ref[...], weight_ref[:, :width]).astype(BF16).astype(F32)
    inner_ref[:, 1 : low + 1] = inner.reshape(reach, low, SLOTS, width)
    place = lax.broadcasted_iota(jnp.int32, (SLOTS, width), 0)
    for line in range(reach):
        inner_ref[line, 0] = jnp.where(place == 0, 0.0, pltpu.roll(inner_ref[line, low], 1, 0))
        inner_ref[line, low + 1] = jnp.where(place == SLOTS - 1, 0.0, pltpu.roll(inner_ref[line, 1], SLOTS - 1, 0))

    conv_bias = conv_bias_ref[...][None]

    def convolve(pair, _):
        for group in range(width // (2 * LANES)):
            cells = slice(group * 2 * LANES, (group + 1) * 2 * LANES)
            half = (group * 2 * LANES) // chunk
            base = group * 2 * LANES - half * chunk
            bias = jnp.broadcast_to(conv_bias[:, cells], (SLOTS, 2 * LANES))
            totals = [[bias for _ in range(2)] for _ in range(lines)]
            for across in range(3):
                for along in range(3):
                    first, second = across_first(across, along)
                    tap = jnp.broadcast_to(conv_ref[first, second : second + 1, cells], (SLOTS, 2 * LANES))
                    for line in range(lines):
                        for sub in range(2):
                            totals[line][sub] += inner_ref[line + across, 2 * pair + sub + along, :, cells] * tap
            for line in range(lines):
                value = jnp.concatenate(totals[line], axis=0)
                value = 0.5 * value
                value = value * jnp.tanh(value) + value
                value = value.astype(BF16)
                for piece in range(2):
                    at = base + piece * LANES
                    start = ((half + at // chunk) * lines + line) * time
                    start = pl.multiple_of(start + pair * (2 * SLOTS), 2 * SLOTS)
                    active_ref[pl.ds(start, 2 * SLOTS), at % chunk : at % chunk + LANES] = value[
                        :, piece * LANES : (piece + 1) * LANES
                    ]
        return 0

    lax.fori_loop(0, low // 2, convolve, 0)

    bias_ref[...] = by_slot(halves, lambda half, way: bias_raw_ref[ks[way] : ks[way] + 1, half * chunk : (half + 1) * chunk])
    for half in range(halves):
        cells = slice(half * chunk, (half + 1) * chunk)
        for way in range(2):
            kind = slice((half * 2 + way) * LANES, (half * 2 + way + 1) * LANES)
            w = proj_raw_ref[ks[way], :, cells].astype(F32)
            ranks = w[:RANK]
            rest = jnp.zeros((LANES - 3 * RANK - 2 * states, chunk), F32)
            w = jnp.concatenate([ranks, ranks, ranks, w[RANK:], rest], axis=0)
            proj_ref[:, kind] = w.T.astype(BF16)
            w = step_raw_ref[ks[way], :, cells]
            high = w.astype(BF16).astype(F32)
            rest = jnp.zeros((LANES - 3 * RANK, chunk), F32)
            step_ref[kind, :] = jnp.concatenate([high, high, w - high, rest], axis=0).astype(BF16)

    piece = 256
    for first in range(0, time * SLOTS, piece):
        row = rows_of(piece, first)
        now = row >> 3
        slot = row & 7
        line = slot & (slot_lines - 1)
        back = (slot >> bits(slot_lines)) & 1
        half = slot >> bits(2 * slot_lines)
        when = jnp.where(back == 1, time - 1 - now, now)
        source = half * (lines * time) + line * time + ((when & (low - 1)) << 3) + (when >> bits(low))
        if slot_lines > lines:
            source = jnp.where(line < lines, source, -1)
        u = dot(one_hot([source], halves * lines * time), active_ref[...])
        steps = pl.ds(first // SLOTS, piece // SLOTS)
        v_ref[steps] = u.reshape(piece // SLOTS, SLOTS, chunk)
        kind = slot >> bits(slot_lines)
        projected = dot(u.astype(BF16), proj_ref[...])
        p = projected[:, :LANES]
        for other in range(1, 2 * halves):
            p = jnp.where(kind == other, projected[:, other * LANES : (other + 1) * LANES], p)
        if halves == 2:
            p = p.reshape(piece // SLOTS, SLOTS, LANES)
            p = p + pltpu.roll(p, SLOTS // 2, 1)
            p = p.reshape(piece, LANES)
        proj_out_ref[steps] = p.reshape(piece // SLOTS, SLOTS, LANES)
        high = p.astype(BF16).astype(F32)
        lane = lax.broadcasted_iota(jnp.int32, p.shape, 1)
        mixed = jnp.where(jnp.logical_and(lane >= RANK, lane < 2 * RANK), p - high, high)
        stacked = jnp.concatenate([jnp.where(kind == k, mixed, 0.0).astype(BF16) for k in range(2 * halves)], axis=1)
        s_ref[steps] = dot(stacked, step_ref[...]).reshape(piece // SLOTS, SLOTS, chunk)

    def soften(lap, _):
        for sub in range(8):
            t = lap * 8 + sub
            for g in range(chunk // LANES):
                cells = slice(g * LANES, (g + 1) * LANES)
                before = s_ref[t, :, cells] + bias_ref[:, cells]
                small = jnp.exp(-jnp.abs(before))
                log1p = jnp.where(small < 0.001, small - 0.5 * small * small, jnp.log(1.0 + small))
                step = jnp.maximum(before, 0.0) + log1p
                s_ref[t, :, cells] = step
        return 0

    lax.fori_loop(0, time // 8, soften, 0)


def scan_kernel(
    axis,
    after_ref,
    coef_ref,
    s_ref,
    u_ref,
    decay_ref,
    skip_raw_ref,
    out_ref,
    v_ref,
    y_ref,
    *spread_refs,
):
    time, _, chunk = s_ref.shape
    halves = decay_ref.shape[2] // chunk
    states = decay_ref.shape[1]
    groups = chunk // LANES
    at_once = max(1, 12 // groups)
    unroll = 16
    laps = time // unroll

    ks = (0, 1) if axis == "col" else (2, 3)
    row = lax.broadcasted_iota(jnp.int32, (2 * LANES, LANES), 0) & (LANES - 1)

    def spread(lap, first, into_ref):
        steps = pl.ds(lap * unroll, unroll)
        coefs = coef_ref[steps].reshape(unroll * SLOTS, LANES)
        high = coefs.astype(BF16)
        both = jnp.concatenate([high, (coefs - high.astype(F32)).astype(BF16)], axis=1)
        lanes = [3 * RANK + kind * states + first + n for kind in range(2) for n in range(at_once)]
        taken = jnp.concatenate([jnp.where(row == lane, 1.0, 0.0).astype(BF16) for lane in lanes], axis=1)
        found = dot(both, taken)
        for k in range(2 * at_once):
            into_ref[steps, k] = found[:, k * LANES : (k + 1) * LANES].reshape(unroll, SLOTS, LANES)

    def begin(lap, _):
        spread(lap, 0, spread_refs[0])
        return 0

    lax.fori_loop(0, laps, begin, 0)
    for first in range(0, states, at_once):
        rates = []
        for n in range(first, first + at_once):
            rates.append([])
            for g in range(groups):
                rate = by_slot(
                    halves,
                    lambda half, way: decay_ref[ks[way], n : n + 1, half * chunk + g * LANES : half * chunk + (g + 1) * LANES],
                )
                rates[-1].append(-LOG2E * jnp.exp(rate))
        if first == 0:
            skips = [
                by_slot(
                    halves,
                    lambda half, way: skip_raw_ref[
                        ks[way] : ks[way] + 1, half * chunk + g * LANES : half * chunk + (g + 1) * LANES
                    ],
                )
                for g in range(groups)
            ]

        def advance(lap, hidden):
            hidden = list(hidden)
            if first + at_once < states:
                spread(lap, first + at_once, spread_refs[(first // at_once + 1) & 1])
            now_ref = spread_refs[(first // at_once) & 1]
            for sub in range(unroll):
                t = lap * unroll + sub
                enter = [now_ref[t, n] for n in range(at_once)]
                leave = [now_ref[t, at_once + n] for n in range(at_once)]
                for g in range(groups):
                    cells = pl.ds(g * LANES, LANES)
                    step = s_ref[t, :, cells]
                    if first == 0:
                        u = u_ref[t, :, cells]
                        value = step * u
                        v_ref[t, :, cells] = value
                        y = skips[g] * u
                    else:
                        value = v_ref[t, :, cells]
                        y = y_ref[t, :, cells]
                    for n in range(at_once):
                        k = n * groups + g
                        h = jnp.exp2(step * rates[n][g]) * hidden[k] + value * enter[n]
                        hidden[k] = h
                        y = y + h * leave[n]
                    y_ref[t, :, cells] = y
            return tuple(hidden)

        zero = jnp.zeros((SLOTS, LANES), F32)
        lax.fori_loop(0, laps, advance, (zero,) * (at_once * groups))

    out_ref[...] = y_ref[...].reshape(time * SLOTS, chunk).astype(BF16)


def join_kernel(parts, lines, axis, after_ref, scanned_ref, *out_refs):
    length = out_refs[0].shape[-2] // lines
    time = parts * length
    chunk = scanned_ref.shape[1]
    halves = out_refs[0].shape[-1] // chunk
    slot_lines = SLOTS // (2 * halves)
    row = rows_of(lines * time)
    line = (row >> bits(length)) & (lines - 1)
    part = row >> bits(lines * length)
    part = part ^ lax.axis_index(axis)
    now = (part << bits(length)) + (row & (length - 1))
    for half in range(halves):
        ahead = now * SLOTS + (half * 2 * slot_lines) + line
        behind = (time - 1 - now) * SLOTS + (half * 2 * slot_lines + slot_lines) + line
        joined = dot(one_hot([ahead, behind], time * SLOTS), scanned_ref[...]).astype(BF16)
        size = lines * length
        for part in range(parts):
            found = joined[part * size : (part + 1) * size]
            if len(out_refs) < parts:
                out_refs[part >> 1][part & 1, :, half * chunk : (half + 1) * chunk] = found
            else:
                out_refs[part][:, half * chunk : (half + 1) * chunk] = found


def join(axis, scanned, parts, lines, length, width, after):
    size = (lines * length, width)
    shapes = [size] * parts if axis == "col" else [(2,) + size] * (parts // 2)
    return pl.pallas_call(
        functools.partial(join_kernel, parts, lines, axis),
        out_shape=[jax.ShapeDtypeStruct(shape, BF16) for shape in shapes],
        in_specs=[pl.BlockSpec(memory_space=pl.ANY), pl.BlockSpec(memory_space=pltpu.VMEM)],
        out_specs=[pl.BlockSpec(memory_space=pltpu.VMEM)] * len(shapes),
        compiler_params=pltpu.CompilerParams(vmem_limit_bytes=24 * 1024 * 1024),
    )(after, scanned)


RANK = 24


def prepare(axis, after, xs, seam, in_weight, conv, conv_bias, proj, step_weight, step_bias, decay_log, skip):
    parts, length, channels = seam.shape
    reach = xs[0].shape[-3]
    lines = reach - 2
    time = parts * length
    width = conv.shape[2]
    states = decay_log.shape[2]
    assert step_weight.shape[1] == RANK and in_weight.shape[1] == 2 * width
    halves = 1 if lines >= 4 else 2
    assert lines <= SLOTS // (2 * halves)
    chunk = width // halves
    vmem = pl.BlockSpec(memory_space=pltpu.VMEM)
    flops = 2 * time * (reach * channels * width + SLOTS * width * 256)
    return pl.pallas_call(
        functools.partial(prepare_kernel, lines, axis),
        out_shape=[
            jax.ShapeDtypeStruct((time, SLOTS, LANES), F32),
            jax.ShapeDtypeStruct((time, SLOTS, chunk), F32),
            jax.ShapeDtypeStruct((time, SLOTS, chunk), F32),
        ],
        in_specs=[pl.BlockSpec(memory_space=pl.ANY)] + [vmem] * (len(xs) + 7),
        out_specs=[vmem, vmem, vmem],
        scratch_shapes=[
            pltpu.VMEM((reach * time, channels), BF16),
            pltpu.VMEM((reach, time // SLOTS + 2, SLOTS, width), F32),
            pltpu.VMEM((halves * lines * time, chunk), BF16),
            pltpu.VMEM((chunk, halves * 2 * LANES), BF16),
            pltpu.VMEM((halves * 2 * LANES, chunk), BF16),
            pltpu.VMEM((SLOTS, chunk), F32),
        ],
        compiler_params=pltpu.CompilerParams(vmem_limit_bytes=24 * 1024 * 1024),
        cost_estimate=pl.CostEstimate(flops=4 * flops, bytes_accessed=4 * 1024 * 1024, transcendentals=time * SLOTS * chunk),
    )(
        after,
        *xs,
        seam,
        in_weight,
        conv,
        conv_bias,
        jnp.swapaxes(proj, 1, 2),
        step_weight,
        step_bias,
    )


def scan(axis, after, coefs, steps, u, decay_log, skip):
    time, _, chunk = steps.shape
    width, states = decay_log.shape[1:]
    at_once = max(1, 12 // (chunk // LANES))
    vmem = pl.BlockSpec(memory_space=pltpu.VMEM)
    return pl.pallas_call(
        functools.partial(scan_kernel, axis),
        out_shape=jax.ShapeDtypeStruct((time * SLOTS, chunk), BF16),
        in_specs=[pl.BlockSpec(memory_space=pl.ANY), vmem, vmem, vmem, vmem, vmem],
        out_specs=vmem,
        scratch_shapes=[
            pltpu.VMEM((time, SLOTS, chunk), F32),
            pltpu.VMEM((time, SLOTS, chunk), F32),
            pltpu.VMEM((time, 2 * at_once, SLOTS, LANES), F32),
            pltpu.VMEM((time, 2 * at_once, SLOTS, LANES), F32),
        ],
        compiler_params=pltpu.CompilerParams(vmem_limit_bytes=(8 << 20) + time * at_once * (16 << 10) + time * 80 * chunk),
        cost_estimate=pl.CostEstimate(
            flops=8 * time * SLOTS * chunk * states,
            bytes_accessed=4 * 1024 * 1024,
            transcendentals=time * SLOTS * chunk * states,
        ),
    )(after, coefs, steps, u, jnp.swapaxes(decay_log, 1, 2), skip)


def end_kernel(columns, gate_ref, gain_ref, weight_ref, *refs):
    pair_refs, beside_ref, row_refs, out_ref, gated_ref = refs[:columns], refs[columns], refs[columns + 1 : -2], refs[-2], refs[-1]
    height, width, channels = out_ref.shape
    size = row_refs[0].shape[0]
    lines = size // width
    swap = flip("col") ^ lax.axis_index("col")
    turn = (flip("row") ^ lax.axis_index("row")) * (width // lax.axis_size("row"))
    row = rows_of(height * width)
    line = (row >> bits(width)) ^ (swap * lines)
    source = (((row & (width - 1)) ^ turn) << bits(height)) + line
    rows = jnp.concatenate([row_ref[...] for row_ref in row_refs], axis=0)
    blocks = []
    for part in range(columns):
        blocks += [pair_refs[part][0], beside_ref[part]]
    columns = jnp.concatenate(blocks, axis=0)
    combined = layer_norm(rows.astype(F32) + dot(one_hot([source], height * width), columns), gain_ref[...][None])
    for part in range(len(row_refs)):
        cells = pl.ds(pl.multiple_of((part ^ swap) * size, size), size)
        gate = gate_ref[cells].astype(F32)
        gated_ref[cells] = (combined[part * size : (part + 1) * size] * (gate / (1.0 + jnp.exp(-gate)))).astype(BF16)
    out = dot(gated_ref[...], weight_ref[...]).astype(BF16)
    out_ref[...] = out.reshape(height, width, channels)


def pair_kernel(*refs):
    count = len(refs) // 2
    own_refs, beside_ref, out_refs = refs[:count], refs[count], refs[count + 1 :]
    for k in range(count):
        out_refs[k][0] = own_refs[k][...]
        out_refs[k][1] = beside_ref[k + 1]


def first_kernel(own_ref, beside_ref, out_ref):
    out_ref[0] = own_ref[...]
    out_ref[1] = beside_ref[0]


def collect_kernel(after_ref, *refs):
    out_ref = refs[-1]
    for k in range(len(refs) - 1):
        out_ref[k] = refs[k][1]


def simple(kernel, shapes, *arrays, after=None):
    vmem = pl.BlockSpec(memory_space=pltpu.VMEM)
    first = [] if after is None else [after]
    many = isinstance(shapes, list)
    return pl.pallas_call(
        kernel,
        out_shape=shapes,
        in_specs=[pl.BlockSpec(memory_space=pl.ANY)] * len(first) + [vmem] * len(arrays),
        out_specs=[vmem] * len(shapes) if many else vmem,
        compiler_params=pltpu.CompilerParams(vmem_limit_bytes=4 * 1024 * 1024),
        cost_estimate=pl.CostEstimate(flops=0, bytes_accessed=2 << 20, transcendentals=0),
    )(*first, *arrays)


def swap(block, axis, k):
    return lax.ppermute(block, axis, [(i, i ^ k) for i in range(lax.axis_size(axis))])


def swap_out(own, beside):
    beside = swap(beside, "row", 1)
    shape = jax.ShapeDtypeStruct((2,) + own[0].shape, own[0].dtype)
    pairs = simple(pair_kernel, [shape] * (len(own) - 1), *own[1:], beside)
    found = {k: swap(pairs[k - 1], "row", 2 * k) for k in range(len(own) - 1, 0, -1)}
    first = simple(first_kernel, jax.ShapeDtypeStruct((2,) + own[0].shape, own[0].dtype), own[0], beside)
    return [first] + [found[k] for k in range(1, len(own))]


def swap_back_far(pairs):
    found = {k: swap(pairs[k], "row", 2 * k) for k in range(len(pairs) - 1, 0, -1)}
    return [pairs[0]] + [found[k] for k in range(1, len(pairs))]


def swap_blocks(blocks, axis):
    count = lax.axis_size(axis)
    found = {k: lax.ppermute(blocks[k], axis, [(i, i ^ k) for i in range(count)]) for k in range(count - 1, 0, -1)}
    return [blocks[0]] + [found[k] for k in range(1, count)]


def pick_kernel(axis, after_ref, *refs):
    x_refs, out_ref = views(refs[:-1], 3), refs[-1]
    place = lax.axis_index(axis) ^ flip(axis)
    line = jnp.where(place == 0, 1, x_refs[0].shape[0] - 2)
    for part, x_ref in enumerate(x_refs):
        out_ref[part] = x_ref[line]


def pick(axis, after, xs):
    return pl.pallas_call(
        functools.partial(pick_kernel, axis),
        out_shape=jax.ShapeDtypeStruct((lax.axis_size("col" if axis == "col" else "row"),) + xs[-1].shape[-2:], xs[-1].dtype),
        in_specs=[pl.BlockSpec(memory_space=pl.ANY)] + [pl.BlockSpec(memory_space=pltpu.VMEM)] * len(xs),
        out_specs=pl.BlockSpec(memory_space=pltpu.VMEM),
        compiler_params=pltpu.CompilerParams(vmem_limit_bytes=4 * 1024 * 1024),
    )(after, *xs)


def seam_of(axis, line):
    count = lax.axis_size(axis)
    height, breadth = lax.axis_size("row"), lax.axis_size("col")
    if axis == "row":
        at = lambda group: (0 if group & 1 else count - 1) * breadth
        ends = [(at(c) + c, at(c) + c + 1) for c in range(breadth - 1)]
    else:
        at = lambda group: 0 if group & 1 else count - 1
        ends = [(at(r) + r * breadth, at(r) + (r + 1) * breadth) for r in range(height - 1)]
    pairs = ends + [(b, a) for a, b in ends]
    return lax.ppermute(line, ("row", "col"), pairs)


def local(
    features,
    norm_gain,
    in_weight,
    conv_weight,
    conv_bias,
    proj_weight,
    step_weight,
    step_bias,
    decay_log,
    skip_gain,
    out_gain,
    out_weight,
):
    height, width, channels = features.shape
    inner = out_weight.shape[0]
    tokens = height * width
    row_lines = height // lax.axis_size("col")
    col_lines = width // lax.axis_size("row")

    rows, cols = lax.axis_size("row"), lax.axis_size("col")
    vmem = pl.BlockSpec(memory_space=pltpu.VMEM)
    normed, *sends = pl.pallas_call(
        functools.partial(cut_kernel, rows),
        out_shape=[jax.ShapeDtypeStruct((tokens, channels), BF16)]
        + [jax.ShapeDtypeStruct((col_lines + 2, height, channels), BF16)] * (rows // 2)
        + [jax.ShapeDtypeStruct((rows // 2, col_lines + 2, height, channels), BF16)]
        + [jax.ShapeDtypeStruct((row_lines + 2, width, channels), BF16)] * cols,
        in_specs=[pl.BlockSpec(features.shape, lambda: (0, 0, 0)), pl.BlockSpec((channels,), lambda: (0,))],
        out_specs=[vmem] * (2 + rows // 2 + cols),
        scratch_shapes=[pltpu.VMEM((tokens, channels), BF16)],
        compiler_params=pltpu.CompilerParams(vmem_limit_bytes=12 * 1024 * 1024),
        cost_estimate=pl.CostEstimate(flops=6_000_000_000, bytes_accessed=2 << 20, transcendentals=tokens),
    )(features, norm_gain)
    weights = (in_weight, conv_weight, conv_bias, proj_weight, step_weight, step_bias, decay_log, skip_gain)
    gate = pl.pallas_call(
        gate_kernel,
        out_shape=jax.ShapeDtypeStruct((tokens, inner), BF16),
        grid=(1,),
        in_specs=[
            pl.BlockSpec((tokens, channels), lambda i: (0, 0)),
            pl.BlockSpec((channels, inner), lambda i: (0, 1)),
        ],
        out_specs=pl.BlockSpec((tokens, inner), lambda i: (0, 0)),
        compiler_params=pltpu.CompilerParams(vmem_limit_bytes=12 * 1024 * 1024),
        cost_estimate=pl.CostEstimate(flops=2 * tokens * channels * inner, bytes_accessed=1 << 20, transcendentals=0),
    )(normed, in_weight)

    half = rows // 2
    row_x = swap_blocks(sends[half + 1 :], "col")
    col_x = swap_out(sends[:half], sends[half])
    row_seam = seam_of("col", pick("col", normed, row_x))
    row_steps = prepare("col", normed, row_x, row_seam, *weights)
    col_seam = seam_of("row", pick("row", row_steps[0], col_x))
    col_steps = prepare("row", row_steps[0], col_x, col_seam, *weights)
    col_y = scan("row", normed, *col_steps, decay_log, skip_gain)
    joined = join("row", col_y, rows, col_lines, height, inner, normed)
    col_y = swap_back_far(joined)
    row_y = scan("col", joined[0], *row_steps, decay_log, skip_gain)
    beside = jax.ShapeDtypeStruct((half,) + joined[0].shape[1:], BF16)
    beside = simple(collect_kernel, beside, *col_y, after=row_y)
    row_y = swap_blocks(join("col", row_y, cols, row_lines, width, inner, beside), "col")
    beside = swap(beside, "row", 1)
    return pl.pallas_call(
        functools.partial(end_kernel, half),
        out_shape=jax.ShapeDtypeStruct(features.shape, BF16),
        scratch_shapes=[pltpu.VMEM((tokens, inner), BF16)],
        compiler_params=pltpu.CompilerParams(vmem_limit_bytes=16 * 1024 * 1024),
    )(gate, out_gain, out_weight, *col_y, beside, *row_y)


def solution(mesh):
    in_specs = (P("row", "col", None), P(), P(), P(), P(), P(), P(), P(), P(), P(), P(), P())
    out_specs = P("row", "col", None)
    return jax.shard_map(local, mesh=mesh, in_specs=in_specs, out_specs=out_specs, check_vma=False)
```

```python
import functools

import jax
import jax.numpy as jnp
from jax import lax
from jax.experimental import pallas as pl
from jax.experimental.pallas import tpu as pltpu
from jax.sharding import PartitionSpec as P

F32 = jnp.float32
BF16 = jnp.bfloat16
LANES = 128
SLOTS = 8
LOG2E = 1.4426950408889634


def bits(value):
    assert value & (value - 1) == 0
    return value.bit_length() - 1


def one_hot(targets, width):
    lane = lax.broadcasted_iota(jnp.int32, targets[0].shape, 1)
    blocks = []
    for block in range(pl.cdiv(width, LANES)):
        hit = targets[0] == lane + block * LANES
        for other in targets[1:]:
            hit = jnp.logical_or(hit, other == lane + block * LANES)
        blocks.append(jnp.where(hit, 1.0, 0.0).astype(BF16))
    return jnp.concatenate(blocks, axis=1)[:, :width]


def rows_of(count, start=0):
    return lax.broadcasted_iota(jnp.int32, (count, LANES), 0) + start


def dot(a, b):
    return jnp.dot(a, b, preferred_element_type=F32)


def layer_norm(values, scale_gain):
    centred = values - jnp.mean(values, axis=-1, keepdims=True)
    spread = jnp.mean(centred * centred, axis=-1, keepdims=True)
    return centred * lax.rsqrt(spread + 1e-05) * scale_gain


def flip(axis):
    other = "col" if axis == "row" else "row"
    return (lax.axis_index(other) & 1) * (lax.axis_size(axis) - 1)


def cut_kernel(columns, feat_ref, gain_ref, norm_ref, *refs):
    col_refs, beside_ref, row_refs, turned_ref = refs[: columns // 2], refs[columns // 2], refs[columns // 2 + 1 : -1], refs[-1]
    height, width, channels = feat_ref.shape
    tile = layer_norm(feat_ref[...].reshape(height * width, channels).astype(F32), gain_ref[...][None]).astype(BF16)
    norm_ref[...] = tile
    reach = row_refs[0].shape[0]
    turn = flip("col") ^ lax.axis_index("col")
    for part, row_ref in enumerate(row_refs):
        for line in range(reach):
            at = (part ^ turn) * reach + line
            row_ref[line] = norm_ref[pl.ds(pl.multiple_of(at * width, width), width)]
    row = rows_of(height * width)
    turned = dot(one_hot([((row & (height - 1)) << bits(width)) + (row >> bits(height))], height * width), tile).astype(
        BF16
    )
    turned_ref[...] = turned
    reach = col_refs[0].shape[0]
    turn = flip("row") ^ lax.axis_index("row")
    for part in range(columns):
        for line in range(reach):
            at = (part ^ turn) * reach + line
            found = turned_ref[pl.ds(pl.multiple_of(at * height, height), height)]
            if part & 1:
                beside_ref[part >> 1, line] = found
            else:
                col_refs[part >> 1][line] = found


def gate_kernel(norm_ref, weight_ref, gate_ref):
    gate_ref[...] = dot(norm_ref[...], weight_ref[...]).astype(BF16)


def views(refs, rank):
    found = []
    for ref in refs:
        found += [ref] if len(ref.shape) == rank else [ref.at[k] for k in range(ref.shape[0])]
    return found


def by_slot(halves, rows):
    found = None
    for kind in range(halves * 2):
        row = rows(kind >> 1, kind & 1)
        row = jnp.broadcast_to(row, (SLOTS, row.shape[1]))
        slot = lax.broadcasted_iota(jnp.int32, row.shape, 0)
        found = row if found is None else jnp.where(slot >= kind * (SLOTS // (halves * 2)), row, found)
    return found


def prepare_kernel(
    lines,
    axis,
    after_ref,
    *refs,
):
    x_refs, refs = views(refs[:-17], 3), refs[-17:]
    (
        before_ref,
        behind_ref,
        weight_ref,
        conv_ref,
        conv_bias_ref,
        proj_raw_ref,
        step_raw_ref,
        bias_raw_ref,
        proj_out_ref,
        s_ref,
        v_ref,
        token_ref,
        inner_ref,
        active_ref,
        proj_ref,
        step_ref,
        bias_ref,
    ) = refs
    ks = (0, 1) if axis == "col" else (2, 3)
    parts, length, channels = before_ref.shape
    reach = lines + 2
    states = (proj_raw_ref.shape[1] - RANK) // 2
    time = parts * length
    low = time // SLOTS
    width = weight_ref.shape[1] // 2
    chunk = s_ref.shape[2]
    halves = width // chunk
    slot_lines = SLOTS // (2 * halves)
    if axis == "row":
        across_first = lambda across, along: (along, across)
    else:
        across_first = lambda across, along: (across, along)

    row = rows_of(time)
    source = ((row & 7) << bits(low)) + (row >> 3)
    orders = [one_hot([source], time), one_hot([source ^ (lax.axis_index(axis) << bits(length))], time)]
    for line in range(reach):
        if 0 < line < reach - 1:
            x = jnp.concatenate([x_ref[line - 1] for x_ref in x_refs], axis=0)
            order = orders[1]
        else:
            x = (behind_ref if line else before_ref)[...].reshape(time, channels)
            order = orders[0]
        token_ref[line * time : (line + 1) * time] = dot(order, x).astype(BF16)
    inner = dot(token_ref[...], weight_ref[:, :width]).astype(BF16).astype(F32)
    inner_ref[:, 1 : low + 1] = inner.reshape(reach, low, SLOTS, width)
    place = lax.broadcasted_iota(jnp.int32, (SLOTS, width), 0)
    for line in range(reach):
        inner_ref[line, 0] = jnp.where(place == 0, 0.0, pltpu.roll(inner_ref[line, low], 1, 0))
        inner_ref[line, low + 1] = jnp.where(place == SLOTS - 1, 0.0, pltpu.roll(inner_ref[line, 1], SLOTS - 1, 0))

    conv_bias = conv_bias_ref[...][None]

    def convolve(pair, _):
        for group in range(width // (2 * LANES)):
            cells = slice(group * 2 * LANES, (group + 1) * 2 * LANES)
            half = (group * 2 * LANES) // chunk
            base = group * 2 * LANES - half * chunk
            bias = jnp.broadcast_to(conv_bias[:, cells], (SLOTS, 2 * LANES))
            totals = [[bias for _ in range(2)] for _ in range(lines)]
            for across in range(3):
                for along in range(3):
                    first, second = across_first(across, along)
                    tap = jnp.broadcast_to(conv_ref[first, second : second + 1, cells], (SLOTS, 2 * LANES))
                    for line in range(lines):
                        for sub in range(2):
                            totals[line][sub] += inner_ref[line + across, 2 * pair + sub + along, :, cells] * tap
            for line in range(lines):
                value = jnp.concatenate(totals[line], axis=0)
                value = 0.5 * value
                value = value * jnp.tanh(value) + value
                value = value.astype(BF16)
                for piece in range(2):
                    at = base + piece * LANES
                    start = ((half + at // chunk) * lines + line) * time
                    start = pl.multiple_of(start + pair * (2 * SLOTS), 2 * SLOTS)
                    active_ref[pl.ds(start, 2 * SLOTS), at % chunk : at % chunk + LANES] = value[
                        :, piece * LANES : (piece + 1) * LANES
                    ]
        return 0

    lax.fori_loop(0, low // 2, convolve, 0)

    bias_ref[...] = by_slot(halves, lambda half, way: bias_raw_ref[ks[way] : ks[way] + 1, half * chunk : (half + 1) * chunk])
    for half in range(halves):
        cells = slice(half * chunk, (half + 1) * chunk)
        for way in range(2):
            kind = slice((half * 2 + way) * LANES, (half * 2 + way + 1) * LANES)
            w = proj_raw_ref[ks[way], :, cells].astype(F32)
            ranks = w[:RANK]
            rest = jnp.zeros((LANES - 3 * RANK - 2 * states, chunk), F32)
            w = jnp.concatenate([ranks, ranks, ranks, w[RANK:], rest], axis=0)
            proj_ref[:, kind] = w.T.astype(BF16)
            w = step_raw_ref[ks[way], :, cells]
            high = w.astype(BF16).astype(F32)
            rest = jnp.zeros((LANES - 3 * RANK, chunk), F32)
            step_ref[kind, :] = jnp.concatenate([high, high, w - high, rest], axis=0).astype(BF16)

    piece = 256
    for first in range(0, time * SLOTS, piece):
        row = rows_of(piece, first)
        now = row >> 3
        slot = row & 7
        line = slot & (slot_lines - 1)
        back = (slot >> bits(slot_lines)) & 1
        half = slot >> bits(2 * slot_lines)
        when = jnp.where(back == 1, time - 1 - now, now)
        source = half * (lines * time) + line * time + ((when & (low - 1)) << 3) + (when >> bits(low))
        if slot_lines > lines:
            source = jnp.where(line < lines, source, -1)
        u = dot(one_hot([source], halves * lines * time), active_ref[...])
        steps = pl.ds(first // SLOTS, piece // SLOTS)
        v_ref[steps] = u.reshape(piece // SLOTS, SLOTS, chunk)
        kind = slot >> bits(slot_lines)
        projected = dot(u.astype(BF16), proj_ref[...])
        p = projected[:, :LANES]
        for other in range(1, 2 * halves):
            p = jnp.where(kind == other, projected[:, other * LANES : (other + 1) * LANES], p)
        if halves == 2:
            p = p.reshape(piece // SLOTS, SLOTS, LANES)
            p = p + pltpu.roll(p, SLOTS // 2, 1)
            p = p.reshape(piece, LANES)
        proj_out_ref[steps] = p.reshape(piece // SLOTS, SLOTS, LANES)
        high = p.astype(BF16).astype(F32)
        lane = lax.broadcasted_iota(jnp.int32, p.shape, 1)
        mixed = jnp.where(jnp.logical_and(lane >= RANK, lane < 2 * RANK), p - high, high)
        stacked = jnp.concatenate([jnp.where(kind == k, mixed, 0.0).astype(BF16) for k in range(2 * halves)], axis=1)
        s_ref[steps] = dot(stacked, step_ref[...]).reshape(piece // SLOTS, SLOTS, chunk)

    def soften(lap, _):
        for sub in range(8):
            t = lap * 8 + sub
            for g in range(chunk // LANES):
                cells = slice(g * LANES, (g + 1) * LANES)
                before = s_ref[t, :, cells] + bias_ref[:, cells]
                small = jnp.exp(-jnp.abs(before))
                log1p = jnp.where(small < 0.001, small - 0.5 * small * small, jnp.log(1.0 + small))
                step = jnp.maximum(before, 0.0) + log1p
                s_ref[t, :, cells] = step
        return 0

    lax.fori_loop(0, time // 8, soften, 0)


def scan_kernel(
    axis,
    after_ref,
    coef_ref,
    s_ref,
    u_ref,
    decay_ref,
    skip_raw_ref,
    out_ref,
    v_ref,
    y_ref,
    spread_ref,
):
    time, _, chunk = s_ref.shape
    halves = decay_ref.shape[2] // chunk
    states = decay_ref.shape[1]
    groups = chunk // LANES
    at_once = max(1, 12 // groups)
    unroll = 16
    laps = time // unroll

    ks = (0, 1) if axis == "col" else (2, 3)
    piece = 32
    row = lax.broadcasted_iota(jnp.int32, (2 * LANES, LANES), 0) & (LANES - 1)
    taken = [jnp.where(row == 3 * RANK + n, 1.0, 0.0).astype(BF16) for n in range(2 * states)]

    def spread(lap, _):
        steps = pl.ds(lap * piece, piece)
        coefs = coef_ref[steps].reshape(piece * SLOTS, LANES)
        high = coefs.astype(BF16)
        both = jnp.concatenate([high, (coefs - high.astype(F32)).astype(BF16)], axis=1)
        for n in range(0, 2 * states, 4):
            found = dot(both, jnp.concatenate(taken[n : n + 4], axis=1))
            for k in range(4):
                spread_ref[steps, n + k] = found[:, k * LANES : (k + 1) * LANES].reshape(piece, SLOTS, LANES)
        return 0

    lax.fori_loop(0, time // piece, spread, 0)
    for first in range(0, states, at_once):
        rates = []
        for n in range(first, first + at_once):
            rates.append([])
            for g in range(groups):
                rate = by_slot(
                    halves,
                    lambda half, way: decay_ref[ks[way], n : n + 1, half * chunk + g * LANES : half * chunk + (g + 1) * LANES],
                )
                rates[-1].append(-LOG2E * jnp.exp(rate))
        if first == 0:
            skips = [
                by_slot(
                    halves,
                    lambda half, way: skip_raw_ref[
                        ks[way] : ks[way] + 1, half * chunk + g * LANES : half * chunk + (g + 1) * LANES
                    ],
                )
                for g in range(groups)
            ]

        def decays(t):
            found = []
            for g in range(groups):
                step = s_ref[t, :, g * LANES : (g + 1) * LANES]
                found.append([jnp.exp2(step * rates[n][g]) for n in range(at_once)])
            return found

        def advance(lap, hidden):
            hidden = list(hidden)
            ahead = decays(lap * unroll) if axis == "col" else None
            for sub in range(unroll):
                t = lap * unroll + sub
                if axis == "col":
                    decay = ahead
                    if sub + 1 < unroll:
                        ahead = decays(t + 1)
                else:
                    decay = decays(t)
                enter = [spread_ref[t, first + n] for n in range(at_once)]
                leave = [spread_ref[t, states + first + n] for n in range(at_once)]
                for g in range(groups):
                    cells = pl.ds(g * LANES, LANES)
                    if first == 0:
                        u = u_ref[t, :, cells]
                        value = s_ref[t, :, cells] * u
                        v_ref[t, :, cells] = value
                        y = skips[g] * u
                    else:
                        value = v_ref[t, :, cells]
                        y = y_ref[t, :, cells]
                    for n in range(at_once):
                        k = n * groups + g
                        h = decay[g][n] * hidden[k] + value * enter[n]
                        hidden[k] = h
                        y = y + h * leave[n]
                    y_ref[t, :, cells] = y
            return tuple(hidden)

        zero = jnp.zeros((SLOTS, LANES), F32)
        lax.fori_loop(0, laps, advance, (zero,) * (at_once * groups))

    out_ref[...] = y_ref[...].reshape(time * SLOTS, chunk).astype(BF16)


def join_kernel(parts, lines, axis, after_ref, scanned_ref, *out_refs):
    length = out_refs[0].shape[-2] // lines
    time = parts * length
    chunk = scanned_ref.shape[1]
    halves = out_refs[0].shape[-1] // chunk
    slot_lines = SLOTS // (2 * halves)
    row = rows_of(lines * time)
    line = (row >> bits(length)) & (lines - 1)
    part = row >> bits(lines * length)
    part = part ^ lax.axis_index(axis)
    now = (part << bits(length)) + (row & (length - 1))
    for half in range(halves):
        ahead = now * SLOTS + (half * 2 * slot_lines) + line
        behind = (time - 1 - now) * SLOTS + (half * 2 * slot_lines + slot_lines) + line
        joined = dot(one_hot([ahead, behind], time * SLOTS), scanned_ref[...]).astype(BF16)
        size = lines * length
        for part in range(parts):
            found = joined[part * size : (part + 1) * size]
            if len(out_refs) < parts:
                out_refs[part >> 1][part & 1, :, half * chunk : (half + 1) * chunk] = found
            else:
                out_refs[part][:, half * chunk : (half + 1) * chunk] = found


def join(axis, scanned, parts, lines, length, width, after):
    size = (lines * length, width)
    shapes = [size] * parts if axis == "col" else [(2,) + size] * (parts // 2)
    return pl.pallas_call(
        functools.partial(join_kernel, parts, lines, axis),
        out_shape=[jax.ShapeDtypeStruct(shape, BF16) for shape in shapes],
        in_specs=[pl.BlockSpec(memory_space=pl.ANY), pl.BlockSpec(memory_space=pltpu.VMEM)],
        out_specs=[pl.BlockSpec(memory_space=pltpu.VMEM)] * len(shapes),
        compiler_params=pltpu.CompilerParams(vmem_limit_bytes=24 * 1024 * 1024),
    )(after, scanned)


RANK = 24


def prepare(axis, after, xs, seams, in_weight, conv, conv_bias, proj, step_weight, step_bias, decay_log, skip):
    parts, length, channels = seams[0].shape
    lines = xs[0].shape[-3]
    reach = lines + 2
    time = parts * length
    width = conv.shape[2]
    states = decay_log.shape[2]
    assert step_weight.shape[1] == RANK and in_weight.shape[1] == 2 * width
    halves = 1 if lines >= 4 else 2
    assert lines <= SLOTS // (2 * halves)
    chunk = width // halves
    vmem = pl.BlockSpec(memory_space=pltpu.VMEM)
    flops = 2 * time * (reach * channels * width + SLOTS * width * 256)
    return pl.pallas_call(
        functools.partial(prepare_kernel, lines, axis),
        out_shape=[
            jax.ShapeDtypeStruct((time, SLOTS, LANES), F32),
            jax.ShapeDtypeStruct((time, SLOTS, chunk), F32),
            jax.ShapeDtypeStruct((time, SLOTS, chunk), F32),
        ],
        in_specs=[pl.BlockSpec(memory_space=pl.ANY)] + [vmem] * (len(xs) + 8),
        out_specs=[vmem, vmem, vmem],
        scratch_shapes=[
            pltpu.VMEM((reach * time, channels), BF16),
            pltpu.VMEM((reach, time // SLOTS + 2, SLOTS, width), F32),
            pltpu.VMEM((halves * lines * time, chunk), BF16),
            pltpu.VMEM((chunk, halves * 2 * LANES), BF16),
            pltpu.VMEM((halves * 2 * LANES, chunk), BF16),
            pltpu.VMEM((SLOTS, chunk), F32),
        ],
        compiler_params=pltpu.CompilerParams(vmem_limit_bytes=24 * 1024 * 1024),
        cost_estimate=pl.CostEstimate(flops=4 * flops, bytes_accessed=4 * 1024 * 1024, transcendentals=time * SLOTS * chunk),
    )(
        after,
        *xs,
        *seams,
        in_weight,
        conv,
        conv_bias,
        jnp.swapaxes(proj, 1, 2),
        step_weight,
        step_bias,
    )


def scan(axis, after, coefs, steps, u, decay_log, skip):
    time, _, chunk = steps.shape
    width, states = decay_log.shape[1:]
    vmem = pl.BlockSpec(memory_space=pltpu.VMEM)
    return pl.pallas_call(
        functools.partial(scan_kernel, axis),
        out_shape=jax.ShapeDtypeStruct((time * SLOTS, chunk), BF16),
        in_specs=[pl.BlockSpec(memory_space=pl.ANY), vmem, vmem, vmem, vmem, vmem],
        out_specs=vmem,
        scratch_shapes=[
            pltpu.VMEM((time, SLOTS, chunk), F32),
            pltpu.VMEM((time, SLOTS, chunk), F32),
            pltpu.VMEM((time, 2 * states, SLOTS, LANES), F32),
        ],
        compiler_params=pltpu.CompilerParams(vmem_limit_bytes=(8 << 20) + time * (136 << 10) + time * 20 * chunk),
        cost_estimate=pl.CostEstimate(
            flops=8 * time * SLOTS * chunk * states,
            bytes_accessed=4 * 1024 * 1024,
            transcendentals=time * SLOTS * chunk * states,
        ),
    )(after, coefs, steps, u, jnp.swapaxes(decay_log, 1, 2), skip)


def end_kernel(columns, gate_ref, gain_ref, weight_ref, *refs):
    pair_refs, beside_ref, row_refs, out_ref, gated_ref = refs[:columns], refs[columns], refs[columns + 1 : -2], refs[-2], refs[-1]
    height, width, channels = out_ref.shape
    size = row_refs[0].shape[0]
    lines = size // width
    swap = flip("col") ^ lax.axis_index("col")
    turn = (flip("row") ^ lax.axis_index("row")) * (width // lax.axis_size("row"))
    row = rows_of(height * width)
    line = (row >> bits(width)) ^ (swap * lines)
    source = (((row & (width - 1)) ^ turn) << bits(height)) + line
    rows = jnp.concatenate([row_ref[...] for row_ref in row_refs], axis=0)
    blocks = []
    for part in range(columns):
        blocks += [pair_refs[part][0], beside_ref[part]]
    columns = jnp.concatenate(blocks, axis=0)
    combined = layer_norm(rows.astype(F32) + dot(one_hot([source], height * width), columns), gain_ref[...][None])
    for part in range(len(row_refs)):
        cells = pl.ds(pl.multiple_of((part ^ swap) * size, size), size)
        gate = gate_ref[cells].astype(F32)
        gated_ref[cells] = (combined[part * size : (part + 1) * size] * (gate / (1.0 + jnp.exp(-gate)))).astype(BF16)
    out = dot(gated_ref[...], weight_ref[...]).astype(BF16)
    out_ref[...] = out.reshape(height, width, channels)


def pair_kernel(*refs):
    count = len(refs) // 2
    own_refs, beside_ref, out_refs = refs[:count], refs[count], refs[count + 1 :]
    for k in range(count):
        out_refs[k][0] = own_refs[k][...]
        out_refs[k][1] = beside_ref[k + 1]


def first_kernel(own_ref, beside_ref, out_ref):
    out_ref[0] = own_ref[...]
    out_ref[1] = beside_ref[0]


def collect_kernel(after_ref, *refs):
    out_ref = refs[-1]
    for k in range(len(refs) - 1):
        out_ref[k] = refs[k][1]


def simple(kernel, shapes, *arrays, after=None):
    vmem = pl.BlockSpec(memory_space=pltpu.VMEM)
    first = [] if after is None else [after]
    many = isinstance(shapes, list)
    return pl.pallas_call(
        kernel,
        out_shape=shapes,
        in_specs=[pl.BlockSpec(memory_space=pl.ANY)] * len(first) + [vmem] * len(arrays),
        out_specs=[vmem] * len(shapes) if many else vmem,
        compiler_params=pltpu.CompilerParams(vmem_limit_bytes=4 * 1024 * 1024),
        cost_estimate=pl.CostEstimate(flops=0, bytes_accessed=2 << 20, transcendentals=0),
    )(*first, *arrays)


def swap(block, axis, k):
    return lax.ppermute(block, axis, [(i, i ^ k) for i in range(lax.axis_size(axis))])


def swap_out(own, beside):
    beside = swap(beside, "row", 1)
    shape = jax.ShapeDtypeStruct((2,) + own[0].shape, own[0].dtype)
    pairs = simple(pair_kernel, [shape] * (len(own) - 1), *own[1:], beside)
    found = {k: swap(pairs[k - 1], "row", 2 * k) for k in range(len(own) - 1, 0, -1)}
    first = simple(first_kernel, jax.ShapeDtypeStruct((2,) + own[0].shape, own[0].dtype), own[0], beside)
    return [first] + [found[k] for k in range(1, len(own))]


def swap_back_far(pairs):
    found = {k: swap(pairs[k], "row", 2 * k) for k in range(len(pairs) - 1, 0, -1)}
    return [pairs[0]] + [found[k] for k in range(1, len(pairs))]


def swap_blocks(blocks, axis):
    count = lax.axis_size(axis)
    found = {k: lax.ppermute(blocks[k], axis, [(i, i ^ k) for i in range(count)]) for k in range(count - 1, 0, -1)}
    return [blocks[0]] + [found[k] for k in range(1, count)]


def pick_kernel(axis, after_ref, *refs):
    x_refs, first_ref, last_ref = views(refs[:-2], 3), refs[-2], refs[-1]
    place = lax.axis_index(axis)
    for k, x_ref in enumerate(x_refs):
        first_ref[k ^ place] = x_ref[0]
        last_ref[k ^ place] = x_ref[x_ref.shape[0] - 1]


def seams_of(axis, after, xs):
    shape = jax.ShapeDtypeStruct((lax.axis_size(axis),) + xs[-1].shape[-2:], xs[-1].dtype)
    vmem = pl.BlockSpec(memory_space=pltpu.VMEM)
    first, last = pl.pallas_call(
        functools.partial(pick_kernel, axis),
        out_shape=[shape, shape],
        in_specs=[pl.BlockSpec(memory_space=pl.ANY)] + [vmem] * len(xs),
        out_specs=[vmem, vmem],
        compiler_params=pltpu.CompilerParams(vmem_limit_bytes=4 * 1024 * 1024),
    )(after, *xs)
    height, breadth = lax.axis_size("row"), lax.axis_size("col")
    chain = []
    if axis == "row":
        for c in range(breadth):
            chain += [r * breadth + c for r in (range(height - 1, -1, -1) if c & 1 else range(height))]
    else:
        for r in range(height):
            chain += [r * breadth + c for c in (range(breadth - 1, -1, -1) if r & 1 else range(breadth))]
    ahead = list(zip(chain[:-1], chain[1:]))
    both = ("row", "col")
    return lax.ppermute(last, both, ahead), lax.ppermute(first, both, [(b, a) for a, b in ahead])


def local(
    features,
    norm_gain,
    in_weight,
    conv_weight,
    conv_bias,
    proj_weight,
    step_weight,
    step_bias,
    decay_log,
    skip_gain,
    out_gain,
    out_weight,
):
    height, width, channels = features.shape
    inner = out_weight.shape[0]
    tokens = height * width
    row_lines = height // lax.axis_size("col")
    col_lines = width // lax.axis_size("row")

    rows, cols = lax.axis_size("row"), lax.axis_size("col")
    vmem = pl.BlockSpec(memory_space=pltpu.VMEM)
    normed, *sends = pl.pallas_call(
        functools.partial(cut_kernel, rows),
        out_shape=[jax.ShapeDtypeStruct((tokens, channels), BF16)]
        + [jax.ShapeDtypeStruct((col_lines, height, channels), BF16)] * (rows // 2)
        + [jax.ShapeDtypeStruct((rows // 2, col_lines, height, channels), BF16)]
        + [jax.ShapeDtypeStruct((row_lines, width, channels), BF16)] * cols,
        in_specs=[pl.BlockSpec(features.shape, lambda: (0, 0, 0)), pl.BlockSpec((channels,), lambda: (0,))],
        out_specs=[vmem] * (2 + rows // 2 + cols),
        scratch_shapes=[pltpu.VMEM((tokens, channels), BF16)],
        compiler_params=pltpu.CompilerParams(vmem_limit_bytes=12 * 1024 * 1024),
        cost_estimate=pl.CostEstimate(flops=6_000_000_000, bytes_accessed=2 << 20, transcendentals=tokens),
    )(features, norm_gain)
    weights = (in_weight, conv_weight, conv_bias, proj_weight, step_weight, step_bias, decay_log, skip_gain)
    gate = pl.pallas_call(
        gate_kernel,
        out_shape=jax.ShapeDtypeStruct((tokens, inner), BF16),
        grid=(1,),
        in_specs=[
            pl.BlockSpec((tokens, channels), lambda i: (0, 0)),
            pl.BlockSpec((channels, inner), lambda i: (0, 1)),
        ],
        out_specs=pl.BlockSpec((tokens, inner), lambda i: (0, 0)),
        compiler_params=pltpu.CompilerParams(vmem_limit_bytes=12 * 1024 * 1024),
        cost_estimate=pl.CostEstimate(flops=2 * tokens * channels * inner, bytes_accessed=1 << 20, transcendentals=0),
    )(normed, in_weight)

    half = rows // 2
    row_x = swap_blocks(sends[half + 1 :], "col")
    col_x = swap_out(sends[:half], sends[half])
    row_steps = prepare("col", normed, row_x, seams_of("col", normed, row_x), *weights)
    col_steps = prepare("row", row_steps[0], col_x, seams_of("row", row_steps[0], col_x), *weights)
    col_y = scan("row", normed, *col_steps, decay_log, skip_gain)
    joined = join("row", col_y, rows, col_lines, height, inner, normed)
    col_y = swap_back_far(joined)
    row_y = scan("col", joined[0], *row_steps, decay_log, skip_gain)
    beside = jax.ShapeDtypeStruct((half,) + joined[0].shape[1:], BF16)
    beside = simple(collect_kernel, beside, *col_y, after=row_y)
    row_y = swap_blocks(join("col", row_y, cols, row_lines, width, inner, beside), "col")
    beside = swap(beside, "row", 1)
    return pl.pallas_call(
        functools.partial(end_kernel, half),
        out_shape=jax.ShapeDtypeStruct(features.shape, BF16),
        scratch_shapes=[pltpu.VMEM((tokens, inner), BF16)],
        compiler_params=pltpu.CompilerParams(vmem_limit_bytes=16 * 1024 * 1024),
    )(gate, out_gain, out_weight, *col_y, beside, *row_y)


def solution(mesh):
    in_specs = (P("row", "col", None), P(), P(), P(), P(), P(), P(), P(), P(), P(), P(), P())
    out_specs = P("row", "col", None)
    return jax.shard_map(local, mesh=mesh, in_specs=in_specs, out_specs=out_specs, check_vma=False)
```

```python
import functools

import jax
import jax.numpy as jnp
from jax import lax
from jax.experimental import pallas as pl
from jax.experimental.pallas import tpu as pltpu
from jax.sharding import PartitionSpec as P

F32 = jnp.float32
BF16 = jnp.bfloat16
LANES = 128
SLOTS = 8
LOG2E = 1.4426950408889634


def bits(value):
    assert value & (value - 1) == 0
    return value.bit_length() - 1


def one_hot(targets, width):
    lane = lax.broadcasted_iota(jnp.int32, targets[0].shape, 1)
    blocks = []
    for block in range(pl.cdiv(width, LANES)):
        hit = targets[0] == lane + block * LANES
        for other in targets[1:]:
            hit = jnp.logical_or(hit, other == lane + block * LANES)
        blocks.append(jnp.where(hit, 1.0, 0.0).astype(BF16))
    return jnp.concatenate(blocks, axis=1)[:, :width]


def rows_of(count, start=0):
    return lax.broadcasted_iota(jnp.int32, (count, LANES), 0) + start


def dot(a, b):
    return jnp.dot(a, b, preferred_element_type=F32)


def layer_norm(values, scale_gain):
    centred = values - jnp.mean(values, axis=-1, keepdims=True)
    spread = jnp.mean(centred * centred, axis=-1, keepdims=True)
    return centred * lax.rsqrt(spread + 1e-05) * scale_gain


def flip(axis):
    other = "col" if axis == "row" else "row"
    return (lax.axis_index(other) & 1) * (lax.axis_size(axis) - 1)


def cut_kernel(columns, feat_ref, gain_ref, norm_ref, *refs):
    col_refs, beside_ref, row_refs, turned_ref = refs[: columns // 2], refs[columns // 2], refs[columns // 2 + 1 : -1], refs[-1]
    height, width, channels = feat_ref.shape
    tile = layer_norm(feat_ref[...].reshape(height * width, channels).astype(F32), gain_ref[...][None]).astype(BF16)
    norm_ref[...] = tile
    reach = row_refs[0].shape[0]
    turn = flip("col") ^ lax.axis_index("col")
    for part, row_ref in enumerate(row_refs):
        for line in range(reach):
            at = jnp.clip((part ^ turn) * (reach - 2) + line - 1, 0, height - 1)
            row_ref[line] = norm_ref[pl.ds(pl.multiple_of(at * width, width), width)]
    row = rows_of(height * width)
    turned = dot(one_hot([((row & (height - 1)) << bits(width)) + (row >> bits(height))], height * width), tile).astype(
        BF16
    )
    turned_ref[...] = turned
    reach = col_refs[0].shape[0]
    turn = flip("row") ^ lax.axis_index("row")
    for part in range(columns):
        for line in range(reach):
            at = jnp.clip((part ^ turn) * (reach - 2) + line - 1, 0, width - 1)
            found = turned_ref[pl.ds(pl.multiple_of(at * height, height), height)]
            if part & 1:
                beside_ref[part >> 1, line] = found
            else:
                col_refs[part >> 1][line] = found


def gate_kernel(norm_ref, weight_ref, gate_ref):
    gate_ref[...] = dot(norm_ref[...], weight_ref[...]).astype(BF16)


def views(refs, rank):
    found = []
    for ref in refs:
        found += [ref] if len(ref.shape) == rank else [ref.at[k] for k in range(ref.shape[0])]
    return found


def by_slot(halves, rows):
    found = None
    for kind in range(halves * 2):
        row = rows(kind >> 1, kind & 1)
        row = jnp.broadcast_to(row, (SLOTS, row.shape[1]))
        slot = lax.broadcasted_iota(jnp.int32, row.shape, 0)
        found = row if found is None else jnp.where(slot >= kind * (SLOTS // (halves * 2)), row, found)
    return found


def prepare_kernel(
    lines,
    axis,
    after_ref,
    *refs,
):
    x_refs, refs = views(refs[:-16], 3), refs[-16:]
    (
        seam_ref,
        weight_ref,
        conv_ref,
        conv_bias_ref,
        proj_raw_ref,
        step_raw_ref,
        bias_raw_ref,
        proj_out_ref,
        s_ref,
        v_ref,
        token_ref,
        inner_ref,
        active_ref,
        proj_ref,
        step_ref,
        bias_ref,
    ) = refs
    ks = (0, 1) if axis == "col" else (2, 3)
    parts, length, channels = seam_ref.shape
    reach = lines + 2
    states = (proj_raw_ref.shape[1] - RANK) // 2
    time = parts * length
    low = time // SLOTS
    width = weight_ref.shape[1] // 2
    chunk = s_ref.shape[2]
    halves = width // chunk
    slot_lines = SLOTS // (2 * halves)
    if axis == "row":
        across_first = lambda across, along: (along, across)
    else:
        across_first = lambda across, along: (across, along)

    row = rows_of(time)
    source = ((row & 7) << bits(low)) + (row >> 3)
    source = source ^ (lax.axis_index(axis) << bits(length))
    order = one_hot([source], time)
    for line in range(reach):
        x = jnp.concatenate([x_ref[line] for x_ref in x_refs], axis=0)
        if line == 0 or line == reach - 1:
            place = lax.axis_index(axis) ^ flip(axis)
            missing = place == (0 if line == 0 else lax.axis_size(axis) - 1)
            x = jnp.where(missing, seam_ref[...].reshape(time, channels), x)
        token_ref[line * time : (line + 1) * time] = dot(order, x).astype(BF16)
    inner = dot(token_ref[...], weight_ref[:, :width]).astype(BF16).astype(F32)
    inner_ref[:, 1 : low + 1] = inner.reshape(reach, low, SLOTS, width)
    place = lax.broadcasted_iota(jnp.int32, (SLOTS, width), 0)
    for line in range(reach):
        inner_ref[line, 0] = jnp.where(place == 0, 0.0, pltpu.roll(inner_ref[line, low], 1, 0))
        inner_ref[line, low + 1] = jnp.where(place == SLOTS - 1, 0.0, pltpu.roll(inner_ref[line, 1], SLOTS - 1, 0))

    conv_bias = conv_bias_ref[...][None]

    def convolve(pair, _):
        for group in range(width // (2 * LANES)):
            cells = slice(group * 2 * LANES, (group + 1) * 2 * LANES)
            half = (group * 2 * LANES) // chunk
            base = group * 2 * LANES - half * chunk
            bias = jnp.broadcast_to(conv_bias[:, cells], (SLOTS, 2 * LANES))
            totals = [[bias for _ in range(2)] for _ in range(lines)]
            for across in range(3):
                for along in range(3):
                    first, second = across_first(across, along)
                    tap = jnp.broadcast_to(conv_ref[first, second : second + 1, cells], (SLOTS, 2 * LANES))
                    for line in range(lines):
                        for sub in range(2):
                            totals[line][sub] += inner_ref[line + across, 2 * pair + sub + along, :, cells] * tap
            for line in range(lines):
                value = jnp.concatenate(totals[line], axis=0)
                value = 0.5 * value
                value = value * jnp.tanh(value) + value
                value = value.astype(BF16)
                for piece in range(2):
                    at = base + piece * LANES
                    start = ((half + at // chunk) * lines + line) * time
                    start = pl.multiple_of(start + pair * (2 * SLOTS), 2 * SLOTS)
                    active_ref[pl.ds(start, 2 * SLOTS), at % chunk : at % chunk + LANES] = value[
                        :, piece * LANES : (piece + 1) * LANES
                    ]
        return 0

    lax.fori_loop(0, low // 2, convolve, 0)

    bias_ref[...] = by_slot(halves, lambda half, way: bias_raw_ref[ks[way] : ks[way] + 1, half * chunk : (half + 1) * chunk])
    for half in range(halves):
        cells = slice(half * chunk, (half + 1) * chunk)
        for way in range(2):
            kind = slice((half * 2 + way) * LANES, (half * 2 + way + 1) * LANES)
            w = proj_raw_ref[ks[way], :, cells].astype(F32)
            ranks = w[:RANK]
            rest = jnp.zeros((LANES - 3 * RANK - 2 * states, chunk), F32)
            w = jnp.concatenate([ranks, ranks, ranks, w[RANK:], rest], axis=0)
            proj_ref[:, kind] = w.T.astype(BF16)
            w = step_raw_ref[ks[way], :, cells]
            high = w.astype(BF16).astype(F32)
            rest = jnp.zeros((LANES - 3 * RANK, chunk), F32)
            step_ref[kind, :] = jnp.concatenate([high, high, w - high, rest], axis=0).astype(BF16)

    piece = 512
    for first in range(0, time * SLOTS, piece):
        row = rows_of(piece, first)
        now = row >> 3
        slot = row & 7
        line = slot & (slot_lines - 1)
        back = (slot >> bits(slot_lines)) & 1
        half = slot >> bits(2 * slot_lines)
        when = jnp.where(back == 1, time - 1 - now, now)
        source = half * (lines * time) + line * time + ((when & (low - 1)) << 3) + (when >> bits(low))
        if slot_lines > lines:
            source = jnp.where(line < lines, source, -1)
        u = dot(one_hot([source], halves * lines * time), active_ref[...])
        steps = pl.ds(first // SLOTS, piece // SLOTS)
        v_ref[steps] = u.reshape(piece // SLOTS, SLOTS, chunk)
        kind = slot >> bits(slot_lines)
        projected = dot(u.astype(BF16), proj_ref[...])
        p = projected[:, :LANES]
        for other in range(1, 2 * halves):
            p = jnp.where(kind == other, projected[:, other * LANES : (other + 1) * LANES], p)
        if halves == 2:
            p = p.reshape(piece // SLOTS, SLOTS, LANES)
            p = p + pltpu.roll(p, SLOTS // 2, 1)
            p = p.reshape(piece, LANES)
        proj_out_ref[steps] = p.reshape(piece // SLOTS, SLOTS, LANES)
        high = p.astype(BF16).astype(F32)
        lane = lax.broadcasted_iota(jnp.int32, p.shape, 1)
        mixed = jnp.where(jnp.logical_and(lane >= RANK, lane < 2 * RANK), p - high, high)
        stacked = jnp.concatenate([jnp.where(kind == k, mixed, 0.0).astype(BF16) for k in range(2 * halves)], axis=1)
        s_ref[steps] = dot(stacked, step_ref[...]).reshape(piece // SLOTS, SLOTS, chunk)

    def soften(lap, _):
        for sub in range(8):
            t = lap * 8 + sub
            for g in range(chunk // LANES):
                cells = slice(g * LANES, (g + 1) * LANES)
                before = s_ref[t, :, cells] + bias_ref[:, cells]
                small = jnp.exp(-jnp.abs(before))
                log1p = jnp.where(small < 0.001, small - 0.5 * small * small, jnp.log(1.0 + small))
                step = jnp.maximum(before, 0.0) + log1p
                s_ref[t, :, cells] = step
        return 0

    lax.fori_loop(0, time // 8, soften, 0)


def scan_kernel(
    axis,
    after_ref,
    coef_ref,
    s_ref,
    u_ref,
    decay_ref,
    skip_raw_ref,
    out_ref,
    v_ref,
    y_ref,
    spread_ref,
):
    time, _, chunk = s_ref.shape
    halves = decay_ref.shape[2] // chunk
    states = decay_ref.shape[1]
    groups = chunk // LANES
    at_once = 4
    unroll = 16 if axis == "col" else 32
    laps = time // unroll

    ks = (0, 1) if axis == "col" else (2, 3)
    piece = 64
    row = lax.broadcasted_iota(jnp.int32, (2 * LANES, LANES), 0) & (LANES - 1)
    taken = [jnp.where(row == 3 * RANK + n, 1.0, 0.0).astype(BF16) for n in range(2 * states)]

    def spread(lap, _):
        steps = pl.ds(lap * piece, piece)
        coefs = coef_ref[steps].reshape(piece * SLOTS, LANES)
        high = coefs.astype(BF16)
        both = jnp.concatenate([high, (coefs - high.astype(F32)).astype(BF16)], axis=1)
        for n in range(0, 2 * states, 4):
            found = dot(both, jnp.concatenate(taken[n : n + 4], axis=1))
            for k in range(4):
                spread_ref[steps, n + k] = found[:, k * LANES : (k + 1) * LANES].reshape(piece, SLOTS, LANES)
        return 0

    lax.fori_loop(0, time // piece, spread, 0)
    for first in range(0, states, at_once):
        rates = []
        for n in range(first, first + at_once):
            rates.append([])
            for g in range(groups):
                rate = by_slot(
                    halves,
                    lambda half, way: decay_ref[ks[way], n : n + 1, half * chunk + g * LANES : half * chunk + (g + 1) * LANES],
                )
                rates[-1].append(-LOG2E * jnp.exp(rate))
        if first == 0:
            skips = [
                by_slot(
                    halves,
                    lambda half, way: skip_raw_ref[
                        ks[way] : ks[way] + 1, half * chunk + g * LANES : half * chunk + (g + 1) * LANES
                    ],
                )
                for g in range(groups)
            ]

        def advance(lap, hidden):
            hidden = list(hidden)
            for sub in range(unroll):
                t = lap * unroll + sub
                enter = [spread_ref[t, first + n] for n in range(at_once)]
                leave = [spread_ref[t, states + first + n] for n in range(at_once)]
                decay = []
                for g in range(groups):
                    step = s_ref[t, :, g * LANES : (g + 1) * LANES]
                    decay.append([jnp.exp2(step * rates[n][g]) for n in range(at_once)])
                for g in range(groups):
                    cells = pl.ds(g * LANES, LANES)
                    if first == 0:
                        u = u_ref[t, :, cells]
                        value = s_ref[t, :, cells] * u
                        v_ref[t, :, cells] = value
                        y = skips[g] * u
                    else:
                        value = v_ref[t, :, cells]
                        y = y_ref[t, :, cells]
                    for n in range(at_once):
                        k = n * groups + g
                        h = decay[g][n] * hidden[k] + value * enter[n]
                        hidden[k] = h
                        y = y + h * leave[n]
                    y_ref[t, :, cells] = y
            return tuple(hidden)

        zero = jnp.zeros((SLOTS, LANES), F32)
        lax.fori_loop(0, laps, advance, (zero,) * (at_once * groups))

    out_ref[...] = y_ref[...].reshape(time * SLOTS, chunk).astype(BF16)


def join_kernel(parts, lines, axis, after_ref, scanned_ref, *out_refs):
    length = out_refs[0].shape[-2] // lines
    time = parts * length
    chunk = scanned_ref.shape[1]
    halves = out_refs[0].shape[-1] // chunk
    slot_lines = SLOTS // (2 * halves)
    row = rows_of(lines * time)
    line = (row >> bits(length)) & (lines - 1)
    part = row >> bits(lines * length)
    part = part ^ lax.axis_index(axis)
    now = (part << bits(length)) + (row & (length - 1))
    for half in range(halves):
        ahead = now * SLOTS + (half * 2 * slot_lines) + line
        behind = (time - 1 - now) * SLOTS + (half * 2 * slot_lines + slot_lines) + line
        joined = dot(one_hot([ahead, behind], time * SLOTS), scanned_ref[...]).astype(BF16)
        size = lines * length
        for part in range(parts):
            found = joined[part * size : (part + 1) * size]
            if len(out_refs) < parts:
                out_refs[part >> 1][part & 1, :, half * chunk : (half + 1) * chunk] = found
            else:
                out_refs[part][:, half * chunk : (half + 1) * chunk] = found


def join(axis, scanned, parts, lines, length, width, after):
    size = (lines * length, width)
    shapes = [size] * parts if axis == "col" else [(2,) + size] * (parts // 2)
    return pl.pallas_call(
        functools.partial(join_kernel, parts, lines, axis),
        out_shape=[jax.ShapeDtypeStruct(shape, BF16) for shape in shapes],
        in_specs=[pl.BlockSpec(memory_space=pl.ANY), pl.BlockSpec(memory_space=pltpu.VMEM)],
        out_specs=[pl.BlockSpec(memory_space=pltpu.VMEM)] * len(shapes),
        compiler_params=pltpu.CompilerParams(vmem_limit_bytes=24 * 1024 * 1024),
    )(after, scanned)


RANK = 24


def prepare(axis, after, xs, seam, in_weight, conv, conv_bias, proj, step_weight, step_bias, decay_log, skip):
    parts, length, channels = seam.shape
    reach = xs[0].shape[-3]
    lines = reach - 2
    time = parts * length
    width = conv.shape[2]
    states = decay_log.shape[2]
    assert step_weight.shape[1] == RANK and in_weight.shape[1] == 2 * width
    halves = 1 if lines >= 4 else 2
    assert lines <= SLOTS // (2 * halves)
    chunk = width // halves
    vmem = pl.BlockSpec(memory_space=pltpu.VMEM)
    flops = 2 * time * (reach * channels * width + SLOTS * width * 256)
    return pl.pallas_call(
        functools.partial(prepare_kernel, lines, axis),
        out_shape=[
            jax.ShapeDtypeStruct((time, SLOTS, LANES), F32),
            jax.ShapeDtypeStruct((time, SLOTS, chunk), F32),
            jax.ShapeDtypeStruct((time, SLOTS, chunk), F32),
        ],
        in_specs=[pl.BlockSpec(memory_space=pl.ANY)] + [vmem] * (len(xs) + 7),
        out_specs=[vmem, vmem, vmem],
        scratch_shapes=[
            pltpu.VMEM((reach * time, channels), BF16),
            pltpu.VMEM((reach, time // SLOTS + 2, SLOTS, width), F32),
            pltpu.VMEM((halves * lines * time, chunk), BF16),
            pltpu.VMEM((chunk, halves * 2 * LANES), BF16),
            pltpu.VMEM((halves * 2 * LANES, chunk), BF16),
            pltpu.VMEM((SLOTS, chunk), F32),
        ],
        compiler_params=pltpu.CompilerParams(vmem_limit_bytes=24 * 1024 * 1024),
        cost_estimate=pl.CostEstimate(flops=4 * flops, bytes_accessed=4 * 1024 * 1024, transcendentals=time * SLOTS * chunk),
    )(
        after,
        *xs,
        seam,
        in_weight,
        conv,
        conv_bias,
        jnp.swapaxes(proj, 1, 2),
        step_weight,
        step_bias,
    )


def scan(axis, after, coefs, steps, u, decay_log, skip):
    time, _, chunk = steps.shape
    width, states = decay_log.shape[1:]
    vmem = pl.BlockSpec(memory_space=pltpu.VMEM)
    return pl.pallas_call(
        functools.partial(scan_kernel, axis),
        out_shape=jax.ShapeDtypeStruct((time * SLOTS, chunk), BF16),
        in_specs=[pl.BlockSpec(memory_space=pl.ANY), vmem, vmem, vmem, vmem, vmem],
        out_specs=vmem,
        scratch_shapes=[
            pltpu.VMEM((time, SLOTS, chunk), F32),
            pltpu.VMEM((time, SLOTS, chunk), F32),
            pltpu.VMEM((time, 2 * states, SLOTS, LANES), F32),
        ],
        compiler_params=pltpu.CompilerParams(vmem_limit_bytes=(8 << 20) + time * (136 << 10) + time * 20 * chunk),
        cost_estimate=pl.CostEstimate(
            flops=8 * time * SLOTS * chunk * states,
            bytes_accessed=4 * 1024 * 1024,
            transcendentals=time * SLOTS * chunk * states,
        ),
    )(after, coefs, steps, u, jnp.swapaxes(decay_log, 1, 2), skip)


def end_kernel(columns, gate_ref, gain_ref, weight_ref, *refs):
    pair_refs, beside_ref, row_refs, out_ref, gated_ref = refs[:columns], refs[columns], refs[columns + 1 : -2], refs[-2], refs[-1]
    height, width, channels = out_ref.shape
    size = row_refs[0].shape[0]
    lines = size // width
    swap = flip("col") ^ lax.axis_index("col")
    turn = (flip("row") ^ lax.axis_index("row")) * (width // lax.axis_size("row"))
    row = rows_of(height * width)
    line = (row >> bits(width)) ^ (swap * lines)
    source = (((row & (width - 1)) ^ turn) << bits(height)) + line
    rows = jnp.concatenate([row_ref[...] for row_ref in row_refs], axis=0)
    blocks = []
    for part in range(columns):
        blocks += [pair_refs[part][0], beside_ref[part]]
    columns = jnp.concatenate(blocks, axis=0)
    combined = layer_norm(rows.astype(F32) + dot(one_hot([source], height * width), columns), gain_ref[...][None])
    for part in range(len(row_refs)):
        cells = pl.ds(pl.multiple_of((part ^ swap) * size, size), size)
        gate = gate_ref[cells].astype(F32)
        gated_ref[cells] = (combined[part * size : (part + 1) * size] * (gate / (1.0 + jnp.exp(-gate)))).astype(BF16)
    out = dot(gated_ref[...], weight_ref[...]).astype(BF16)
    out_ref[...] = out.reshape(height, width, channels)


def pair_kernel(*refs):
    count = len(refs) // 2
    own_refs, beside_ref, out_refs = refs[:count], refs[count], refs[count + 1 :]
    for k in range(count):
        out_refs[k][0] = own_refs[k][...]
        out_refs[k][1] = beside_ref[k + 1]


def first_kernel(own_ref, beside_ref, out_ref):
    out_ref[0] = own_ref[...]
    out_ref[1] = beside_ref[0]


def collect_kernel(after_ref, *refs):
    out_ref = refs[-1]
    for k in range(len(refs) - 1):
        out_ref[k] = refs[k][1]


def simple(kernel, shapes, *arrays, after=None):
    vmem = pl.BlockSpec(memory_space=pltpu.VMEM)
    first = [] if after is None else [after]
    many = isinstance(shapes, list)
    return pl.pallas_call(
        kernel,
        out_shape=shapes,
        in_specs=[pl.BlockSpec(memory_space=pl.ANY)] * len(first) + [vmem] * len(arrays),
        out_specs=[vmem] * len(shapes) if many else vmem,
        compiler_params=pltpu.CompilerParams(vmem_limit_bytes=4 * 1024 * 1024),
        cost_estimate=pl.CostEstimate(flops=0, bytes_accessed=2 << 20, transcendentals=0),
    )(*first, *arrays)


def swap(block, axis, k):
    return lax.ppermute(block, axis, [(i, i ^ k) for i in range(lax.axis_size(axis))])


def swap_out(own, beside):
    beside = swap(beside, "row", 1)
    shape = jax.ShapeDtypeStruct((2,) + own[0].shape, own[0].dtype)
    pairs = simple(pair_kernel, [shape] * (len(own) - 1), *own[1:], beside)
    found = {k: swap(pairs[k - 1], "row", 2 * k) for k in range(len(own) - 1, 0, -1)}
    first = simple(first_kernel, jax.ShapeDtypeStruct((2,) + own[0].shape, own[0].dtype), own[0], beside)
    return [first] + [found[k] for k in range(1, len(own))]


def swap_back_far(pairs):
    found = {k: swap(pairs[k], "row", 2 * k) for k in range(len(pairs) - 1, 0, -1)}
    return [pairs[0]] + [found[k] for k in range(1, len(pairs))]


def swap_blocks(blocks, axis):
    count = lax.axis_size(axis)
    found = {k: lax.ppermute(blocks[k], axis, [(i, i ^ k) for i in range(count)]) for k in range(count - 1, 0, -1)}
    return [blocks[0]] + [found[k] for k in range(1, count)]


def pick_kernel(axis, after_ref, *refs):
    x_refs, out_ref = views(refs[:-1], 3), refs[-1]
    place = lax.axis_index(axis) ^ flip(axis)
    line = jnp.where(place == 0, 1, x_refs[0].shape[0] - 2)
    for part, x_ref in enumerate(x_refs):
        out_ref[part] = x_ref[line]


def pick(axis, after, xs):
    return pl.pallas_call(
        functools.partial(pick_kernel, axis),
        out_shape=jax.ShapeDtypeStruct((lax.axis_size("col" if axis == "col" else "row"),) + xs[-1].shape[-2:], xs[-1].dtype),
        in_specs=[pl.BlockSpec(memory_space=pl.ANY)] + [pl.BlockSpec(memory_space=pltpu.VMEM)] * len(xs),
        out_specs=pl.BlockSpec(memory_space=pltpu.VMEM),
        compiler_params=pltpu.CompilerParams(vmem_limit_bytes=4 * 1024 * 1024),
    )(after, *xs)


def seam_of(axis, line):
    count = lax.axis_size(axis)
    height, breadth = lax.axis_size("row"), lax.axis_size("col")
    if axis == "row":
        at = lambda group: (0 if group & 1 else count - 1) * breadth
        ends = [(at(c) + c, at(c) + c + 1) for c in range(breadth - 1)]
    else:
        at = lambda group: 0 if group & 1 else count - 1
        ends = [(at(r) + r * breadth, at(r) + (r + 1) * breadth) for r in range(height - 1)]
    pairs = ends + [(b, a) for a, b in ends]
    return lax.ppermute(line, ("row", "col"), pairs)


def local(
    features,
    norm_gain,
    in_weight,
    conv_weight,
    conv_bias,
    proj_weight,
    step_weight,
    step_bias,
    decay_log,
    skip_gain,
    out_gain,
    out_weight,
):
    height, width, channels = features.shape
    inner = out_weight.shape[0]
    tokens = height * width
    row_lines = height // lax.axis_size("col")
    col_lines = width // lax.axis_size("row")

    rows, cols = lax.axis_size("row"), lax.axis_size("col")
    vmem = pl.BlockSpec(memory_space=pltpu.VMEM)
    normed, *sends = pl.pallas_call(
        functools.partial(cut_kernel, rows),
        out_shape=[jax.ShapeDtypeStruct((tokens, channels), BF16)]
        + [jax.ShapeDtypeStruct((col_lines + 2, height, channels), BF16)] * (rows // 2)
        + [jax.ShapeDtypeStruct((rows // 2, col_lines + 2, height, channels), BF16)]
        + [jax.ShapeDtypeStruct((row_lines + 2, width, channels), BF16)] * cols,
        in_specs=[pl.BlockSpec(features.shape, lambda: (0, 0, 0)), pl.BlockSpec((channels,), lambda: (0,))],
        out_specs=[vmem] * (2 + rows // 2 + cols),
        scratch_shapes=[pltpu.VMEM((tokens, channels), BF16)],
        compiler_params=pltpu.CompilerParams(vmem_limit_bytes=12 * 1024 * 1024),
        cost_estimate=pl.CostEstimate(flops=6_000_000_000, bytes_accessed=2 << 20, transcendentals=tokens),
    )(features, norm_gain)
    weights = (in_weight, conv_weight, conv_bias, proj_weight, step_weight, step_bias, decay_log, skip_gain)
    gate = pl.pallas_call(
        gate_kernel,
        out_shape=jax.ShapeDtypeStruct((tokens, inner), BF16),
        grid=(1,),
        in_specs=[
            pl.BlockSpec((tokens, channels), lambda i: (0, 0)),
            pl.BlockSpec((channels, inner), lambda i: (0, 1)),
        ],
        out_specs=pl.BlockSpec((tokens, inner), lambda i: (0, 0)),
        compiler_params=pltpu.CompilerParams(vmem_limit_bytes=12 * 1024 * 1024),
        cost_estimate=pl.CostEstimate(flops=2 * tokens * channels * inner, bytes_accessed=1 << 20, transcendentals=0),
    )(normed, in_weight)

    half = rows // 2
    row_x = swap_blocks(sends[half + 1 :], "col")
    col_x = swap_out(sends[:half], sends[half])
    row_seam = seam_of("col", pick("col", normed, row_x))
    row_steps = prepare("col", normed, row_x, row_seam, *weights)
    col_seam = seam_of("row", pick("row", row_steps[0], col_x))
    col_steps = prepare("row", row_steps[0], col_x, col_seam, *weights)
    col_y = scan("row", normed, *col_steps, decay_log, skip_gain)
    joined = join("row", col_y, rows, col_lines, height, inner, normed)
    col_y = swap_back_far(joined)
    row_y = scan("col", joined[0], *row_steps, decay_log, skip_gain)
    beside = jax.ShapeDtypeStruct((half,) + joined[0].shape[1:], BF16)
    beside = simple(collect_kernel, beside, *col_y, after=row_y)
    row_y = swap_blocks(join("col", row_y, cols, row_lines, width, inner, beside), "col")
    beside = swap(beside, "row", 1)
    return pl.pallas_call(
        functools.partial(end_kernel, half),
        out_shape=jax.ShapeDtypeStruct(features.shape, BF16),
        scratch_shapes=[pltpu.VMEM((tokens, inner), BF16)],
        compiler_params=pltpu.CompilerParams(vmem_limit_bytes=16 * 1024 * 1024),
    )(gate, out_gain, out_weight, *col_y, beside, *row_y)


def solution(mesh):
    in_specs = (P("row", "col", None), P(), P(), P(), P(), P(), P(), P(), P(), P(), P(), P())
    out_specs = P("row", "col", None)
    return jax.shard_map(local, mesh=mesh, in_specs=in_specs, out_specs=out_specs, check_vma=False)
```

```python
import functools

import jax
import jax.numpy as jnp
from jax import lax
from jax.experimental import pallas as pl
from jax.experimental.pallas import tpu as pltpu
from jax.sharding import PartitionSpec as P

F32 = jnp.float32
BF16 = jnp.bfloat16
LANES = 128
SLOTS = 8
LOG2E = 1.4426950408889634


def bits(value):
    assert value & (value - 1) == 0
    return value.bit_length() - 1


def one_hot(targets, width):
    lane = lax.broadcasted_iota(jnp.int32, targets[0].shape, 1)
    blocks = []
    for block in range(pl.cdiv(width, LANES)):
        hit = targets[0] == lane + block * LANES
        for other in targets[1:]:
            hit = jnp.logical_or(hit, other == lane + block * LANES)
        blocks.append(jnp.where(hit, 1.0, 0.0).astype(BF16))
    return jnp.concatenate(blocks, axis=1)[:, :width]


def rows_of(count, start=0):
    return lax.broadcasted_iota(jnp.int32, (count, LANES), 0) + start


def dot(a, b):
    return jnp.dot(a, b, preferred_element_type=F32)


def layer_norm(values, scale_gain):
    centred = values - jnp.mean(values, axis=-1, keepdims=True)
    spread = jnp.mean(centred * centred, axis=-1, keepdims=True)
    return centred * lax.rsqrt(spread + 1e-05) * scale_gain


def flip(axis):
    other = "col" if axis == "row" else "row"
    return (lax.axis_index(other) & 1) * (lax.axis_size(axis) - 1)


def edge_kernel(feat_ref, *out_refs):
    height, width, channels = feat_ref.shape
    tile = feat_ref[...].reshape(height * width, channels)
    for second in range(2):
        odd = (lax.axis_index("row") + second) & 1
        out_refs[second][...] = feat_ref[jnp.where(odd == 1, 0, height - 1)]
        odd = (lax.axis_index("col") + second) & 1
        picked = one_hot([(rows_of(height) << bits(width)) + jnp.where(odd == 1, 0, width - 1)], height * width)
        out_refs[2 + second][...] = dot(picked, tile).astype(BF16)


def cut_kernel(columns, feat_ref, gain_ref, *refs):
    edge_refs, norm_ref, refs = refs[:4], refs[4], refs[5:]
    col_refs, beside_ref, row_refs = refs[: columns // 2], refs[columns // 2], refs[columns // 2 + 1 : -2]
    by_row_ref, by_col_ref = refs[-2:]
    height, width, channels = feat_ref.shape
    tokens = height * width
    gain = gain_ref[...][None]

    def normed(values):
        return layer_norm(values.astype(F32), gain).astype(BF16)

    tile = normed(feat_ref[...].reshape(tokens, channels))
    norm_ref[...] = tile
    by_row_ref[width : width + tokens] = tile
    row = rows_of(tokens)
    turned = dot(one_hot([((row & (height - 1)) << bits(width)) + (row >> bits(height))], tokens), tile)
    by_col_ref[height : height + tokens] = turned.astype(BF16)
    for axis, ext_ref, size in (("row", by_row_ref, width), ("col", by_col_ref, height)):
        first, second = edge_refs[:2] if axis == "row" else edge_refs[2:]
        first, second = normed(first[...]), normed(second[...])
        odd = (lax.axis_index(axis) & 1) == 1
        ext_ref[0:size] = jnp.where(odd, first, second)
        ext_ref[size + tokens : 2 * size + tokens] = jnp.where(odd, second, first)

    reach = row_refs[0].shape[0]
    turn = flip("col") ^ lax.axis_index("col")
    for part, row_ref in enumerate(row_refs):
        for line in range(reach):
            at = (part ^ turn) * (reach - 2) + line
            row_ref[line] = by_row_ref[pl.ds(pl.multiple_of(at * width, width), width)]
    reach = col_refs[0].shape[0]
    turn = flip("row") ^ lax.axis_index("row")
    for part in range(columns):
        for line in range(reach):
            at = (part ^ turn) * (reach - 2) + line
            found = by_col_ref[pl.ds(pl.multiple_of(at * height, height), height)]
            if part & 1:
                beside_ref[part >> 1, line] = found
            else:
                col_refs[part >> 1][line] = found


def gate_kernel(norm_ref, weight_ref, gate_ref):
    gate_ref[...] = dot(norm_ref[...], weight_ref[...]).astype(BF16)


def views(refs, rank):
    found = []
    for ref in refs:
        found += [ref] if len(ref.shape) == rank else [ref.at[k] for k in range(ref.shape[0])]
    return found


def by_slot(halves, rows):
    found = None
    for kind in range(halves * 2):
        row = rows(kind >> 1, kind & 1)
        row = jnp.broadcast_to(row, (SLOTS, row.shape[1]))
        slot = lax.broadcasted_iota(jnp.int32, row.shape, 0)
        found = row if found is None else jnp.where(slot >= kind * (SLOTS // (halves * 2)), row, found)
    return found


def prepare_kernel(
    lines,
    axis,
    after_ref,
    *refs,
):
    x_refs, refs = views(refs[:-15], 3), refs[-15:]
    (
        weight_ref,
        conv_ref,
        conv_bias_ref,
        proj_raw_ref,
        step_raw_ref,
        bias_raw_ref,
        proj_out_ref,
        s_ref,
        v_ref,
        token_ref,
        inner_ref,
        active_ref,
        proj_ref,
        step_ref,
        bias_ref,
    ) = refs
    ks = (0, 1) if axis == "col" else (2, 3)
    reach, length, channels = x_refs[0].shape
    parts = len(x_refs)
    states = (proj_raw_ref.shape[1] - RANK) // 2
    time = parts * length
    low = time // SLOTS
    width = weight_ref.shape[1] // 2
    chunk = s_ref.shape[2]
    halves = width // chunk
    slot_lines = SLOTS // (2 * halves)
    if axis == "row":
        across_first = lambda across, along: (along, across)
    else:
        across_first = lambda across, along: (across, along)

    row = rows_of(time)
    source = ((row & 7) << bits(low)) + (row >> 3)
    source = source ^ (lax.axis_index(axis) << bits(length))
    order = one_hot([source], time)
    for line in range(reach):
        x = jnp.concatenate([x_ref[line] for x_ref in x_refs], axis=0)
        token_ref[line * time : (line + 1) * time] = dot(order, x).astype(BF16)
    inner = dot(token_ref[...], weight_ref[:, :width]).astype(BF16).astype(F32)
    inner_ref[:, 1 : low + 1] = inner.reshape(reach, low, SLOTS, width)
    place = lax.broadcasted_iota(jnp.int32, (SLOTS, width), 0)
    for line in range(reach):
        inner_ref[line, 0] = jnp.where(place == 0, 0.0, pltpu.roll(inner_ref[line, low], 1, 0))
        inner_ref[line, low + 1] = jnp.where(place == SLOTS - 1, 0.0, pltpu.roll(inner_ref[line, 1], SLOTS - 1, 0))

    conv_bias = conv_bias_ref[...][None]

    def convolve(pair, _):
        for group in range(width // (2 * LANES)):
            cells = slice(group * 2 * LANES, (group + 1) * 2 * LANES)
            half = (group * 2 * LANES) // chunk
            base = group * 2 * LANES - half * chunk
            bias = jnp.broadcast_to(conv_bias[:, cells], (SLOTS, 2 * LANES))
            totals = [[bias for _ in range(2)] for _ in range(lines)]
            for across in range(3):
                for along in range(3):
                    first, second = across_first(across, along)
                    tap = jnp.broadcast_to(conv_ref[first, second : second + 1, cells], (SLOTS, 2 * LANES))
                    for line in range(lines):
                        for sub in range(2):
                            totals[line][sub] += inner_ref[line + across, 2 * pair + sub + along, :, cells] * tap
            for line in range(lines):
                value = jnp.concatenate(totals[line], axis=0)
                value = 0.5 * value
                value = value * jnp.tanh(value) + value
                value = value.astype(BF16)
                for piece in range(2):
                    at = base + piece * LANES
                    start = ((half + at // chunk) * lines + line) * time
                    start = pl.multiple_of(start + pair * (2 * SLOTS), 2 * SLOTS)
                    active_ref[pl.ds(start, 2 * SLOTS), at % chunk : at % chunk + LANES] = value[
                        :, piece * LANES : (piece + 1) * LANES
                    ]
        return 0

    lax.fori_loop(0, low // 2, convolve, 0)

    bias_ref[...] = by_slot(halves, lambda half, way: bias_raw_ref[ks[way] : ks[way] + 1, half * chunk : (half + 1) * chunk])
    for half in range(halves):
        cells = slice(half * chunk, (half + 1) * chunk)
        for way in range(2):
            kind = slice((half * 2 + way) * LANES, (half * 2 + way + 1) * LANES)
            w = proj_raw_ref[ks[way], :, cells].astype(F32)
            ranks = w[:RANK]
            rest = jnp.zeros((LANES - 3 * RANK - 2 * states, chunk), F32)
            w = jnp.concatenate([ranks, ranks, ranks, w[RANK:], rest], axis=0)
            proj_ref[:, kind] = w.T.astype(BF16)
            w = step_raw_ref[ks[way], :, cells]
            high = w.astype(BF16).astype(F32)
            rest = jnp.zeros((LANES - 3 * RANK, chunk), F32)
            step_ref[kind, :] = jnp.concatenate([high, high, w - high, rest], axis=0).astype(BF16)

    piece = 512
    for first in range(0, time * SLOTS, piece):
        row = rows_of(piece, first)
        now = row >> 3
        slot = row & 7
        line = slot & (slot_lines - 1)
        back = (slot >> bits(slot_lines)) & 1
        half = slot >> bits(2 * slot_lines)
        when = jnp.where(back == 1, time - 1 - now, now)
        source = half * (lines * time) + line * time + ((when & (low - 1)) << 3) + (when >> bits(low))
        if slot_lines > lines:
            source = jnp.where(line < lines, source, -1)
        u = dot(one_hot([source], halves * lines * time), active_ref[...])
        steps = pl.ds(first // SLOTS, piece // SLOTS)
        v_ref[steps] = u.reshape(piece // SLOTS, SLOTS, chunk)
        kind = slot >> bits(slot_lines)
        projected = dot(u.astype(BF16), proj_ref[...])
        p = projected[:, :LANES]
        for other in range(1, 2 * halves):
            p = jnp.where(kind == other, projected[:, other * LANES : (other + 1) * LANES], p)
        if halves == 2:
            p = p.reshape(piece // SLOTS, SLOTS, LANES)
            p = p + pltpu.roll(p, SLOTS // 2, 1)
            p = p.reshape(piece, LANES)
        proj_out_ref[steps] = p.reshape(piece // SLOTS, SLOTS, LANES)
        high = p.astype(BF16).astype(F32)
        lane = lax.broadcasted_iota(jnp.int32, p.shape, 1)
        mixed = jnp.where(jnp.logical_and(lane >= RANK, lane < 2 * RANK), p - high, high)
        stacked = jnp.concatenate([jnp.where(kind == k, mixed, 0.0).astype(BF16) for k in range(2 * halves)], axis=1)
        s_ref[steps] = dot(stacked, step_ref[...]).reshape(piece // SLOTS, SLOTS, chunk)

    def soften(lap, _):
        for sub in range(8):
            t = lap * 8 + sub
            for g in range(chunk // LANES):
                cells = slice(g * LANES, (g + 1) * LANES)
                before = s_ref[t, :, cells] + bias_ref[:, cells]
                small = jnp.exp(-jnp.abs(before))
                log1p = jnp.where(small < 0.001, small - 0.5 * small * small, jnp.log(1.0 + small))
                step = jnp.maximum(before, 0.0) + log1p
                s_ref[t, :, cells] = step
        return 0

    lax.fori_loop(0, time // 8, soften, 0)


def scan_kernel(
    axis,
    after_ref,
    coef_ref,
    s_ref,
    u_ref,
    decay_ref,
    skip_raw_ref,
    out_ref,
    v_ref,
    y_ref,
    spread_ref,
):
    time, _, chunk = s_ref.shape
    halves = decay_ref.shape[2] // chunk
    states = decay_ref.shape[1]
    groups = chunk // LANES
    at_once = 4
    unroll = 16 if axis == "col" else 32
    laps = time // unroll

    ks = (0, 1) if axis == "col" else (2, 3)
    piece = 64
    row = lax.broadcasted_iota(jnp.int32, (2 * LANES, LANES), 0) & (LANES - 1)
    taken = [jnp.where(row == 3 * RANK + n, 1.0, 0.0).astype(BF16) for n in range(2 * states)]

    def spread(lap, _):
        steps = pl.ds(lap * piece, piece)
        coefs = coef_ref[steps].reshape(piece * SLOTS, LANES)
        high = coefs.astype(BF16)
        both = jnp.concatenate([high, (coefs - high.astype(F32)).astype(BF16)], axis=1)
        for n in range(0, 2 * states, 4):
            found = dot(both, jnp.concatenate(taken[n : n + 4], axis=1))
            for k in range(4):
                spread_ref[steps, n + k] = found[:, k * LANES : (k + 1) * LANES].reshape(piece, SLOTS, LANES)
        return 0

    lax.fori_loop(0, time // piece, spread, 0)
    for first in range(0, states, at_once):
        rates = []
        for n in range(first, first + at_once):
            rates.append([])
            for g in range(groups):
                rate = by_slot(
                    halves,
                    lambda half, way: decay_ref[ks[way], n : n + 1, half * chunk + g * LANES : half * chunk + (g + 1) * LANES],
                )
                rates[-1].append(-LOG2E * jnp.exp(rate))
        if first == 0:
            skips = [
                by_slot(
                    halves,
                    lambda half, way: skip_raw_ref[
                        ks[way] : ks[way] + 1, half * chunk + g * LANES : half * chunk + (g + 1) * LANES
                    ],
                )
                for g in range(groups)
            ]

        def advance(lap, hidden):
            hidden = list(hidden)
            for sub in range(unroll):
                t = lap * unroll + sub
                enter = [spread_ref[t, first + n] for n in range(at_once)]
                leave = [spread_ref[t, states + first + n] for n in range(at_once)]
                decay = []
                for g in range(groups):
                    step = s_ref[t, :, g * LANES : (g + 1) * LANES]
                    decay.append([jnp.exp2(step * rates[n][g]) for n in range(at_once)])
                for g in range(groups):
                    cells = pl.ds(g * LANES, LANES)
                    if first == 0:
                        u = u_ref[t, :, cells]
                        value = s_ref[t, :, cells] * u
                        v_ref[t, :, cells] = value
                        y = skips[g] * u
                    else:
                        value = v_ref[t, :, cells]
                        y = y_ref[t, :, cells]
                    for n in range(at_once):
                        k = n * groups + g
                        h = decay[g][n] * hidden[k] + value * enter[n]
                        hidden[k] = h
                        y = y + h * leave[n]
                    y_ref[t, :, cells] = y
            return tuple(hidden)

        zero = jnp.zeros((SLOTS, LANES), F32)
        lax.fori_loop(0, laps, advance, (zero,) * (at_once * groups))

    out_ref[...] = y_ref[...].reshape(time * SLOTS, chunk).astype(BF16)


def join_kernel(parts, lines, axis, after_ref, scanned_ref, *out_refs):
    length = out_refs[0].shape[-2] // lines
    time = parts * length
    chunk = scanned_ref.shape[1]
    halves = out_refs[0].shape[-1] // chunk
    slot_lines = SLOTS // (2 * halves)
    row = rows_of(lines * time)
    line = (row >> bits(length)) & (lines - 1)
    part = row >> bits(lines * length)
    part = part ^ lax.axis_index(axis)
    now = (part << bits(length)) + (row & (length - 1))
    for half in range(halves):
        ahead = now * SLOTS + (half * 2 * slot_lines) + line
        behind = (time - 1 - now) * SLOTS + (half * 2 * slot_lines + slot_lines) + line
        joined = dot(one_hot([ahead, behind], time * SLOTS), scanned_ref[...]).astype(BF16)
        size = lines * length
        for part in range(parts):
            found = joined[part * size : (part + 1) * size]
            if len(out_refs) < parts:
                out_refs[part >> 1][part & 1, :, half * chunk : (half + 1) * chunk] = found
            else:
                out_refs[part][:, half * chunk : (half + 1) * chunk] = found


def join(axis, scanned, parts, lines, length, width, after):
    size = (lines * length, width)
    shapes = [size] * parts if axis == "col" else [(2,) + size] * (parts // 2)
    return pl.pallas_call(
        functools.partial(join_kernel, parts, lines, axis),
        out_shape=[jax.ShapeDtypeStruct(shape, BF16) for shape in shapes],
        in_specs=[pl.BlockSpec(memory_space=pl.ANY), pl.BlockSpec(memory_space=pltpu.VMEM)],
        out_specs=[pl.BlockSpec(memory_space=pltpu.VMEM)] * len(shapes),
        compiler_params=pltpu.CompilerParams(vmem_limit_bytes=24 * 1024 * 1024),
    )(after, scanned)


RANK = 24


def prepare(axis, after, xs, in_weight, conv, conv_bias, proj, step_weight, step_bias, decay_log, skip):
    parts = lax.axis_size(axis)
    reach, length, channels = xs[0].shape[-3:]
    lines = reach - 2
    time = parts * length
    width = conv.shape[2]
    states = decay_log.shape[2]
    assert step_weight.shape[1] == RANK and in_weight.shape[1] == 2 * width
    halves = 1 if lines >= 4 else 2
    assert lines <= SLOTS // (2 * halves)
    chunk = width // halves
    vmem = pl.BlockSpec(memory_space=pltpu.VMEM)
    flops = 2 * time * (reach * channels * width + SLOTS * width * 256)
    return pl.pallas_call(
        functools.partial(prepare_kernel, lines, axis),
        out_shape=[
            jax.ShapeDtypeStruct((time, SLOTS, LANES), F32),
            jax.ShapeDtypeStruct((time, SLOTS, chunk), F32),
            jax.ShapeDtypeStruct((time, SLOTS, chunk), F32),
        ],
        in_specs=[pl.BlockSpec(memory_space=pl.ANY)] + [vmem] * (len(xs) + 6),
        out_specs=[vmem, vmem, vmem],
        scratch_shapes=[
            pltpu.VMEM((reach * time, channels), BF16),
            pltpu.VMEM((reach, time // SLOTS + 2, SLOTS, width), F32),
            pltpu.VMEM((halves * lines * time, chunk), BF16),
            pltpu.VMEM((chunk, halves * 2 * LANES), BF16),
            pltpu.VMEM((halves * 2 * LANES, chunk), BF16),
            pltpu.VMEM((SLOTS, chunk), F32),
        ],
        compiler_params=pltpu.CompilerParams(vmem_limit_bytes=24 * 1024 * 1024),
        cost_estimate=pl.CostEstimate(flops=4 * flops, bytes_accessed=4 * 1024 * 1024, transcendentals=time * SLOTS * chunk),
    )(
        after,
        *xs,
        in_weight,
        conv,
        conv_bias,
        jnp.swapaxes(proj, 1, 2),
        step_weight,
        step_bias,
    )


def scan(axis, after, coefs, steps, u, decay_log, skip):
    time, _, chunk = steps.shape
    width, states = decay_log.shape[1:]
    vmem = pl.BlockSpec(memory_space=pltpu.VMEM)
    return pl.pallas_call(
        functools.partial(scan_kernel, axis),
        out_shape=jax.ShapeDtypeStruct((time * SLOTS, chunk), BF16),
        in_specs=[pl.BlockSpec(memory_space=pl.ANY), vmem, vmem, vmem, vmem, vmem],
        out_specs=vmem,
        scratch_shapes=[
            pltpu.VMEM((time, SLOTS, chunk), F32),
            pltpu.VMEM((time, SLOTS, chunk), F32),
            pltpu.VMEM((time, 2 * states, SLOTS, LANES), F32),
        ],
        compiler_params=pltpu.CompilerParams(vmem_limit_bytes=(8 << 20) + time * (136 << 10) + time * 20 * chunk),
        cost_estimate=pl.CostEstimate(
            flops=8 * time * SLOTS * chunk * states,
            bytes_accessed=4 * 1024 * 1024,
            transcendentals=time * SLOTS * chunk * states,
        ),
    )(after, coefs, steps, u, jnp.swapaxes(decay_log, 1, 2), skip)


def end_kernel(columns, gate_ref, gain_ref, weight_ref, *refs):
    pair_refs, beside_ref, row_refs, out_ref, gated_ref = refs[:columns], refs[columns], refs[columns + 1 : -2], refs[-2], refs[-1]
    height, width, channels = out_ref.shape
    size = row_refs[0].shape[0]
    lines = size // width
    swap = flip("col") ^ lax.axis_index("col")
    turn = (flip("row") ^ lax.axis_index("row")) * (width // lax.axis_size("row"))
    row = rows_of(height * width)
    line = (row >> bits(width)) ^ (swap * lines)
    source = (((row & (width - 1)) ^ turn) << bits(height)) + line
    rows = jnp.concatenate([row_ref[...] for row_ref in row_refs], axis=0)
    blocks = []
    for part in range(columns):
        blocks += [pair_refs[part][0], beside_ref[part]]
    columns = jnp.concatenate(blocks, axis=0)
    combined = layer_norm(rows.astype(F32) + dot(one_hot([source], height * width), columns), gain_ref[...][None])
    for part in range(len(row_refs)):
        cells = pl.ds(pl.multiple_of((part ^ swap) * size, size), size)
        gate = gate_ref[cells].astype(F32)
        gated_ref[cells] = (combined[part * size : (part + 1) * size] * (gate / (1.0 + jnp.exp(-gate)))).astype(BF16)
    out = dot(gated_ref[...], weight_ref[...]).astype(BF16)
    out_ref[...] = out.reshape(height, width, channels)


def pair_kernel(*refs):
    count = len(refs) // 2
    own_refs, beside_ref, out_refs = refs[:count], refs[count], refs[count + 1 :]
    for k in range(count):
        out_refs[k][0] = own_refs[k][...]
        out_refs[k][1] = beside_ref[k + 1]


def first_kernel(own_ref, beside_ref, out_ref):
    out_ref[0] = own_ref[...]
    out_ref[1] = beside_ref[0]


def collect_kernel(after_ref, *refs):
    out_ref = refs[-1]
    for k in range(len(refs) - 1):
        out_ref[k] = refs[k][1]


def simple(kernel, shapes, *arrays, after=None):
    vmem = pl.BlockSpec(memory_space=pltpu.VMEM)
    first = [] if after is None else [after]
    many = isinstance(shapes, list)
    return pl.pallas_call(
        kernel,
        out_shape=shapes,
        in_specs=[pl.BlockSpec(memory_space=pl.ANY)] * len(first) + [vmem] * len(arrays),
        out_specs=[vmem] * len(shapes) if many else vmem,
        compiler_params=pltpu.CompilerParams(vmem_limit_bytes=4 * 1024 * 1024),
        cost_estimate=pl.CostEstimate(flops=0, bytes_accessed=2 << 20, transcendentals=0),
    )(*first, *arrays)


def swap(block, axis, k):
    return lax.ppermute(block, axis, [(i, i ^ k) for i in range(lax.axis_size(axis))])


def swap_out(own, beside):
    beside = swap(beside, "row", 1)
    shape = jax.ShapeDtypeStruct((2,) + own[0].shape, own[0].dtype)
    pairs = simple(pair_kernel, [shape] * (len(own) - 1), *own[1:], beside)
    found = {k: swap(pairs[k - 1], "row", 2 * k) for k in range(len(own) - 1, 0, -1)}
    first = simple(first_kernel, jax.ShapeDtypeStruct((2,) + own[0].shape, own[0].dtype), own[0], beside)
    return [first] + [found[k] for k in range(1, len(own))]


def swap_back_far(pairs):
    found = {k: swap(pairs[k], "row", 2 * k) for k in range(len(pairs) - 1, 0, -1)}
    return [pairs[0]] + [found[k] for k in range(1, len(pairs))]


def swap_blocks(blocks, axis):
    count = lax.axis_size(axis)
    found = {k: lax.ppermute(blocks[k], axis, [(i, i ^ k) for i in range(count)]) for k in range(count - 1, 0, -1)}
    return [blocks[0]] + [found[k] for k in range(1, count)]


def neighbours(first, second, axis):
    count = lax.axis_size(axis)
    pairs = [(i, i + 1) for i in range(1, count - 1, 2)]
    return swap(first, axis, 1), lax.ppermute(second, axis, pairs + [(b, a) for a, b in pairs])


def local(
    features,
    norm_gain,
    in_weight,
    conv_weight,
    conv_bias,
    proj_weight,
    step_weight,
    step_bias,
    decay_log,
    skip_gain,
    out_gain,
    out_weight,
):
    height, width, channels = features.shape
    inner = out_weight.shape[0]
    tokens = height * width
    row_lines = height // lax.axis_size("col")
    col_lines = width // lax.axis_size("row")

    rows, cols = lax.axis_size("row"), lax.axis_size("col")
    vmem = pl.BlockSpec(memory_space=pltpu.VMEM)
    edges = simple(
        edge_kernel,
        [jax.ShapeDtypeStruct((width, channels), BF16)] * 2 + [jax.ShapeDtypeStruct((height, channels), BF16)] * 2,
        features,
    )
    edges = neighbours(*edges[:2], "row") + neighbours(*edges[2:], "col")
    normed, *sends = pl.pallas_call(
        functools.partial(cut_kernel, rows),
        out_shape=[jax.ShapeDtypeStruct((tokens, channels), BF16)]
        + [jax.ShapeDtypeStruct((col_lines + 2, height, channels), BF16)] * (rows // 2)
        + [jax.ShapeDtypeStruct((rows // 2, col_lines + 2, height, channels), BF16)]
        + [jax.ShapeDtypeStruct((row_lines + 2, width, channels), BF16)] * cols,
        in_specs=[vmem, pl.BlockSpec((channels,), lambda: (0,))] + [vmem] * 4,
        out_specs=[vmem] * (2 + rows // 2 + cols),
        scratch_shapes=[
            pltpu.VMEM((tokens + 2 * width, channels), BF16),
            pltpu.VMEM((tokens + 2 * height, channels), BF16),
        ],
        compiler_params=pltpu.CompilerParams(vmem_limit_bytes=12 * 1024 * 1024),
        cost_estimate=pl.CostEstimate(flops=6_000_000_000, bytes_accessed=2 << 20, transcendentals=tokens),
    )(features, norm_gain, *edges)
    weights = (in_weight, conv_weight, conv_bias, proj_weight, step_weight, step_bias, decay_log, skip_gain)
    gate = pl.pallas_call(
        gate_kernel,
        out_shape=jax.ShapeDtypeStruct((tokens, inner), BF16),
        grid=(1,),
        in_specs=[
            pl.BlockSpec((tokens, channels), lambda i: (0, 0)),
            pl.BlockSpec((channels, inner), lambda i: (0, 1)),
        ],
        out_specs=pl.BlockSpec((tokens, inner), lambda i: (0, 0)),
        compiler_params=pltpu.CompilerParams(vmem_limit_bytes=12 * 1024 * 1024),
        cost_estimate=pl.CostEstimate(flops=2 * tokens * channels * inner, bytes_accessed=1 << 20, transcendentals=0),
    )(normed, in_weight)

    half = rows // 2
    row_x = swap_blocks(sends[half + 1 :], "col")
    col_x = swap_out(sends[:half], sends[half])
    row_steps = prepare("col", normed, row_x, *weights)
    col_steps = prepare("row", row_steps[0], col_x, *weights)
    col_y = scan("row", normed, *col_steps, decay_log, skip_gain)
    joined = join("row", col_y, rows, col_lines, height, inner, normed)
    col_y = swap_back_far(joined)
    row_y = scan("col", joined[0], *row_steps, decay_log, skip_gain)
    beside = jax.ShapeDtypeStruct((half,) + joined[0].shape[1:], BF16)
    beside = simple(collect_kernel, beside, *col_y, after=row_y)
    row_y = swap_blocks(join("col", row_y, cols, row_lines, width, inner, beside), "col")
    beside = swap(beside, "row", 1)
    return pl.pallas_call(
        functools.partial(end_kernel, half),
        out_shape=jax.ShapeDtypeStruct(features.shape, BF16),
        scratch_shapes=[pltpu.VMEM((tokens, inner), BF16)],
        compiler_params=pltpu.CompilerParams(vmem_limit_bytes=16 * 1024 * 1024),
    )(gate, out_gain, out_weight, *col_y, beside, *row_y)


def solution(mesh):
    in_specs = (P("row", "col", None), P(), P(), P(), P(), P(), P(), P(), P(), P(), P(), P())
    out_specs = P("row", "col", None)
    return jax.shard_map(local, mesh=mesh, in_specs=in_specs, out_specs=out_specs, check_vma=False)
```

```python
import functools

import jax
import jax.numpy as jnp
from jax import lax
from jax.experimental import pallas as pl
from jax.experimental.pallas import tpu as pltpu
from jax.sharding import PartitionSpec as P

F32 = jnp.float32
BF16 = jnp.bfloat16
LANES = 128
SLOTS = 8
LOG2E = 1.4426950408889634


def bits(value):
    assert value & (value - 1) == 0
    return value.bit_length() - 1


def one_hot(targets, width):
    lane = lax.broadcasted_iota(jnp.int32, targets[0].shape, 1)
    blocks = []
    for block in range(pl.cdiv(width, LANES)):
        hit = targets[0] == lane + block * LANES
        for other in targets[1:]:
            hit = jnp.logical_or(hit, other == lane + block * LANES)
        blocks.append(jnp.where(hit, 1.0, 0.0).astype(BF16))
    return jnp.concatenate(blocks, axis=1)[:, :width]


def rows_of(count, start=0):
    return lax.broadcasted_iota(jnp.int32, (count, LANES), 0) + start


def dot(a, b):
    return jnp.dot(a, b, preferred_element_type=F32)


def layer_norm(values, scale_gain):
    centred = values - jnp.mean(values, axis=-1, keepdims=True)
    spread = jnp.mean(centred * centred, axis=-1, keepdims=True)
    return centred * lax.rsqrt(spread + 1e-05) * scale_gain


def flip(axis):
    other = "col" if axis == "row" else "row"
    return (lax.axis_index(other) & 1) * (lax.axis_size(axis) - 1)


def cut_kernel(columns, feat_ref, gain_ref, norm_ref, *refs):
    col_refs, beside_ref, row_refs, turned_ref = refs[: columns // 2], refs[columns // 2], refs[columns // 2 + 1 : -1], refs[-1]
    height, width, channels = feat_ref.shape
    tile = layer_norm(feat_ref[...].reshape(height * width, channels).astype(F32), gain_ref[...][None]).astype(BF16)
    norm_ref[...] = tile
    reach = row_refs[0].shape[0]
    turn = flip("col") ^ lax.axis_index("col")
    for part, row_ref in enumerate(row_refs):
        for line in range(reach):
            at = jnp.clip((part ^ turn) * (reach - 2) + line - 1, 0, height - 1)
            row_ref[line] = norm_ref[pl.ds(pl.multiple_of(at * width, width), width)]
    row = rows_of(height * width)
    turned = dot(one_hot([((row & (height - 1)) << bits(width)) + (row >> bits(height))], height * width), tile).astype(
        BF16
    )
    turned_ref[...] = turned
    reach = col_refs[0].shape[0]
    turn = flip("row") ^ lax.axis_index("row")
    for part in range(columns):
        for line in range(reach):
            at = jnp.clip((part ^ turn) * (reach - 2) + line - 1, 0, width - 1)
            found = turned_ref[pl.ds(pl.multiple_of(at * height, height), height)]
            if part & 1:
                beside_ref[part >> 1, line] = found
            else:
                col_refs[part >> 1][line] = found


def gate_kernel(norm_ref, weight_ref, gate_ref):
    gate_ref[...] = dot(norm_ref[...], weight_ref[...]).astype(BF16)


def views(refs, rank):
    found = []
    for ref in refs:
        found += [ref] if len(ref.shape) == rank else [ref.at[k] for k in range(ref.shape[0])]
    return found


def by_slot(halves, rows):
    found = None
    for kind in range(halves * 2):
        row = rows(kind >> 1, kind & 1)
        row = jnp.broadcast_to(row, (SLOTS, row.shape[1]))
        slot = lax.broadcasted_iota(jnp.int32, row.shape, 0)
        found = row if found is None else jnp.where(slot >= kind * (SLOTS // (halves * 2)), row, found)
    return found


def prepare_kernel(
    lines,
    axis,
    after_ref,
    *refs,
):
    x_refs, refs = views(refs[:-16], 3), refs[-16:]
    (
        seam_ref,
        weight_ref,
        conv_ref,
        conv_bias_ref,
        proj_raw_ref,
        step_raw_ref,
        bias_raw_ref,
        proj_out_ref,
        s_ref,
        v_ref,
        token_ref,
        inner_ref,
        active_ref,
        proj_ref,
        step_ref,
        bias_ref,
    ) = refs
    ks = (0, 1) if axis == "col" else (2, 3)
    parts, length, channels = seam_ref.shape
    reach = lines + 2
    states = (proj_raw_ref.shape[1] - RANK) // 2
    time = parts * length
    low = time // SLOTS
    width = weight_ref.shape[1] // 2
    chunk = s_ref.shape[2]
    halves = width // chunk
    slot_lines = SLOTS // (2 * halves)
    if axis == "row":
        across_first = lambda across, along: (along, across)
    else:
        across_first = lambda across, along: (across, along)

    row = rows_of(time)
    source = ((row & 7) << bits(low)) + (row >> 3)
    source = source ^ (lax.axis_index(axis) << bits(length))
    order = one_hot([source], time)
    for line in range(reach):
        x = jnp.concatenate([x_ref[line] for x_ref in x_refs], axis=0)
        if line == 0 or line == reach - 1:
            place = lax.axis_index(axis) ^ flip(axis)
            missing = place == (0 if line == 0 else lax.axis_size(axis) - 1)
            x = jnp.where(missing, seam_ref[...].reshape(time, channels), x)
        token_ref[line * time : (line + 1) * time] = dot(order, x).astype(BF16)
    inner = dot(token_ref[...], weight_ref[:, :width]).astype(BF16).astype(F32)
    inner_ref[:, 1 : low + 1] = inner.reshape(reach, low, SLOTS, width)
    place = lax.broadcasted_iota(jnp.int32, (SLOTS, width), 0)
    for line in range(reach):
        inner_ref[line, 0] = jnp.where(place == 0, 0.0, pltpu.roll(inner_ref[line, low], 1, 0))
        inner_ref[line, low + 1] = jnp.where(place == SLOTS - 1, 0.0, pltpu.roll(inner_ref[line, 1], SLOTS - 1, 0))

    conv_bias = conv_bias_ref[...][None]

    def convolve(pair, _):
        for group in range(width // (2 * LANES)):
            cells = slice(group * 2 * LANES, (group + 1) * 2 * LANES)
            half = (group * 2 * LANES) // chunk
            base = group * 2 * LANES - half * chunk
            bias = jnp.broadcast_to(conv_bias[:, cells], (SLOTS, 2 * LANES))
            totals = [[bias for _ in range(2)] for _ in range(lines)]
            for across in range(3):
                for along in range(3):
                    first, second = across_first(across, along)
                    tap = jnp.broadcast_to(conv_ref[first, second : second + 1, cells], (SLOTS, 2 * LANES))
                    for line in range(lines):
                        for sub in range(2):
                            totals[line][sub] += inner_ref[line + across, 2 * pair + sub + along, :, cells] * tap
            for line in range(lines):
                value = jnp.concatenate(totals[line], axis=0)
                value = 0.5 * value
                value = value * jnp.tanh(value) + value
                value = value.astype(BF16)
                for piece in range(2):
                    at = base + piece * LANES
                    start = ((half + at // chunk) * lines + line) * time
                    start = pl.multiple_of(start + pair * (2 * SLOTS), 2 * SLOTS)
                    active_ref[pl.ds(start, 2 * SLOTS), at % chunk : at % chunk + LANES] = value[
                        :, piece * LANES : (piece + 1) * LANES
                    ]
        return 0

    lax.fori_loop(0, low // 2, convolve, 0)

    bias_ref[...] = by_slot(halves, lambda half, way: bias_raw_ref[ks[way] : ks[way] + 1, half * chunk : (half + 1) * chunk])
    for half in range(halves):
        cells = slice(half * chunk, (half + 1) * chunk)
        for way in range(2):
            kind = slice((half * 2 + way) * LANES, (half * 2 + way + 1) * LANES)
            w = proj_raw_ref[ks[way], :, cells].astype(F32)
            ranks = w[:RANK]
            rest = jnp.zeros((LANES - 3 * RANK - 2 * states, chunk), F32)
            w = jnp.concatenate([ranks, ranks, ranks, w[RANK:], rest], axis=0)
            proj_ref[:, kind] = w.T.astype(BF16)
            w = step_raw_ref[ks[way], :, cells]
            high = w.astype(BF16).astype(F32)
            rest = jnp.zeros((LANES - 3 * RANK, chunk), F32)
            step_ref[kind, :] = jnp.concatenate([high, high, w - high, rest], axis=0).astype(BF16)

    piece = 512
    for first in range(0, time * SLOTS, piece):
        row = rows_of(piece, first)
        now = row >> 3
        slot = row & 7
        line = slot & (slot_lines - 1)
        back = (slot >> bits(slot_lines)) & 1
        half = slot >> bits(2 * slot_lines)
        when = jnp.where(back == 1, time - 1 - now, now)
        source = half * (lines * time) + line * time + ((when & (low - 1)) << 3) + (when >> bits(low))
        if slot_lines > lines:
            source = jnp.where(line < lines, source, -1)
        u = dot(one_hot([source], halves * lines * time), active_ref[...])
        steps = pl.ds(first // SLOTS, piece // SLOTS)
        v_ref[steps] = u.reshape(piece // SLOTS, SLOTS, chunk)
        kind = slot >> bits(slot_lines)
        projected = dot(u.astype(BF16), proj_ref[...])
        p = projected[:, :LANES]
        for other in range(1, 2 * halves):
            p = jnp.where(kind == other, projected[:, other * LANES : (other + 1) * LANES], p)
        if halves == 2:
            p = p.reshape(piece // SLOTS, SLOTS, LANES)
            p = p + pltpu.roll(p, SLOTS // 2, 1)
            p = p.reshape(piece, LANES)
        proj_out_ref[steps] = p.reshape(piece // SLOTS, SLOTS, LANES)
        high = p.astype(BF16).astype(F32)
        lane = lax.broadcasted_iota(jnp.int32, p.shape, 1)
        mixed = jnp.where(jnp.logical_and(lane >= RANK, lane < 2 * RANK), p - high, high)
        stacked = jnp.concatenate([jnp.where(kind == k, mixed, 0.0).astype(BF16) for k in range(2 * halves)], axis=1)
        s_ref[steps] = dot(stacked, step_ref[...]).reshape(piece // SLOTS, SLOTS, chunk)

    def soften(lap, _):
        for sub in range(8):
            t = lap * 8 + sub
            for g in range(chunk // LANES):
                cells = slice(g * LANES, (g + 1) * LANES)
                before = s_ref[t, :, cells] + bias_ref[:, cells]
                small = jnp.exp(-jnp.abs(before))
                log1p = jnp.where(small < 0.001, small - 0.5 * small * small, jnp.log(1.0 + small))
                step = jnp.maximum(before, 0.0) + log1p
                s_ref[t, :, cells] = step
        return 0

    lax.fori_loop(0, time // 8, soften, 0)


def scan_kernel(
    axis,
    after_ref,
    coef_ref,
    s_ref,
    u_ref,
    decay_ref,
    skip_raw_ref,
    out_ref,
    v_ref,
    y_ref,
    spread_ref,
):
    time, _, chunk = s_ref.shape
    halves = decay_ref.shape[2] // chunk
    states = decay_ref.shape[1]
    groups = chunk // LANES
    at_once = 4
    unroll = 16 if axis == "col" else 32
    laps = time // unroll

    ks = (0, 1) if axis == "col" else (2, 3)
    piece = 64
    row = lax.broadcasted_iota(jnp.int32, (LANES, LANES), 0)
    taken = [jnp.where(row == 3 * RANK + n, 1.0, 0.0).astype(BF16) for n in range(2 * states)]

    def spread(lap, _):
        steps = pl.ds(lap * piece, piece)
        coefs = coef_ref[steps].reshape(piece * SLOTS, LANES).astype(BF16)
        for n in range(0, 2 * states, 4):
            found = dot(coefs, jnp.concatenate(taken[n : n + 4], axis=1))
            found = [found[:, k * LANES : (k + 1) * LANES].reshape(piece, SLOTS, LANES) for k in range(4)]
            for k in range(0, 4, 2):
                spread_ref[steps, (n + k) // 2] = jnp.concatenate(found[k : k + 2], axis=1).astype(BF16)
        return 0

    lax.fori_loop(0, time // piece, spread, 0)
    for first in range(0, states, at_once):
        rates = []
        for n in range(first, first + at_once):
            rates.append([])
            for g in range(groups):
                rate = by_slot(
                    halves,
                    lambda half, way: decay_ref[ks[way], n : n + 1, half * chunk + g * LANES : half * chunk + (g + 1) * LANES],
                )
                rates[-1].append(-LOG2E * jnp.exp(rate))
        if first == 0:
            skips = [
                by_slot(
                    halves,
                    lambda half, way: skip_raw_ref[
                        ks[way] : ks[way] + 1, half * chunk + g * LANES : half * chunk + (g + 1) * LANES
                    ],
                )
                for g in range(groups)
            ]

        def advance(lap, hidden):
            hidden = list(hidden)
            for sub in range(unroll):
                t = lap * unroll + sub
                enter, leave = [], []
                for n in range(first, first + at_once, 2):
                    both = spread_ref[t, n // 2].astype(F32)
                    enter += [both[:SLOTS], both[SLOTS:]]
                    both = spread_ref[t, (states + n) // 2].astype(F32)
                    leave += [both[:SLOTS], both[SLOTS:]]
                decay = []
                for g in range(groups):
                    step = s_ref[t, :, g * LANES : (g + 1) * LANES]
                    decay.append([jnp.exp2(step * rates[n][g]) for n in range(at_once)])
                for g in range(groups):
                    cells = pl.ds(g * LANES, LANES)
                    if first == 0:
                        u = u_ref[t, :, cells]
                        value = s_ref[t, :, cells] * u
                        v_ref[t, :, cells] = value
                        y = skips[g] * u
                    else:
                        value = v_ref[t, :, cells]
                        y = y_ref[t, :, cells]
                    for n in range(at_once):
                        k = n * groups + g
                        h = decay[g][n] * hidden[k] + value * enter[n]
                        hidden[k] = h
                        y = y + h * leave[n]
                    y_ref[t, :, cells] = y
            return tuple(hidden)

        zero = jnp.zeros((SLOTS, LANES), F32)
        lax.fori_loop(0, laps, advance, (zero,) * (at_once * groups))

    out_ref[...] = y_ref[...].reshape(time * SLOTS, chunk).astype(BF16)


def join_kernel(parts, lines, axis, after_ref, scanned_ref, *out_refs):
    length = out_refs[0].shape[-2] // lines
    time = parts * length
    chunk = scanned_ref.shape[1]
    halves = out_refs[0].shape[-1] // chunk
    slot_lines = SLOTS // (2 * halves)
    row = rows_of(lines * time)
    line = (row >> bits(length)) & (lines - 1)
    part = row >> bits(lines * length)
    part = part ^ lax.axis_index(axis)
    now = (part << bits(length)) + (row & (length - 1))
    for half in range(halves):
        ahead = now * SLOTS + (half * 2 * slot_lines) + line
        behind = (time - 1 - now) * SLOTS + (half * 2 * slot_lines + slot_lines) + line
        joined = dot(one_hot([ahead, behind], time * SLOTS), scanned_ref[...]).astype(BF16)
        size = lines * length
        for part in range(parts):
            found = joined[part * size : (part + 1) * size]
            if len(out_refs) < parts:
                out_refs[part >> 1][part & 1, :, half * chunk : (half + 1) * chunk] = found
            else:
                out_refs[part][:, half * chunk : (half + 1) * chunk] = found


def join(axis, scanned, parts, lines, length, width, after):
    size = (lines * length, width)
    shapes = [size] * parts if axis == "col" else [(2,) + size] * (parts // 2)
    return pl.pallas_call(
        functools.partial(join_kernel, parts, lines, axis),
        out_shape=[jax.ShapeDtypeStruct(shape, BF16) for shape in shapes],
        in_specs=[pl.BlockSpec(memory_space=pl.ANY), pl.BlockSpec(memory_space=pltpu.VMEM)],
        out_specs=[pl.BlockSpec(memory_space=pltpu.VMEM)] * len(shapes),
        compiler_params=pltpu.CompilerParams(vmem_limit_bytes=24 * 1024 * 1024),
    )(after, scanned)


RANK = 24


def prepare(axis, after, xs, seam, in_weight, conv, conv_bias, proj, step_weight, step_bias, decay_log, skip):
    parts, length, channels = seam.shape
    reach = xs[0].shape[-3]
    lines = reach - 2
    time = parts * length
    width = conv.shape[2]
    states = decay_log.shape[2]
    assert step_weight.shape[1] == RANK and in_weight.shape[1] == 2 * width
    halves = 1 if lines >= 4 else 2
    assert lines <= SLOTS // (2 * halves)
    chunk = width // halves
    vmem = pl.BlockSpec(memory_space=pltpu.VMEM)
    flops = 2 * time * (reach * channels * width + SLOTS * width * 256)
    return pl.pallas_call(
        functools.partial(prepare_kernel, lines, axis),
        out_shape=[
            jax.ShapeDtypeStruct((time, SLOTS, LANES), F32),
            jax.ShapeDtypeStruct((time, SLOTS, chunk), F32),
            jax.ShapeDtypeStruct((time, SLOTS, chunk), F32),
        ],
        in_specs=[pl.BlockSpec(memory_space=pl.ANY)] + [vmem] * (len(xs) + 7),
        out_specs=[vmem, vmem, vmem],
        scratch_shapes=[
            pltpu.VMEM((reach * time, channels), BF16),
            pltpu.VMEM((reach, time // SLOTS + 2, SLOTS, width), F32),
            pltpu.VMEM((halves * lines * time, chunk), BF16),
            pltpu.VMEM((chunk, halves * 2 * LANES), BF16),
            pltpu.VMEM((halves * 2 * LANES, chunk), BF16),
            pltpu.VMEM((SLOTS, chunk), F32),
        ],
        compiler_params=pltpu.CompilerParams(vmem_limit_bytes=24 * 1024 * 1024),
        cost_estimate=pl.CostEstimate(flops=4 * flops, bytes_accessed=4 * 1024 * 1024, transcendentals=time * SLOTS * chunk),
    )(
        after,
        *xs,
        seam,
        in_weight,
        conv,
        conv_bias,
        jnp.swapaxes(proj, 1, 2),
        step_weight,
        step_bias,
    )


def scan(axis, after, coefs, steps, u, decay_log, skip):
    time, _, chunk = steps.shape
    width, states = decay_log.shape[1:]
    vmem = pl.BlockSpec(memory_space=pltpu.VMEM)
    return pl.pallas_call(
        functools.partial(scan_kernel, axis),
        out_shape=jax.ShapeDtypeStruct((time * SLOTS, chunk), BF16),
        in_specs=[pl.BlockSpec(memory_space=pl.ANY), vmem, vmem, vmem, vmem, vmem],
        out_specs=vmem,
        scratch_shapes=[
            pltpu.VMEM((time, SLOTS, chunk), F32),
            pltpu.VMEM((time, SLOTS, chunk), F32),
            pltpu.VMEM((time, states, 2 * SLOTS, LANES), BF16),
        ],
        compiler_params=pltpu.CompilerParams(vmem_limit_bytes=(8 << 20) + time * (136 << 10) + time * 20 * chunk),
        cost_estimate=pl.CostEstimate(
            flops=8 * time * SLOTS * chunk * states,
            bytes_accessed=4 * 1024 * 1024,
            transcendentals=time * SLOTS * chunk * states,
        ),
    )(after, coefs, steps, u, jnp.swapaxes(decay_log, 1, 2), skip)


def end_kernel(columns, gate_ref, gain_ref, weight_ref, *refs):
    pair_refs, beside_ref, row_refs, out_ref, gated_ref = refs[:columns], refs[columns], refs[columns + 1 : -2], refs[-2], refs[-1]
    height, width, channels = out_ref.shape
    size = row_refs[0].shape[0]
    lines = size // width
    swap = flip("col") ^ lax.axis_index("col")
    turn = (flip("row") ^ lax.axis_index("row")) * (width // lax.axis_size("row"))
    row = rows_of(height * width)
    line = (row >> bits(width)) ^ (swap * lines)
    source = (((row & (width - 1)) ^ turn) << bits(height)) + line
    rows = jnp.concatenate([row_ref[...] for row_ref in row_refs], axis=0)
    blocks = []
    for part in range(columns):
        blocks += [pair_refs[part][0], beside_ref[part]]
    columns = jnp.concatenate(blocks, axis=0)
    combined = layer_norm(rows.astype(F32) + dot(one_hot([source], height * width), columns), gain_ref[...][None])
    for part in range(len(row_refs)):
        cells = pl.ds(pl.multiple_of((part ^ swap) * size, size), size)
        gate = gate_ref[cells].astype(F32)
        gated_ref[cells] = (combined[part * size : (part + 1) * size] * (gate / (1.0 + jnp.exp(-gate)))).astype(BF16)
    out = dot(gated_ref[...], weight_ref[...]).astype(BF16)
    out_ref[...] = out.reshape(height, width, channels)


def pair_kernel(*refs):
    count = len(refs) // 2
    own_refs, beside_ref, out_refs = refs[:count], refs[count], refs[count + 1 :]
    for k in range(count):
        out_refs[k][0] = own_refs[k][...]
        out_refs[k][1] = beside_ref[k + 1]


def first_kernel(own_ref, beside_ref, out_ref):
    out_ref[0] = own_ref[...]
    out_ref[1] = beside_ref[0]


def collect_kernel(after_ref, *refs):
    out_ref = refs[-1]
    for k in range(len(refs) - 1):
        out_ref[k] = refs[k][1]


def simple(kernel, shapes, *arrays, after=None):
    vmem = pl.BlockSpec(memory_space=pltpu.VMEM)
    first = [] if after is None else [after]
    many = isinstance(shapes, list)
    return pl.pallas_call(
        kernel,
        out_shape=shapes,
        in_specs=[pl.BlockSpec(memory_space=pl.ANY)] * len(first) + [vmem] * len(arrays),
        out_specs=[vmem] * len(shapes) if many else vmem,
        compiler_params=pltpu.CompilerParams(vmem_limit_bytes=4 * 1024 * 1024),
        cost_estimate=pl.CostEstimate(flops=0, bytes_accessed=2 << 20, transcendentals=0),
    )(*first, *arrays)


def swap(block, axis, k):
    return lax.ppermute(block, axis, [(i, i ^ k) for i in range(lax.axis_size(axis))])


def swap_out(own, beside):
    beside = swap(beside, "row", 1)
    shape = jax.ShapeDtypeStruct((2,) + own[0].shape, own[0].dtype)
    pairs = simple(pair_kernel, [shape] * (len(own) - 1), *own[1:], beside)
    found = {k: swap(pairs[k - 1], "row", 2 * k) for k in range(len(own) - 1, 0, -1)}
    first = simple(first_kernel, jax.ShapeDtypeStruct((2,) + own[0].shape, own[0].dtype), own[0], beside)
    return [first] + [found[k] for k in range(1, len(own))]


def swap_back_far(pairs):
    found = {k: swap(pairs[k], "row", 2 * k) for k in range(len(pairs) - 1, 0, -1)}
    return [pairs[0]] + [found[k] for k in range(1, len(pairs))]


def swap_blocks(blocks, axis):
    count = lax.axis_size(axis)
    found = {k: lax.ppermute(blocks[k], axis, [(i, i ^ k) for i in range(count)]) for k in range(count - 1, 0, -1)}
    return [blocks[0]] + [found[k] for k in range(1, count)]


def pick_kernel(axis, after_ref, *refs):
    x_refs, out_ref = views(refs[:-1], 3), refs[-1]
    place = lax.axis_index(axis) ^ flip(axis)
    line = jnp.where(place == 0, 1, x_refs[0].shape[0] - 2)
    for part, x_ref in enumerate(x_refs):
        out_ref[part] = x_ref[line]


def pick(axis, after, xs):
    return pl.pallas_call(
        functools.partial(pick_kernel, axis),
        out_shape=jax.ShapeDtypeStruct((lax.axis_size("col" if axis == "col" else "row"),) + xs[-1].shape[-2:], xs[-1].dtype),
        in_specs=[pl.BlockSpec(memory_space=pl.ANY)] + [pl.BlockSpec(memory_space=pltpu.VMEM)] * len(xs),
        out_specs=pl.BlockSpec(memory_space=pltpu.VMEM),
        compiler_params=pltpu.CompilerParams(vmem_limit_bytes=4 * 1024 * 1024),
    )(after, *xs)


def seam_of(axis, line):
    count = lax.axis_size(axis)
    height, breadth = lax.axis_size("row"), lax.axis_size("col")
    if axis == "row":
        at = lambda group: (0 if group & 1 else count - 1) * breadth
        ends = [(at(c) + c, at(c) + c + 1) for c in range(breadth - 1)]
    else:
        at = lambda group: 0 if group & 1 else count - 1
        ends = [(at(r) + r * breadth, at(r) + (r + 1) * breadth) for r in range(height - 1)]
    pairs = ends + [(b, a) for a, b in ends]
    return lax.ppermute(line, ("row", "col"), pairs)


def local(
    features,
    norm_gain,
    in_weight,
    conv_weight,
    conv_bias,
    proj_weight,
    step_weight,
    step_bias,
    decay_log,
    skip_gain,
    out_gain,
    out_weight,
):
    height, width, channels = features.shape
    inner = out_weight.shape[0]
    tokens = height * width
    row_lines = height // lax.axis_size("col")
    col_lines = width // lax.axis_size("row")

    rows, cols = lax.axis_size("row"), lax.axis_size("col")
    vmem = pl.BlockSpec(memory_space=pltpu.VMEM)
    normed, *sends = pl.pallas_call(
        functools.partial(cut_kernel, rows),
        out_shape=[jax.ShapeDtypeStruct((tokens, channels), BF16)]
        + [jax.ShapeDtypeStruct((col_lines + 2, height, channels), BF16)] * (rows // 2)
        + [jax.ShapeDtypeStruct((rows // 2, col_lines + 2, height, channels), BF16)]
        + [jax.ShapeDtypeStruct((row_lines + 2, width, channels), BF16)] * cols,
        in_specs=[pl.BlockSpec(features.shape, lambda: (0, 0, 0)), pl.BlockSpec((channels,), lambda: (0,))],
        out_specs=[vmem] * (2 + rows // 2 + cols),
        scratch_shapes=[pltpu.VMEM((tokens, channels), BF16)],
        compiler_params=pltpu.CompilerParams(vmem_limit_bytes=12 * 1024 * 1024),
        cost_estimate=pl.CostEstimate(flops=6_000_000_000, bytes_accessed=2 << 20, transcendentals=tokens),
    )(features, norm_gain)
    weights = (in_weight, conv_weight, conv_bias, proj_weight, step_weight, step_bias, decay_log, skip_gain)
    gate = pl.pallas_call(
        gate_kernel,
        out_shape=jax.ShapeDtypeStruct((tokens, inner), BF16),
        grid=(1,),
        in_specs=[
            pl.BlockSpec((tokens, channels), lambda i: (0, 0)),
            pl.BlockSpec((channels, inner), lambda i: (0, 1)),
        ],
        out_specs=pl.BlockSpec((tokens, inner), lambda i: (0, 0)),
        compiler_params=pltpu.CompilerParams(vmem_limit_bytes=12 * 1024 * 1024),
        cost_estimate=pl.CostEstimate(flops=2 * tokens * channels * inner, bytes_accessed=1 << 20, transcendentals=0),
    )(normed, in_weight)

    half = rows // 2
    row_x = swap_blocks(sends[half + 1 :], "col")
    col_x = swap_out(sends[:half], sends[half])
    row_seam = seam_of("col", pick("col", normed, row_x))
    row_steps = prepare("col", normed, row_x, row_seam, *weights)
    col_seam = seam_of("row", pick("row", row_steps[0], col_x))
    col_steps = prepare("row", row_steps[0], col_x, col_seam, *weights)
    col_y = scan("row", normed, *col_steps, decay_log, skip_gain)
    joined = join("row", col_y, rows, col_lines, height, inner, normed)
    col_y = swap_back_far(joined)
    row_y = scan("col", joined[0], *row_steps, decay_log, skip_gain)
    beside = jax.ShapeDtypeStruct((half,) + joined[0].shape[1:], BF16)
    beside = simple(collect_kernel, beside, *col_y, after=row_y)
    row_y = swap_blocks(join("col", row_y, cols, row_lines, width, inner, beside), "col")
    beside = swap(beside, "row", 1)
    return pl.pallas_call(
        functools.partial(end_kernel, half),
        out_shape=jax.ShapeDtypeStruct(features.shape, BF16),
        scratch_shapes=[pltpu.VMEM((tokens, inner), BF16)],
        compiler_params=pltpu.CompilerParams(vmem_limit_bytes=16 * 1024 * 1024),
    )(gate, out_gain, out_weight, *col_y, beside, *row_y)


def solution(mesh):
    in_specs = (P("row", "col", None), P(), P(), P(), P(), P(), P(), P(), P(), P(), P(), P())
    out_specs = P("row", "col", None)
    return jax.shard_map(local, mesh=mesh, in_specs=in_specs, out_specs=out_specs, check_vma=False)
```

```python
import functools

import jax
import jax.numpy as jnp
from jax import lax
from jax.experimental import pallas as pl
from jax.experimental.pallas import tpu as pltpu
from jax.sharding import PartitionSpec as P

F32 = jnp.float32
BF16 = jnp.bfloat16
LANES = 128
SLOTS = 8
LOG2E = 1.4426950408889634


def bits(value):
    assert value & (value - 1) == 0
    return value.bit_length() - 1


def one_hot(targets, width):
    lane = lax.broadcasted_iota(jnp.int32, targets[0].shape, 1)
    blocks = []
    for block in range(pl.cdiv(width, LANES)):
        hit = targets[0] == lane + block * LANES
        for other in targets[1:]:
            hit = jnp.logical_or(hit, other == lane + block * LANES)
        blocks.append(jnp.where(hit, 1.0, 0.0).astype(BF16))
    return jnp.concatenate(blocks, axis=1)[:, :width]


def rows_of(count, start=0):
    return lax.broadcasted_iota(jnp.int32, (count, LANES), 0) + start


def dot(a, b):
    return jnp.dot(a, b, preferred_element_type=F32)


def layer_norm(values, scale_gain):
    centred = values - jnp.mean(values, axis=-1, keepdims=True)
    spread = jnp.mean(centred * centred, axis=-1, keepdims=True)
    return centred * lax.rsqrt(spread + 1e-05) * scale_gain


def flip(axis):
    other = "col" if axis == "row" else "row"
    return (lax.axis_index(other) & 1) * (lax.axis_size(axis) - 1)


def cut_kernel(columns, feat_ref, gain_ref, norm_ref, *refs):
    col_refs, beside_ref, row_refs, turned_ref = refs[: columns // 2], refs[columns // 2], refs[columns // 2 + 1 : -1], refs[-1]
    height, width, channels = feat_ref.shape
    tile = layer_norm(feat_ref[...].reshape(height * width, channels).astype(F32), gain_ref[...][None]).astype(BF16)
    norm_ref[...] = tile
    reach = row_refs[0].shape[0]
    turn = flip("col") ^ lax.axis_index("col")
    for part, row_ref in enumerate(row_refs):
        for line in range(reach):
            at = jnp.clip((part ^ turn) * (reach - 2) + line - 1, 0, height - 1)
            row_ref[line] = norm_ref[pl.ds(pl.multiple_of(at * width, width), width)]
    row = rows_of(height * width)
    turned = dot(one_hot([((row & (height - 1)) << bits(width)) + (row >> bits(height))], height * width), tile).astype(
        BF16
    )
    turned_ref[...] = turned
    reach = col_refs[0].shape[0]
    turn = flip("row") ^ lax.axis_index("row")
    for part in range(columns):
        for line in range(reach):
            at = jnp.clip((part ^ turn) * (reach - 2) + line - 1, 0, width - 1)
            found = turned_ref[pl.ds(pl.multiple_of(at * height, height), height)]
            if part & 1:
                beside_ref[part >> 1, line] = found
            else:
                col_refs[part >> 1][line] = found


def gate_kernel(norm_ref, weight_ref, gate_ref):
    gate_ref[...] = dot(norm_ref[...], weight_ref[...]).astype(BF16)


def views(refs, rank):
    found = []
    for ref in refs:
        found += [ref] if len(ref.shape) == rank else [ref.at[k] for k in range(ref.shape[0])]
    return found


def by_slot(halves, rows):
    found = None
    for kind in range(halves * 2):
        row = rows(kind >> 1, kind & 1)
        row = jnp.broadcast_to(row, (SLOTS, row.shape[1]))
        slot = lax.broadcasted_iota(jnp.int32, row.shape, 0)
        found = row if found is None else jnp.where(slot >= kind * (SLOTS // (halves * 2)), row, found)
    return found


def prepare_kernel(
    lines,
    axis,
    after_ref,
    *refs,
):
    x_refs, refs = views(refs[:-16], 3), refs[-16:]
    (
        seam_ref,
        weight_ref,
        conv_ref,
        conv_bias_ref,
        proj_raw_ref,
        step_raw_ref,
        bias_raw_ref,
        proj_out_ref,
        s_ref,
        v_ref,
        token_ref,
        inner_ref,
        active_ref,
        proj_ref,
        step_ref,
        bias_ref,
    ) = refs
    ks = (0, 1) if axis == "col" else (2, 3)
    parts, length, channels = seam_ref.shape
    reach = lines + 2
    states = (proj_raw_ref.shape[1] - RANK) // 2
    time = parts * length
    low = time // SLOTS
    width = weight_ref.shape[1] // 2
    chunk = s_ref.shape[2]
    halves = width // chunk
    slot_lines = SLOTS // (2 * halves)
    if axis == "row":
        across_first = lambda across, along: (along, across)
    else:
        across_first = lambda across, along: (across, along)

    row = rows_of(time)
    source = ((row & 7) << bits(low)) + (row >> 3)
    source = source ^ (lax.axis_index(axis) << bits(length))
    order = one_hot([source], time)
    for line in range(reach):
        x = jnp.concatenate([x_ref[line] for x_ref in x_refs], axis=0)
        if line == 0 or line == reach - 1:
            place = lax.axis_index(axis) ^ flip(axis)
            missing = place == (0 if line == 0 else lax.axis_size(axis) - 1)
            x = jnp.where(missing, seam_ref[...].reshape(time, channels), x)
        token_ref[line * time : (line + 1) * time] = dot(order, x).astype(BF16)
    inner = dot(token_ref[...], weight_ref[:, :width]).astype(BF16).astype(F32)
    inner_ref[:, 1 : low + 1] = inner.reshape(reach, low, SLOTS, width)
    place = lax.broadcasted_iota(jnp.int32, (SLOTS, width), 0)
    for line in range(reach):
        inner_ref[line, 0] = jnp.where(place == 0, 0.0, pltpu.roll(inner_ref[line, low], 1, 0))
        inner_ref[line, low + 1] = jnp.where(place == SLOTS - 1, 0.0, pltpu.roll(inner_ref[line, 1], SLOTS - 1, 0))

    conv_bias = conv_bias_ref[...][None]

    def convolve(pair, _):
        for group in range(width // (2 * LANES)):
            cells = slice(group * 2 * LANES, (group + 1) * 2 * LANES)
            half = (group * 2 * LANES) // chunk
            base = group * 2 * LANES - half * chunk
            bias = jnp.broadcast_to(conv_bias[:, cells], (SLOTS, 2 * LANES))
            totals = [[bias for _ in range(2)] for _ in range(lines)]
            for across in range(3):
                for along in range(3):
                    first, second = across_first(across, along)
                    tap = jnp.broadcast_to(conv_ref[first, second : second + 1, cells], (SLOTS, 2 * LANES))
                    for line in range(lines):
                        for sub in range(2):
                            totals[line][sub] += inner_ref[line + across, 2 * pair + sub + along, :, cells] * tap
            for line in range(lines):
                value = jnp.concatenate(totals[line], axis=0)
                value = 0.5 * value
                value = value * jnp.tanh(value) + value
                value = value.astype(BF16)
                for piece in range(2):
                    at = base + piece * LANES
                    start = ((half + at // chunk) * lines + line) * time
                    start = pl.multiple_of(start + pair * (2 * SLOTS), 2 * SLOTS)
                    active_ref[pl.ds(start, 2 * SLOTS), at % chunk : at % chunk + LANES] = value[
                        :, piece * LANES : (piece + 1) * LANES
                    ]
        return 0

    lax.fori_loop(0, low // 2, convolve, 0)

    bias_ref[...] = by_slot(halves, lambda half, way: bias_raw_ref[ks[way] : ks[way] + 1, half * chunk : (half + 1) * chunk])
    for half in range(halves):
        cells = slice(half * chunk, (half + 1) * chunk)
        for way in range(2):
            kind = slice((half * 2 + way) * LANES, (half * 2 + way + 1) * LANES)
            w = proj_raw_ref[ks[way], :, cells].astype(F32)
            ranks = w[:RANK]
            rest = jnp.zeros((LANES - 3 * RANK - 2 * states, chunk), F32)
            w = jnp.concatenate([ranks, ranks, ranks, w[RANK:], rest], axis=0)
            proj_ref[:, kind] = w.T.astype(BF16)
            w = step_raw_ref[ks[way], :, cells]
            high = w.astype(BF16).astype(F32)
            rest = jnp.zeros((LANES - 3 * RANK, chunk), F32)
            step_ref[kind, :] = jnp.concatenate([high, high, w - high, rest], axis=0).astype(BF16)

    piece = 512
    for first in range(0, time * SLOTS, piece):
        row = rows_of(piece, first)
        now = row >> 3
        slot = row & 7
        line = slot & (slot_lines - 1)
        back = (slot >> bits(slot_lines)) & 1
        half = slot >> bits(2 * slot_lines)
        when = jnp.where(back == 1, time - 1 - now, now)
        source = half * (lines * time) + line * time + ((when & (low - 1)) << 3) + (when >> bits(low))
        if slot_lines > lines:
            source = jnp.where(line < lines, source, -1)
        u = dot(one_hot([source], halves * lines * time), active_ref[...])
        steps = pl.ds(first // SLOTS, piece // SLOTS)
        v_ref[steps] = u.reshape(piece // SLOTS, SLOTS, chunk)
        kind = slot >> bits(slot_lines)
        projected = dot(u.astype(BF16), proj_ref[...])
        p = projected[:, :LANES]
        for other in range(1, 2 * halves):
            p = jnp.where(kind == other, projected[:, other * LANES : (other + 1) * LANES], p)
        if halves == 2:
            p = p.reshape(piece // SLOTS, SLOTS, LANES)
            p = p + pltpu.roll(p, SLOTS // 2, 1)
            p = p.reshape(piece, LANES)
        proj_out_ref[steps] = p.reshape(piece // SLOTS, SLOTS, LANES)
        high = p.astype(BF16).astype(F32)
        lane = lax.broadcasted_iota(jnp.int32, p.shape, 1)
        mixed = jnp.where(jnp.logical_and(lane >= RANK, lane < 2 * RANK), p - high, high)
        stacked = jnp.concatenate([jnp.where(kind == k, mixed, 0.0).astype(BF16) for k in range(2 * halves)], axis=1)
        s_ref[steps] = dot(stacked, step_ref[...]).reshape(piece // SLOTS, SLOTS, chunk)

    def soften(lap, _):
        for sub in range(8):
            t = lap * 8 + sub
            for g in range(chunk // LANES):
                cells = slice(g * LANES, (g + 1) * LANES)
                before = s_ref[t, :, cells] + bias_ref[:, cells]
                small = jnp.exp(-jnp.abs(before))
                log1p = jnp.where(small < 0.001, small - 0.5 * small * small, jnp.log(1.0 + small))
                step = jnp.maximum(before, 0.0) + log1p
                s_ref[t, :, cells] = step
        return 0

    lax.fori_loop(0, time // 8, soften, 0)


def scan_kernel(
    axis,
    after_ref,
    coef_ref,
    s_ref,
    u_ref,
    decay_ref,
    skip_raw_ref,
    out_ref,
    v_ref,
    y_ref,
    spread_ref,
):
    time, _, chunk = s_ref.shape
    halves = decay_ref.shape[2] // chunk
    states = decay_ref.shape[1]
    groups = chunk // LANES
    at_once = 4 if groups > 3 else 8
    unroll = 32 if axis == "col" else 16
    laps = time // unroll

    ks = (0, 1) if axis == "col" else (2, 3)
    piece = 64
    row = lax.broadcasted_iota(jnp.int32, (2 * LANES, LANES), 0) & (LANES - 1)
    taken = [jnp.where(row == 3 * RANK + n, 1.0, 0.0).astype(BF16) for n in range(2 * states)]

    def spread(lap, _):
        steps = pl.ds(lap * piece, piece)
        coefs = coef_ref[steps].reshape(piece * SLOTS, LANES)
        high = coefs.astype(BF16)
        both = jnp.concatenate([high, (coefs - high.astype(F32)).astype(BF16)], axis=1)
        for n in range(0, 2 * states, 4):
            found = dot(both, jnp.concatenate(taken[n : n + 4], axis=1))
            for k in range(4):
                spread_ref[steps, n + k] = found[:, k * LANES : (k + 1) * LANES].reshape(piece, SLOTS, LANES)
        return 0

    lax.fori_loop(0, time // piece, spread, 0)
    for first in range(0, states, at_once):
        rates = []
        for n in range(first, first + at_once):
            rates.append([])
            for g in range(groups):
                rate = by_slot(
                    halves,
                    lambda half, way: decay_ref[ks[way], n : n + 1, half * chunk + g * LANES : half * chunk + (g + 1) * LANES],
                )
                rates[-1].append(-LOG2E * jnp.exp(rate))
        if first == 0:
            skips = [
                by_slot(
                    halves,
                    lambda half, way: skip_raw_ref[
                        ks[way] : ks[way] + 1, half * chunk + g * LANES : half * chunk + (g + 1) * LANES
                    ],
                )
                for g in range(groups)
            ]

        def advance(lap, hidden):
            hidden = list(hidden)
            for sub in range(unroll):
                t = lap * unroll + sub
                enter = [spread_ref[t, first + n] for n in range(at_once)]
                leave = [spread_ref[t, states + first + n] for n in range(at_once)]
                decay = []
                for g in range(groups):
                    step = s_ref[t, :, g * LANES : (g + 1) * LANES]
                    decay.append([jnp.exp2(step * rates[n][g]) for n in range(at_once)])
                for g in range(groups):
                    cells = pl.ds(g * LANES, LANES)
                    if first == 0:
                        u = u_ref[t, :, cells]
                        value = s_ref[t, :, cells] * u
                        v_ref[t, :, cells] = value
                        y = skips[g] * u
                    else:
                        value = v_ref[t, :, cells]
                        y = y_ref[t, :, cells]
                    for n in range(at_once):
                        k = n * groups + g
                        h = decay[g][n] * hidden[k] + value * enter[n]
                        hidden[k] = h
                        y = y + h * leave[n]
                    y_ref[t, :, cells] = y
            return tuple(hidden)

        zero = jnp.zeros((SLOTS, LANES), F32)
        lax.fori_loop(0, laps, advance, (zero,) * (at_once * groups))

    out_ref[...] = y_ref[...].reshape(time * SLOTS, chunk).astype(BF16)


def join_kernel(parts, lines, axis, after_ref, scanned_ref, *out_refs):
    length = out_refs[0].shape[-2] // lines
    time = parts * length
    chunk = scanned_ref.shape[1]
    halves = out_refs[0].shape[-1] // chunk
    slot_lines = SLOTS // (2 * halves)
    row = rows_of(lines * time)
    line = (row >> bits(length)) & (lines - 1)
    part = row >> bits(lines * length)
    part = part ^ lax.axis_index(axis)
    now = (part << bits(length)) + (row & (length - 1))
    for half in range(halves):
        ahead = now * SLOTS + (half * 2 * slot_lines) + line
        behind = (time - 1 - now) * SLOTS + (half * 2 * slot_lines + slot_lines) + line
        joined = dot(one_hot([ahead, behind], time * SLOTS), scanned_ref[...]).astype(BF16)
        size = lines * length
        for part in range(parts):
            found = joined[part * size : (part + 1) * size]
            if len(out_refs) < parts:
                out_refs[part >> 1][part & 1, :, half * chunk : (half + 1) * chunk] = found
            else:
                out_refs[part][:, half * chunk : (half + 1) * chunk] = found


def join(axis, scanned, parts, lines, length, width, after):
    size = (lines * length, width)
    shapes = [size] * parts if axis == "col" else [(2,) + size] * (parts // 2)
    return pl.pallas_call(
        functools.partial(join_kernel, parts, lines, axis),
        out_shape=[jax.ShapeDtypeStruct(shape, BF16) for shape in shapes],
        in_specs=[pl.BlockSpec(memory_space=pl.ANY), pl.BlockSpec(memory_space=pltpu.VMEM)],
        out_specs=[pl.BlockSpec(memory_space=pltpu.VMEM)] * len(shapes),
        compiler_params=pltpu.CompilerParams(vmem_limit_bytes=24 * 1024 * 1024),
    )(after, scanned)


RANK = 24


def prepare(axis, after, xs, seam, in_weight, conv, conv_bias, proj, step_weight, step_bias, decay_log, skip):
    parts, length, channels = seam.shape
    reach = xs[0].shape[-3]
    lines = reach - 2
    time = parts * length
    width = conv.shape[2]
    states = decay_log.shape[2]
    assert step_weight.shape[1] == RANK and in_weight.shape[1] == 2 * width
    halves = 1 if lines >= 4 else 2
    assert lines <= SLOTS // (2 * halves)
    chunk = width // halves
    vmem = pl.BlockSpec(memory_space=pltpu.VMEM)
    flops = 2 * time * (reach * channels * width + SLOTS * width * 256)
    return pl.pallas_call(
        functools.partial(prepare_kernel, lines, axis),
        out_shape=[
            jax.ShapeDtypeStruct((time, SLOTS, LANES), F32),
            jax.ShapeDtypeStruct((time, SLOTS, chunk), F32),
            jax.ShapeDtypeStruct((time, SLOTS, chunk), F32),
        ],
        in_specs=[pl.BlockSpec(memory_space=pl.ANY)] + [vmem] * (len(xs) + 7),
        out_specs=[vmem, vmem, vmem],
        scratch_shapes=[
            pltpu.VMEM((reach * time, channels), BF16),
            pltpu.VMEM((reach, time // SLOTS + 2, SLOTS, width), F32),
            pltpu.VMEM((halves * lines * time, chunk), BF16),
            pltpu.VMEM((chunk, halves * 2 * LANES), BF16),
            pltpu.VMEM((halves * 2 * LANES, chunk), BF16),
            pltpu.VMEM((SLOTS, chunk), F32),
        ],
        compiler_params=pltpu.CompilerParams(vmem_limit_bytes=24 * 1024 * 1024),
        cost_estimate=pl.CostEstimate(flops=4 * flops, bytes_accessed=4 * 1024 * 1024, transcendentals=time * SLOTS * chunk),
    )(
        after,
        *xs,
        seam,
        in_weight,
        conv,
        conv_bias,
        jnp.swapaxes(proj, 1, 2),
        step_weight,
        step_bias,
    )


def scan(axis, after, coefs, steps, u, decay_log, skip):
    time, _, chunk = steps.shape
    width, states = decay_log.shape[1:]
    vmem = pl.BlockSpec(memory_space=pltpu.VMEM)
    return pl.pallas_call(
        functools.partial(scan_kernel, axis),
        out_shape=jax.ShapeDtypeStruct((time * SLOTS, chunk), BF16),
        in_specs=[pl.BlockSpec(memory_space=pl.ANY), vmem, vmem, vmem, vmem, vmem],
        out_specs=vmem,
        scratch_shapes=[
            pltpu.VMEM((time, SLOTS, chunk), F32),
            pltpu.VMEM((time, SLOTS, chunk), F32),
            pltpu.VMEM((time, 2 * states, SLOTS, LANES), F32),
        ],
        compiler_params=pltpu.CompilerParams(vmem_limit_bytes=(8 << 20) + time * (136 << 10) + time * 20 * chunk),
        cost_estimate=pl.CostEstimate(
            flops=8 * time * SLOTS * chunk * states,
            bytes_accessed=4 * 1024 * 1024,
            transcendentals=time * SLOTS * chunk * states,
        ),
    )(after, coefs, steps, u, jnp.swapaxes(decay_log, 1, 2), skip)


def end_kernel(columns, gate_ref, gain_ref, weight_ref, *refs):
    pair_refs, beside_ref, row_refs, out_ref, gated_ref = refs[:columns], refs[columns], refs[columns + 1 : -2], refs[-2], refs[-1]
    height, width, channels = out_ref.shape
    size = row_refs[0].shape[0]
    lines = size // width
    swap = flip("col") ^ lax.axis_index("col")
    turn = (flip("row") ^ lax.axis_index("row")) * (width // lax.axis_size("row"))
    row = rows_of(height * width)
    line = (row >> bits(width)) ^ (swap * lines)
    source = (((row & (width - 1)) ^ turn) << bits(height)) + line
    rows = jnp.concatenate([row_ref[...] for row_ref in row_refs], axis=0)
    blocks = []
    for part in range(columns):
        blocks += [pair_refs[part][0], beside_ref[part]]
    columns = jnp.concatenate(blocks, axis=0)
    combined = layer_norm(rows.astype(F32) + dot(one_hot([source], height * width), columns), gain_ref[...][None])
    for part in range(len(row_refs)):
        cells = pl.ds(pl.multiple_of((part ^ swap) * size, size), size)
        gate = gate_ref[cells].astype(F32)
        gated_ref[cells] = (combined[part * size : (part + 1) * size] * (gate / (1.0 + jnp.exp(-gate)))).astype(BF16)
    out = dot(gated_ref[...], weight_ref[...]).astype(BF16)
    out_ref[...] = out.reshape(height, width, channels)


def pair_kernel(*refs):
    count = len(refs) // 2
    own_refs, beside_ref, out_refs = refs[:count], refs[count], refs[count + 1 :]
    for k in range(count):
        out_refs[k][0] = own_refs[k][...]
        out_refs[k][1] = beside_ref[k + 1]


def first_kernel(own_ref, beside_ref, out_ref):
    out_ref[0] = own_ref[...]
    out_ref[1] = beside_ref[0]


def collect_kernel(after_ref, *refs):
    out_ref = refs[-1]
    for k in range(len(refs) - 1):
        out_ref[k] = refs[k][1]


def simple(kernel, shapes, *arrays, after=None):
    vmem = pl.BlockSpec(memory_space=pltpu.VMEM)
    first = [] if after is None else [after]
    many = isinstance(shapes, list)
    return pl.pallas_call(
        kernel,
        out_shape=shapes,
        in_specs=[pl.BlockSpec(memory_space=pl.ANY)] * len(first) + [vmem] * len(arrays),
        out_specs=[vmem] * len(shapes) if many else vmem,
        compiler_params=pltpu.CompilerParams(vmem_limit_bytes=4 * 1024 * 1024),
        cost_estimate=pl.CostEstimate(flops=0, bytes_accessed=2 << 20, transcendentals=0),
    )(*first, *arrays)


def swap(block, axis, k):
    return lax.ppermute(block, axis, [(i, i ^ k) for i in range(lax.axis_size(axis))])


def swap_out(own, beside):
    beside = swap(beside, "row", 1)
    shape = jax.ShapeDtypeStruct((2,) + own[0].shape, own[0].dtype)
    pairs = simple(pair_kernel, [shape] * (len(own) - 1), *own[1:], beside)
    found = {k: swap(pairs[k - 1], "row", 2 * k) for k in range(len(own) - 1, 0, -1)}
    first = simple(first_kernel, jax.ShapeDtypeStruct((2,) + own[0].shape, own[0].dtype), own[0], beside)
    return [first] + [found[k] for k in range(1, len(own))]


def swap_back_far(pairs):
    found = {k: swap(pairs[k], "row", 2 * k) for k in range(len(pairs) - 1, 0, -1)}
    return [pairs[0]] + [found[k] for k in range(1, len(pairs))]


def swap_blocks(blocks, axis):
    count = lax.axis_size(axis)
    found = {k: lax.ppermute(blocks[k], axis, [(i, i ^ k) for i in range(count)]) for k in range(count - 1, 0, -1)}
    return [blocks[0]] + [found[k] for k in range(1, count)]


def pick_kernel(axis, after_ref, *refs):
    x_refs, out_ref = views(refs[:-1], 3), refs[-1]
    place = lax.axis_index(axis) ^ flip(axis)
    line = jnp.where(place == 0, 1, x_refs[0].shape[0] - 2)
    for part, x_ref in enumerate(x_refs):
        out_ref[part] = x_ref[line]


def pick(axis, after, xs):
    return pl.pallas_call(
        functools.partial(pick_kernel, axis),
        out_shape=jax.ShapeDtypeStruct((lax.axis_size("col" if axis == "col" else "row"),) + xs[-1].shape[-2:], xs[-1].dtype),
        in_specs=[pl.BlockSpec(memory_space=pl.ANY)] + [pl.BlockSpec(memory_space=pltpu.VMEM)] * len(xs),
        out_specs=pl.BlockSpec(memory_space=pltpu.VMEM),
        compiler_params=pltpu.CompilerParams(vmem_limit_bytes=4 * 1024 * 1024),
    )(after, *xs)


def seam_of(axis, line):
    count = lax.axis_size(axis)
    height, breadth = lax.axis_size("row"), lax.axis_size("col")
    if axis == "row":
        at = lambda group: (0 if group & 1 else count - 1) * breadth
        ends = [(at(c) + c, at(c) + c + 1) for c in range(breadth - 1)]
    else:
        at = lambda group: 0 if group & 1 else count - 1
        ends = [(at(r) + r * breadth, at(r) + (r + 1) * breadth) for r in range(height - 1)]
    pairs = ends + [(b, a) for a, b in ends]
    return lax.ppermute(line, ("row", "col"), pairs)


def local(
    features,
    norm_gain,
    in_weight,
    conv_weight,
    conv_bias,
    proj_weight,
    step_weight,
    step_bias,
    decay_log,
    skip_gain,
    out_gain,
    out_weight,
):
    height, width, channels = features.shape
    inner = out_weight.shape[0]
    tokens = height * width
    row_lines = height // lax.axis_size("col")
    col_lines = width // lax.axis_size("row")

    rows, cols = lax.axis_size("row"), lax.axis_size("col")
    vmem = pl.BlockSpec(memory_space=pltpu.VMEM)
    normed, *sends = pl.pallas_call(
        functools.partial(cut_kernel, rows),
        out_shape=[jax.ShapeDtypeStruct((tokens, channels), BF16)]
        + [jax.ShapeDtypeStruct((col_lines + 2, height, channels), BF16)] * (rows // 2)
        + [jax.ShapeDtypeStruct((rows // 2, col_lines + 2, height, channels), BF16)]
        + [jax.ShapeDtypeStruct((row_lines + 2, width, channels), BF16)] * cols,
        in_specs=[pl.BlockSpec(features.shape, lambda: (0, 0, 0)), pl.BlockSpec((channels,), lambda: (0,))],
        out_specs=[vmem] * (2 + rows // 2 + cols),
        scratch_shapes=[pltpu.VMEM((tokens, channels), BF16)],
        compiler_params=pltpu.CompilerParams(vmem_limit_bytes=12 * 1024 * 1024),
        cost_estimate=pl.CostEstimate(flops=6_000_000_000, bytes_accessed=2 << 20, transcendentals=tokens),
    )(features, norm_gain)
    weights = (in_weight, conv_weight, conv_bias, proj_weight, step_weight, step_bias, decay_log, skip_gain)
    gate = pl.pallas_call(
        gate_kernel,
        out_shape=jax.ShapeDtypeStruct((tokens, inner), BF16),
        grid=(1,),
        in_specs=[
            pl.BlockSpec((tokens, channels), lambda i: (0, 0)),
            pl.BlockSpec((channels, inner), lambda i: (0, 1)),
        ],
        out_specs=pl.BlockSpec((tokens, inner), lambda i: (0, 0)),
        compiler_params=pltpu.CompilerParams(vmem_limit_bytes=12 * 1024 * 1024),
        cost_estimate=pl.CostEstimate(flops=2 * tokens * channels * inner, bytes_accessed=1 << 20, transcendentals=0),
    )(normed, in_weight)

    half = rows // 2
    row_x = swap_blocks(sends[half + 1 :], "col")
    col_x = swap_out(sends[:half], sends[half])
    row_seam = seam_of("col", pick("col", normed, row_x))
    row_steps = prepare("col", normed, row_x, row_seam, *weights)
    col_seam = seam_of("row", pick("row", row_steps[0], col_x))
    col_steps = prepare("row", row_steps[0], col_x, col_seam, *weights)
    col_y = scan("row", normed, *col_steps, decay_log, skip_gain)
    joined = join("row", col_y, rows, col_lines, height, inner, normed)
    col_y = swap_back_far(joined)
    row_y = scan("col", joined[0], *row_steps, decay_log, skip_gain)
    beside = jax.ShapeDtypeStruct((half,) + joined[0].shape[1:], BF16)
    beside = simple(collect_kernel, beside, *col_y, after=row_y)
    row_y = swap_blocks(join("col", row_y, cols, row_lines, width, inner, beside), "col")
    beside = swap(beside, "row", 1)
    return pl.pallas_call(
        functools.partial(end_kernel, half),
        out_shape=jax.ShapeDtypeStruct(features.shape, BF16),
        scratch_shapes=[pltpu.VMEM((tokens, inner), BF16)],
        compiler_params=pltpu.CompilerParams(vmem_limit_bytes=16 * 1024 * 1024),
    )(gate, out_gain, out_weight, *col_y, beside, *row_y)


def solution(mesh):
    in_specs = (P("row", "col", None), P(), P(), P(), P(), P(), P(), P(), P(), P(), P(), P())
    out_specs = P("row", "col", None)
    return jax.shard_map(local, mesh=mesh, in_specs=in_specs, out_specs=out_specs, check_vma=False)
```

```python
import functools

import jax
import jax.numpy as jnp
from jax import lax
from jax.experimental import pallas as pl
from jax.experimental.pallas import tpu as pltpu
from jax.sharding import PartitionSpec as P

F32 = jnp.float32
BF16 = jnp.bfloat16
LANES = 128
SLOTS = 8
LOG2E = 1.4426950408889634


def bits(value):
    assert value & (value - 1) == 0
    return value.bit_length() - 1


def one_hot(targets, width):
    lane = lax.broadcasted_iota(jnp.int32, targets[0].shape, 1)
    blocks = []
    for block in range(pl.cdiv(width, LANES)):
        hit = targets[0] == lane + block * LANES
        for other in targets[1:]:
            hit = jnp.logical_or(hit, other == lane + block * LANES)
        blocks.append(jnp.where(hit, 1.0, 0.0).astype(BF16))
    return jnp.concatenate(blocks, axis=1)[:, :width]


def rows_of(count, start=0):
    return lax.broadcasted_iota(jnp.int32, (count, LANES), 0) + start


def dot(a, b):
    return jnp.dot(a, b, preferred_element_type=F32)


def layer_norm(values, scale_gain):
    centred = values - jnp.mean(values, axis=-1, keepdims=True)
    spread = jnp.mean(centred * centred, axis=-1, keepdims=True)
    return centred * lax.rsqrt(spread + 1e-05) * scale_gain


def flip(axis):
    other = "col" if axis == "row" else "row"
    return (lax.axis_index(other) & 1) * (lax.axis_size(axis) - 1)


def cut_kernel(columns, feat_ref, gain_ref, norm_ref, *refs):
    col_refs, beside_ref, row_refs, turned_ref = refs[: columns // 2], refs[columns // 2], refs[columns // 2 + 1 : -1], refs[-1]
    height, width, channels = feat_ref.shape
    tile = layer_norm(feat_ref[...].reshape(height * width, channels).astype(F32), gain_ref[...][None]).astype(BF16)
    norm_ref[...] = tile
    reach = row_refs[0].shape[0]
    turn = flip("col") ^ lax.axis_index("col")
    for part, row_ref in enumerate(row_refs):
        for line in range(reach):
            at = jnp.clip((part ^ turn) * (reach - 2) + line - 1, 0, height - 1)
            row_ref[line] = norm_ref[pl.ds(pl.multiple_of(at * width, width), width)]
    row = rows_of(height * width)
    turned = dot(one_hot([((row & (height - 1)) << bits(width)) + (row >> bits(height))], height * width), tile).astype(
        BF16
    )
    turned_ref[...] = turned
    reach = col_refs[0].shape[0]
    turn = flip("row") ^ lax.axis_index("row")
    for part in range(columns):
        for line in range(reach):
            at = jnp.clip((part ^ turn) * (reach - 2) + line - 1, 0, width - 1)
            found = turned_ref[pl.ds(pl.multiple_of(at * height, height), height)]
            if part & 1:
                beside_ref[part >> 1, line] = found
            else:
                col_refs[part >> 1][line] = found


def gate_kernel(norm_ref, weight_ref, gate_ref):
    gate_ref[...] = dot(norm_ref[...], weight_ref[...]).astype(BF16)


def views(refs, rank):
    found = []
    for ref in refs:
        found += [ref] if len(ref.shape) == rank else [ref.at[k] for k in range(ref.shape[0])]
    return found


def by_slot(halves, rows):
    found = None
    for kind in range(halves * 2):
        row = rows(kind >> 1, kind & 1)
        row = jnp.broadcast_to(row, (SLOTS, row.shape[1]))
        slot = lax.broadcasted_iota(jnp.int32, row.shape, 0)
        found = row if found is None else jnp.where(slot >= kind * (SLOTS // (halves * 2)), row, found)
    return found


def prepare_kernel(
    lines,
    axis,
    after_ref,
    *refs,
):
    x_refs, refs = views(refs[:-16], 3), refs[-16:]
    (
        seam_ref,
        weight_ref,
        conv_ref,
        conv_bias_ref,
        proj_raw_ref,
        step_raw_ref,
        bias_raw_ref,
        proj_out_ref,
        s_ref,
        v_ref,
        token_ref,
        inner_ref,
        active_ref,
        proj_ref,
        step_ref,
        bias_ref,
    ) = refs
    ks = (0, 1) if axis == "col" else (2, 3)
    parts, length, channels = seam_ref.shape
    reach = lines + 2
    states = (proj_raw_ref.shape[1] - RANK) // 2
    time = parts * length
    low = time // SLOTS
    width = weight_ref.shape[1] // 2
    chunk = s_ref.shape[2]
    halves = width // chunk
    slot_lines = SLOTS // (2 * halves)
    if axis == "row":
        across_first = lambda across, along: (along, across)
    else:
        across_first = lambda across, along: (across, along)

    row = rows_of(time)
    source = ((row & 7) << bits(low)) + (row >> 3)
    source = source ^ (lax.axis_index(axis) << bits(length))
    order = one_hot([source], time)
    for line in range(reach):
        x = jnp.concatenate([x_ref[line] for x_ref in x_refs], axis=0)
        if line == 0 or line == reach - 1:
            place = lax.axis_index(axis) ^ flip(axis)
            missing = place == (0 if line == 0 else lax.axis_size(axis) - 1)
            x = jnp.where(missing, seam_ref[...].reshape(time, channels), x)
        token_ref[line * time : (line + 1) * time] = dot(order, x).astype(BF16)
    inner = dot(token_ref[...], weight_ref[:, :width]).astype(BF16).astype(F32)
    inner_ref[:, 1 : low + 1] = inner.reshape(reach, low, SLOTS, width)
    place = lax.broadcasted_iota(jnp.int32, (SLOTS, width), 0)
    for line in range(reach):
        inner_ref[line, 0] = jnp.where(place == 0, 0.0, pltpu.roll(inner_ref[line, low], 1, 0))
        inner_ref[line, low + 1] = jnp.where(place == SLOTS - 1, 0.0, pltpu.roll(inner_ref[line, 1], SLOTS - 1, 0))

    conv_bias = conv_bias_ref[...][None]

    def convolve(pair, _):
        for group in range(width // (2 * LANES)):
            cells = slice(group * 2 * LANES, (group + 1) * 2 * LANES)
            half = (group * 2 * LANES) // chunk
            base = group * 2 * LANES - half * chunk
            bias = jnp.broadcast_to(conv_bias[:, cells], (SLOTS, 2 * LANES))
            totals = [[bias for _ in range(2)] for _ in range(lines)]
            for across in range(3):
                for along in range(3):
                    first, second = across_first(across, along)
                    tap = jnp.broadcast_to(conv_ref[first, second : second + 1, cells], (SLOTS, 2 * LANES))
                    for line in range(lines):
                        for sub in range(2):
                            totals[line][sub] += inner_ref[line + across, 2 * pair + sub + along, :, cells] * tap
            for line in range(lines):
                value = jnp.concatenate(totals[line], axis=0)
                value = 0.5 * value
                value = value * jnp.tanh(value) + value
                value = value.astype(BF16)
                for piece in range(2):
                    at = base + piece * LANES
                    start = ((half + at // chunk) * lines + line) * time
                    start = pl.multiple_of(start + pair * (2 * SLOTS), 2 * SLOTS)
                    active_ref[pl.ds(start, 2 * SLOTS), at % chunk : at % chunk + LANES] = value[
                        :, piece * LANES : (piece + 1) * LANES
                    ]
        return 0

    lax.fori_loop(0, low // 2, convolve, 0)

    bias_ref[...] = by_slot(halves, lambda half, way: bias_raw_ref[ks[way] : ks[way] + 1, half * chunk : (half + 1) * chunk])
    for half in range(halves):
        cells = slice(half * chunk, (half + 1) * chunk)
        for way in range(2):
            kind = slice((half * 2 + way) * LANES, (half * 2 + way + 1) * LANES)
            w = proj_raw_ref[ks[way], :, cells].astype(F32)
            ranks = w[:RANK]
            rest = jnp.zeros((LANES - 3 * RANK - 2 * states, chunk), F32)
            w = jnp.concatenate([ranks, ranks, ranks, w[RANK:], rest], axis=0)
            proj_ref[:, kind] = w.T.astype(BF16)
            w = step_raw_ref[ks[way], :, cells]
            high = w.astype(BF16).astype(F32)
            rest = jnp.zeros((LANES - 3 * RANK, chunk), F32)
            step_ref[kind, :] = jnp.concatenate([high, high, w - high, rest], axis=0).astype(BF16)

    piece = min(1024, time * SLOTS)
    for first in range(0, time * SLOTS, piece):
        row = rows_of(piece, first)
        now = row >> 3
        slot = row & 7
        line = slot & (slot_lines - 1)
        back = (slot >> bits(slot_lines)) & 1
        half = slot >> bits(2 * slot_lines)
        when = jnp.where(back == 1, time - 1 - now, now)
        source = half * (lines * time) + line * time + ((when & (low - 1)) << 3) + (when >> bits(low))
        if slot_lines > lines:
            source = jnp.where(line < lines, source, -1)
        u = dot(one_hot([source], halves * lines * time), active_ref[...])
        steps = pl.ds(first // SLOTS, piece // SLOTS)
        v_ref[steps] = u.reshape(piece // SLOTS, SLOTS, chunk)
        kind = slot >> bits(slot_lines)
        projected = dot(u.astype(BF16), proj_ref[...])
        p = projected[:, :LANES]
        for other in range(1, 2 * halves):
            p = jnp.where(kind == other, projected[:, other * LANES : (other + 1) * LANES], p)
        if halves == 2:
            p = p.reshape(piece // SLOTS, SLOTS, LANES)
            p = p + pltpu.roll(p, SLOTS // 2, 1)
            p = p.reshape(piece, LANES)
        proj_out_ref[steps] = p.reshape(piece // SLOTS, SLOTS, LANES)
        high = p.astype(BF16).astype(F32)
        lane = lax.broadcasted_iota(jnp.int32, p.shape, 1)
        mixed = jnp.where(jnp.logical_and(lane >= RANK, lane < 2 * RANK), p - high, high)
        stacked = jnp.concatenate([jnp.where(kind == k, mixed, 0.0).astype(BF16) for k in range(2 * halves)], axis=1)
        s_ref[steps] = dot(stacked, step_ref[...]).reshape(piece // SLOTS, SLOTS, chunk)

    def soften(lap, _):
        for sub in range(8):
            t = lap * 8 + sub
            for g in range(chunk // LANES):
                cells = slice(g * LANES, (g + 1) * LANES)
                before = s_ref[t, :, cells] + bias_ref[:, cells]
                small = jnp.exp(-jnp.abs(before))
                log1p = jnp.where(small < 0.001, small - 0.5 * small * small, jnp.log(1.0 + small))
                step = jnp.maximum(before, 0.0) + log1p
                s_ref[t, :, cells] = step
        return 0

    lax.fori_loop(0, time // 8, soften, 0)


def scan_kernel(
    axis,
    after_ref,
    coef_ref,
    s_ref,
    u_ref,
    decay_ref,
    skip_raw_ref,
    out_ref,
    v_ref,
    y_ref,
    spread_ref,
):
    time, _, chunk = s_ref.shape
    halves = decay_ref.shape[2] // chunk
    states = decay_ref.shape[1]
    groups = chunk // LANES
    at_once = 4
    unroll = 32
    laps = time // unroll

    ks = (0, 1) if axis == "col" else (2, 3)
    piece = 64
    row = lax.broadcasted_iota(jnp.int32, (2 * LANES, LANES), 0) & (LANES - 1)
    taken = [jnp.where(row == 3 * RANK + n, 1.0, 0.0).astype(BF16) for n in range(2 * states)]

    def spread(lap, _):
        steps = pl.ds(lap * piece, piece)
        coefs = coef_ref[steps].reshape(piece * SLOTS, LANES)
        high = coefs.astype(BF16)
        both = jnp.concatenate([high, (coefs - high.astype(F32)).astype(BF16)], axis=1)
        for n in range(0, 2 * states, 4):
            found = dot(both, jnp.concatenate(taken[n : n + 4], axis=1))
            for k in range(4):
                spread_ref[steps, n + k] = found[:, k * LANES : (k + 1) * LANES].reshape(piece, SLOTS, LANES)
        return 0

    lax.fori_loop(0, time // piece, spread, 0)
    for first in range(0, states, at_once):
        rates = []
        for n in range(first, first + at_once):
            rates.append([])
            for g in range(groups):
                rate = by_slot(
                    halves,
                    lambda half, way: decay_ref[ks[way], n : n + 1, half * chunk + g * LANES : half * chunk + (g + 1) * LANES],
                )
                rates[-1].append(-LOG2E * jnp.exp(rate))
        if first == 0:
            skips = [
                by_slot(
                    halves,
                    lambda half, way: skip_raw_ref[
                        ks[way] : ks[way] + 1, half * chunk + g * LANES : half * chunk + (g + 1) * LANES
                    ],
                )
                for g in range(groups)
            ]

        def advance(lap, hidden):
            hidden = list(hidden)
            for sub in range(unroll):
                t = lap * unroll + sub
                enter = [spread_ref[t, first + n] for n in range(at_once)]
                leave = [spread_ref[t, states + first + n] for n in range(at_once)]
                decay = []
                for g in range(groups):
                    step = s_ref[t, :, g * LANES : (g + 1) * LANES]
                    decay.append([jnp.exp2(step * rates[n][g]) for n in range(at_once)])
                for g in range(groups):
                    cells = pl.ds(g * LANES, LANES)
                    if first == 0:
                        u = u_ref[t, :, cells]
                        value = s_ref[t, :, cells] * u
                        v_ref[t, :, cells] = value
                        y = skips[g] * u
                    else:
                        value = v_ref[t, :, cells]
                        y = y_ref[t, :, cells]
                    for n in range(at_once):
                        k = n * groups + g
                        h = decay[g][n] * hidden[k] + value * enter[n]
                        hidden[k] = h
                        y = y + h * leave[n]
                    y_ref[t, :, cells] = y
            return tuple(hidden)

        zero = jnp.zeros((SLOTS, LANES), F32)
        lax.fori_loop(0, laps, advance, (zero,) * (at_once * groups))

    out_ref[...] = y_ref[...].reshape(time * SLOTS, chunk).astype(BF16)


def join_kernel(parts, lines, axis, after_ref, scanned_ref, *out_refs):
    length = out_refs[0].shape[-2] // lines
    time = parts * length
    chunk = scanned_ref.shape[1]
    halves = out_refs[0].shape[-1] // chunk
    slot_lines = SLOTS // (2 * halves)
    row = rows_of(lines * time)
    line = (row >> bits(length)) & (lines - 1)
    part = row >> bits(lines * length)
    part = part ^ lax.axis_index(axis)
    now = (part << bits(length)) + (row & (length - 1))
    for half in range(halves):
        ahead = now * SLOTS + (half * 2 * slot_lines) + line
        behind = (time - 1 - now) * SLOTS + (half * 2 * slot_lines + slot_lines) + line
        joined = dot(one_hot([ahead, behind], time * SLOTS), scanned_ref[...]).astype(BF16)
        size = lines * length
        for part in range(parts):
            found = joined[part * size : (part + 1) * size]
            if len(out_refs) < parts:
                out_refs[part >> 1][part & 1, :, half * chunk : (half + 1) * chunk] = found
            else:
                out_refs[part][:, half * chunk : (half + 1) * chunk] = found


def join(axis, scanned, parts, lines, length, width, after):
    size = (lines * length, width)
    shapes = [size] * parts if axis == "col" else [(2,) + size] * (parts // 2)
    return pl.pallas_call(
        functools.partial(join_kernel, parts, lines, axis),
        out_shape=[jax.ShapeDtypeStruct(shape, BF16) for shape in shapes],
        in_specs=[pl.BlockSpec(memory_space=pl.ANY), pl.BlockSpec(memory_space=pltpu.VMEM)],
        out_specs=[pl.BlockSpec(memory_space=pltpu.VMEM)] * len(shapes),
        compiler_params=pltpu.CompilerParams(vmem_limit_bytes=24 * 1024 * 1024),
    )(after, scanned)


RANK = 24


def prepare(axis, after, xs, seam, in_weight, conv, conv_bias, proj, step_weight, step_bias, decay_log, skip):
    parts, length, channels = seam.shape
    reach = xs[0].shape[-3]
    lines = reach - 2
    time = parts * length
    width = conv.shape[2]
    states = decay_log.shape[2]
    assert step_weight.shape[1] == RANK and in_weight.shape[1] == 2 * width
    halves = 1 if lines >= 4 else 2
    assert lines <= SLOTS // (2 * halves)
    chunk = width // halves
    vmem = pl.BlockSpec(memory_space=pltpu.VMEM)
    flops = 2 * time * (reach * channels * width + SLOTS * width * 256)
    return pl.pallas_call(
        functools.partial(prepare_kernel, lines, axis),
        out_shape=[
            jax.ShapeDtypeStruct((time, SLOTS, LANES), F32),
            jax.ShapeDtypeStruct((time, SLOTS, chunk), F32),
            jax.ShapeDtypeStruct((time, SLOTS, chunk), F32),
        ],
        in_specs=[pl.BlockSpec(memory_space=pl.ANY)] + [vmem] * (len(xs) + 7),
        out_specs=[vmem, vmem, vmem],
        scratch_shapes=[
            pltpu.VMEM((reach * time, channels), BF16),
            pltpu.VMEM((reach, time // SLOTS + 2, SLOTS, width), F32),
            pltpu.VMEM((halves * lines * time, chunk), BF16),
            pltpu.VMEM((chunk, halves * 2 * LANES), BF16),
            pltpu.VMEM((halves * 2 * LANES, chunk), BF16),
            pltpu.VMEM((SLOTS, chunk), F32),
        ],
        compiler_params=pltpu.CompilerParams(vmem_limit_bytes=24 * 1024 * 1024),
        cost_estimate=pl.CostEstimate(flops=4 * flops, bytes_accessed=4 * 1024 * 1024, transcendentals=time * SLOTS * chunk),
    )(
        after,
        *xs,
        seam,
        in_weight,
        conv,
        conv_bias,
        jnp.swapaxes(proj, 1, 2),
        step_weight,
        step_bias,
    )


def scan(axis, after, coefs, steps, u, decay_log, skip):
    time, _, chunk = steps.shape
    width, states = decay_log.shape[1:]
    vmem = pl.BlockSpec(memory_space=pltpu.VMEM)
    return pl.pallas_call(
        functools.partial(scan_kernel, axis),
        out_shape=jax.ShapeDtypeStruct((time * SLOTS, chunk), BF16),
        in_specs=[pl.BlockSpec(memory_space=pl.ANY), vmem, vmem, vmem, vmem, vmem],
        out_specs=vmem,
        scratch_shapes=[
            pltpu.VMEM((time, SLOTS, chunk), F32),
            pltpu.VMEM((time, SLOTS, chunk), F32),
            pltpu.VMEM((time, 2 * states, SLOTS, LANES), F32),
        ],
        compiler_params=pltpu.CompilerParams(vmem_limit_bytes=(8 << 20) + time * (136 << 10) + time * 20 * chunk),
        cost_estimate=pl.CostEstimate(
            flops=8 * time * SLOTS * chunk * states,
            bytes_accessed=4 * 1024 * 1024,
            transcendentals=time * SLOTS * chunk * states,
        ),
    )(after, coefs, steps, u, jnp.swapaxes(decay_log, 1, 2), skip)


def end_kernel(columns, gate_ref, gain_ref, weight_ref, *refs):
    pair_refs, beside_ref, row_refs, out_ref, gated_ref = refs[:columns], refs[columns], refs[columns + 1 : -2], refs[-2], refs[-1]
    height, width, channels = out_ref.shape
    size = row_refs[0].shape[0]
    lines = size // width
    swap = flip("col") ^ lax.axis_index("col")
    turn = (flip("row") ^ lax.axis_index("row")) * (width // lax.axis_size("row"))
    row = rows_of(height * width)
    line = (row >> bits(width)) ^ (swap * lines)
    source = (((row & (width - 1)) ^ turn) << bits(height)) + line
    rows = jnp.concatenate([row_ref[...] for row_ref in row_refs], axis=0)
    blocks = []
    for part in range(columns):
        blocks += [pair_refs[part][0], beside_ref[part]]
    columns = jnp.concatenate(blocks, axis=0)
    combined = layer_norm(rows.astype(F32) + dot(one_hot([source], height * width), columns), gain_ref[...][None])
    for part in range(len(row_refs)):
        cells = pl.ds(pl.multiple_of((part ^ swap) * size, size), size)
        gate = gate_ref[cells].astype(F32)
        gated_ref[cells] = (combined[part * size : (part + 1) * size] * (gate / (1.0 + jnp.exp(-gate)))).astype(BF16)
    out = dot(gated_ref[...], weight_ref[...]).astype(BF16)
    out_ref[...] = out.reshape(height, width, channels)


def pair_kernel(*refs):
    count = len(refs) // 2
    own_refs, beside_ref, out_refs = refs[:count], refs[count], refs[count + 1 :]
    for k in range(count):
        out_refs[k][0] = own_refs[k][...]
        out_refs[k][1] = beside_ref[k + 1]


def first_kernel(own_ref, beside_ref, out_ref):
    out_ref[0] = own_ref[...]
    out_ref[1] = beside_ref[0]


def collect_kernel(after_ref, *refs):
    out_ref = refs[-1]
    for k in range(len(refs) - 1):
        out_ref[k] = refs[k][1]


def simple(kernel, shapes, *arrays, after=None):
    vmem = pl.BlockSpec(memory_space=pltpu.VMEM)
    first = [] if after is None else [after]
    many = isinstance(shapes, list)
    return pl.pallas_call(
        kernel,
        out_shape=shapes,
        in_specs=[pl.BlockSpec(memory_space=pl.ANY)] * len(first) + [vmem] * len(arrays),
        out_specs=[vmem] * len(shapes) if many else vmem,
        compiler_params=pltpu.CompilerParams(vmem_limit_bytes=4 * 1024 * 1024),
        cost_estimate=pl.CostEstimate(flops=0, bytes_accessed=2 << 20, transcendentals=0),
    )(*first, *arrays)


def swap(block, axis, k):
    return lax.ppermute(block, axis, [(i, i ^ k) for i in range(lax.axis_size(axis))])


def swap_out(own, beside):
    beside = swap(beside, "row", 1)
    shape = jax.ShapeDtypeStruct((2,) + own[0].shape, own[0].dtype)
    pairs = simple(pair_kernel, [shape] * (len(own) - 1), *own[1:], beside)
    found = {k: swap(pairs[k - 1], "row", 2 * k) for k in range(len(own) - 1, 0, -1)}
    first = simple(first_kernel, jax.ShapeDtypeStruct((2,) + own[0].shape, own[0].dtype), own[0], beside)
    return [first] + [found[k] for k in range(1, len(own))]


def swap_back_far(pairs):
    found = {k: swap(pairs[k], "row", 2 * k) for k in range(len(pairs) - 1, 0, -1)}
    return [pairs[0]] + [found[k] for k in range(1, len(pairs))]


def swap_blocks(blocks, axis):
    count = lax.axis_size(axis)
    found = {k: lax.ppermute(blocks[k], axis, [(i, i ^ k) for i in range(count)]) for k in range(count - 1, 0, -1)}
    return [blocks[0]] + [found[k] for k in range(1, count)]


def pick_kernel(axis, after_ref, *refs):
    x_refs, out_ref = views(refs[:-1], 3), refs[-1]
    place = lax.axis_index(axis) ^ flip(axis)
    line = jnp.where(place == 0, 1, x_refs[0].shape[0] - 2)
    for part, x_ref in enumerate(x_refs):
        out_ref[part] = x_ref[line]


def pick(axis, after, xs):
    return pl.pallas_call(
        functools.partial(pick_kernel, axis),
        out_shape=jax.ShapeDtypeStruct((lax.axis_size("col" if axis == "col" else "row"),) + xs[-1].shape[-2:], xs[-1].dtype),
        in_specs=[pl.BlockSpec(memory_space=pl.ANY)] + [pl.BlockSpec(memory_space=pltpu.VMEM)] * len(xs),
        out_specs=pl.BlockSpec(memory_space=pltpu.VMEM),
        compiler_params=pltpu.CompilerParams(vmem_limit_bytes=4 * 1024 * 1024),
    )(after, *xs)


def seam_of(axis, line):
    count = lax.axis_size(axis)
    height, breadth = lax.axis_size("row"), lax.axis_size("col")
    if axis == "row":
        at = lambda group: (0 if group & 1 else count - 1) * breadth
        ends = [(at(c) + c, at(c) + c + 1) for c in range(breadth - 1)]
    else:
        at = lambda group: 0 if group & 1 else count - 1
        ends = [(at(r) + r * breadth, at(r) + (r + 1) * breadth) for r in range(height - 1)]
    pairs = ends + [(b, a) for a, b in ends]
    return lax.ppermute(line, ("row", "col"), pairs)


def local(
    features,
    norm_gain,
    in_weight,
    conv_weight,
    conv_bias,
    proj_weight,
    step_weight,
    step_bias,
    decay_log,
    skip_gain,
    out_gain,
    out_weight,
):
    height, width, channels = features.shape
    inner = out_weight.shape[0]
    tokens = height * width
    row_lines = height // lax.axis_size("col")
    col_lines = width // lax.axis_size("row")

    rows, cols = lax.axis_size("row"), lax.axis_size("col")
    vmem = pl.BlockSpec(memory_space=pltpu.VMEM)
    normed, *sends = pl.pallas_call(
        functools.partial(cut_kernel, rows),
        out_shape=[jax.ShapeDtypeStruct((tokens, channels), BF16)]
        + [jax.ShapeDtypeStruct((col_lines + 2, height, channels), BF16)] * (rows // 2)
        + [jax.ShapeDtypeStruct((rows // 2, col_lines + 2, height, channels), BF16)]
        + [jax.ShapeDtypeStruct((row_lines + 2, width, channels), BF16)] * cols,
        in_specs=[pl.BlockSpec(features.shape, lambda: (0, 0, 0)), pl.BlockSpec((channels,), lambda: (0,))],
        out_specs=[vmem] * (2 + rows // 2 + cols),
        scratch_shapes=[pltpu.VMEM((tokens, channels), BF16)],
        compiler_params=pltpu.CompilerParams(vmem_limit_bytes=12 * 1024 * 1024),
        cost_estimate=pl.CostEstimate(flops=6_000_000_000, bytes_accessed=2 << 20, transcendentals=tokens),
    )(features, norm_gain)
    weights = (in_weight, conv_weight, conv_bias, proj_weight, step_weight, step_bias, decay_log, skip_gain)
    gate = pl.pallas_call(
        gate_kernel,
        out_shape=jax.ShapeDtypeStruct((tokens, inner), BF16),
        grid=(1,),
        in_specs=[
            pl.BlockSpec((tokens, channels), lambda i: (0, 0)),
            pl.BlockSpec((channels, inner), lambda i: (0, 1)),
        ],
        out_specs=pl.BlockSpec((tokens, inner), lambda i: (0, 0)),
        compiler_params=pltpu.CompilerParams(vmem_limit_bytes=12 * 1024 * 1024),
        cost_estimate=pl.CostEstimate(flops=2 * tokens * channels * inner, bytes_accessed=1 << 20, transcendentals=0),
    )(normed, in_weight)

    half = rows // 2
    row_x = swap_blocks(sends[half + 1 :], "col")
    col_x = swap_out(sends[:half], sends[half])
    row_seam = seam_of("col", pick("col", normed, row_x))
    row_steps = prepare("col", normed, row_x, row_seam, *weights)
    col_seam = seam_of("row", pick("row", row_steps[0], col_x))
    col_steps = prepare("row", row_steps[0], col_x, col_seam, *weights)
    col_y = scan("row", normed, *col_steps, decay_log, skip_gain)
    joined = join("row", col_y, rows, col_lines, height, inner, normed)
    col_y = swap_back_far(joined)
    row_y = scan("col", joined[0], *row_steps, decay_log, skip_gain)
    beside = jax.ShapeDtypeStruct((half,) + joined[0].shape[1:], BF16)
    beside = simple(collect_kernel, beside, *col_y, after=row_y)
    row_y = swap_blocks(join("col", row_y, cols, row_lines, width, inner, beside), "col")
    beside = swap(beside, "row", 1)
    return pl.pallas_call(
        functools.partial(end_kernel, half),
        out_shape=jax.ShapeDtypeStruct(features.shape, BF16),
        scratch_shapes=[pltpu.VMEM((tokens, inner), BF16)],
        compiler_params=pltpu.CompilerParams(vmem_limit_bytes=16 * 1024 * 1024),
    )(gate, out_gain, out_weight, *col_y, beside, *row_y)


def solution(mesh):
    in_specs = (P("row", "col", None), P(), P(), P(), P(), P(), P(), P(), P(), P(), P(), P())
    out_specs = P("row", "col", None)
    return jax.shard_map(local, mesh=mesh, in_specs=in_specs, out_specs=out_specs, check_vma=False)
```
